32 devices in a mesh: seq: 8 (over z, x), head: 4 (over y, core).
Axes of the slice: x: 2, y: 2, z: 4, core: 2. Of those that a mesh axis runs over, the one named last changes fastest.
Arguments:
- tokens: bfloat16 [8, 2048, 512], P(None, 'seq', 'head'), may hold values from -6 to 6
- norm_gain: float32 [512], replicated, may hold values from 0.5 to 1.5
- query_weight: bfloat16 [512, 512], P(None, 'head'), may hold values from -0.25 to 0.25
- key_weight: bfloat16 [512, 512], P(None, 'head'), may hold values from -0.25 to 0.25
- value_weight: bfloat16 [512, 512], P(None, 'head'), may hold values from -0.25 to 0.25
- attention_output_weight: bfloat16 [512, 512], P('head'), may hold values from -1.5 to 1.5
- feedforward_norm_gain: float32 [512], replicated, may hold values from 0.5 to 1.5
- up_weight: bfloat16 [512, 2048], P(None, 'head'), may hold values from -0.25 to 0.25
- down_weight: bfloat16 [2048, 512], P('head'), may hold values from -0.1875 to 0.1875
- segment_ids: int32 [8, 2048], P(None, 'seq'), may hold values from 0 to 15, never falling along the last dimension, each value on 1 to 1024 neighbouring positions
- out_grad: bfloat16 [8, 2048, 512], P(None, 'seq', 'head'), may hold values from -6 to 6
Outputs:
- layer_out: bfloat16 [8, 2048, 512], P(None, 'seq', 'head')
- input_grad: float32 [8, 2048, 512], P(None, 'seq', 'head')
- norm_gain_grad: float32 [512], P('head')
- query_weight_grad: float32 [512, 512], P(None, 'head')
- key_weight_grad: float32 [512, 512], P(None, 'head')
- value_weight_grad: float32 [512, 512], P(None, 'head')
- out_weight_grad: float32 [512, 512], P('head')
- ffn_gain_grad: float32 [512], P('head')
- up_weight_grad: float32 [512, 2048], P(None, 'head')
- down_weight_grad: float32 [2048, 512], P('head')
The draws below stay inside these ranges and needn't reach their ends.
Inputs may be any that keep to these rules, and one draw needn't show every extreme that they name: `segment_ids`: in each sequence the ids start at 0 and rise by one at each document start; 16 documents of 1 to 1024 tokens, the longest exactly 1024.
All inputs are finite; a program needn't handle non-finite values.
Results may differ from the reference program's by a relative error of at most 0.017.
Values may be sent and summed in bfloat16 or wider, within the bound.
A program may use at most 256 MiB of HBM per device.

```python
import math
from functools import partial
import jax
import jax.numpy as jnp
import numpy as np
from jax import lax

D = 512
H = 8
DH = 64
FF = 2048
MB = 8
BLOCK = 256
L = 2048
DOCS = 16
MOST = 1024


def steps_of(own_key, shape, split, least, high):
    gain = 1.0
    for axis_at, blocks in split:
        draws = jax.random.uniform(jax.random.fold_in(jax.random.fold_in(own_key, 6), axis_at), (blocks,), jnp.float32, least / len(split), high / len(split))
        gain = gain * jnp.repeat(jnp.exp(draws), shape[axis_at] // blocks).reshape((-1,) + (1,) * (len(shape) - 1 - axis_at))
    return gain


def profile(count, total, limit, lean):
    portions = [(1 << 20) // math.isqrt(standing ** lean) + 1 for standing in range(2, count + 1)]
    surplus, holding = total - limit - (count - 1), [1] * (count - 1)
    while surplus > 0:
        free = [i for i in range(count - 1) if holding[i] < limit]
        pool, budget = sum([portions[i] for i in free]), surplus
        for i in free:
            more = min(limit - holding[i], max(1, budget * portions[i] // pool), surplus)
            holding[i] = holding[i] + more
            surplus = surplus - more
    return np.array([limit] + holding)


def uneven(own_key, count, total, reach, lean):
    if count == 2:
        one = jax.random.randint(own_key, (), max(1, total - reach), min(reach, total - 1) + 1)
        return jnp.stack([one, total - one])
    sizes = jnp.asarray(profile(count, total, reach, lean), jnp.int32)
    pairs = (count - 1) // 2
    giver, receiver = sizes[1:1 + 2 * pairs:2], sizes[2:2 + 2 * pairs:2]
    slack = jnp.minimum(giver - 1, reach - receiver)
    passed = jax.random.randint(jax.random.fold_in(own_key, 1), (pairs,), 0, 1 << 20) % (slack + 1)
    sizes = sizes.at[1:1 + 2 * pairs:2].set(giver - passed).at[2:2 + 2 * pairs:2].set(receiver + passed)
    return sizes[jax.random.permutation(jax.random.fold_in(own_key, 2), count)]


def gaussian(stream_key, shape, width, limit, split=(), kind=jnp.bfloat16):
    gain = steps_of(stream_key, shape, split, -0.22, 0.18) if split else 1.0
    values = jax.random.normal(stream_key, shape, jnp.float32) * width * gain
    return jnp.minimum(jnp.maximum(values, -limit), limit).astype(kind)


def setup_inputs(seed: int = 0) -> dict:
    splits = jax.random.split(jax.random.key(seed), 12)
    return {
        "tokens": gaussian(splits[0], (MB, L, D), 1.0, 6.0, ((1, 8), (2, 4))),
        "norm_gain": jnp.clip(1.0 + 0.1 * jax.random.normal(splits[1], (D,), jnp.float32), 0.5, 1.5),
        "query_weight": gaussian(splits[2], (D, D), D ** -0.5, 0.25, ((1, 4),)),
        "key_weight": gaussian(splits[3], (D, D), D ** -0.5, 0.25, ((1, 4),)),
        "value_weight": gaussian(splits[4], (D, D), D ** -0.5, 0.25, ((1, 4),)),
        "attention_output_weight": gaussian(splits[5], (D, D), (D // 32) ** -0.5, 1.5, ((0, 4),)),
        "feedforward_norm_gain": jnp.clip(1.0 + 0.1 * jax.random.normal(splits[6], (D,), jnp.float32), 0.5, 1.5),
        "up_weight": gaussian(splits[7], (D, FF), D ** -0.5, 0.25, ((1, 4),)),
        "down_weight": gaussian(splits[8], (FF, D), (FF // 2) ** -0.5, 0.1875, ((0, 4),)),
        "segment_ids": jax.vmap(lambda own: jnp.searchsorted(jnp.cumsum(uneven(own, DOCS, L, MOST, 2)), jnp.arange(L), side="right"))(jax.random.split(splits[9], MB)).reshape((MB, L)).astype(jnp.int32),
        "out_grad": gaussian(splits[10], (MB, L, D), 1.0, 6.0, ((1, 8), (2, 4))),
    }


FULL_PRECISION = lax.Precision.HIGHEST
EPSILON = 1e-05

@jax.custom_vjp
def low(v):
    return lax.optimization_barrier(v.astype(jnp.bfloat16)).astype(jnp.float32)

@jax.custom_vjp
def low_back(v):
    return v

def low_keep(v):
    return (low(v), None)

def low_pass(kept, grad):
    return (grad,)

def back_keep(v):
    return (v, None)

def back_low(kept, grad):
    return (low(grad),)
low.defvjp(low_keep, low_pass)
low_back.defvjp(back_keep, back_low)

def matmul(left, right):
    return jnp.dot(left, right, precision=FULL_PRECISION, preferred_element_type=jnp.float32)

def layer_norm(values, gain_row):
    center = values - lax.optimization_barrier(jnp.mean(values, axis=-1, keepdims=True))
    variance = lax.optimization_barrier(jnp.mean(center * center, axis=-1, keepdims=True))
    return center * lax.rsqrt(variance + EPSILON) * gain_row

def feature(values):
    return jnp.where(values > 0, values + 1.0, jnp.exp(jnp.minimum(values, 0.0)))

def attend(query_feat, key_feat, value_rows, seg_float):
    length = query_feat.shape[0]
    blocks_all = length // BLOCK
    causal = jnp.tril(jnp.ones((BLOCK, BLOCK), jnp.float32))

    @jax.checkpoint
    def block_step(state_in, items):
        prior_s, previous_normalizer, prior_last = state_in
        query_blk, key_blk, value_blk, seg_blk = items
        same_mask = causal * (seg_blk[:, None] == seg_blk[None, :]).astype(jnp.float32)
        scores = jnp.einsum('thd,shd->hts', query_blk, key_blk, precision=FULL_PRECISION) * same_mask[None]
        carry_on = (seg_blk == prior_last).astype(jnp.float32)
        numerator = jnp.einsum('hts,she->the', low(scores), value_blk, precision=FULL_PRECISION)
        numerator = numerator + carry_on[:, None, None] * jnp.einsum('thd,hde->the', query_blk, prior_s, precision=FULL_PRECISION)
        denominator = lax.optimization_barrier(jnp.sum(scores, axis=2)).T + carry_on[:, None] * jnp.einsum('thd,hd->th', query_blk, previous_normalizer, precision=FULL_PRECISION)
        result = numerator / denominator[:, :, None]
        block_last = seg_blk[-1]
        tail_mask = (seg_blk == block_last).astype(jnp.float32)
        tail_keys = key_blk * tail_mask[:, None, None]
        block_s = jnp.einsum('shd,she->hde', tail_keys, value_blk, precision=FULL_PRECISION)
        block_z = lax.optimization_barrier(jnp.sum(tail_keys, axis=0))
        keep_gate = (prior_last >= block_last).astype(jnp.float32)
        final_state = (block_s + keep_gate * prior_s, block_z + keep_gate * previous_normalizer, jnp.maximum(prior_last, block_last))
        return (final_state, result)
    start = (jnp.zeros((H, DH, DH), jnp.float32), jnp.zeros((H, DH), jnp.float32), jnp.array(-1.0, jnp.float32))
    items = (query_feat.reshape(blocks_all, BLOCK, H, DH), key_feat.reshape(blocks_all, BLOCK, H, DH), value_rows.reshape(blocks_all, BLOCK, H, DH), seg_float.reshape(blocks_all, BLOCK))
    _, outputs = lax.scan(block_step, start, items)
    return outputs.reshape(length, H * DH)

def layer(seg_float, inputs, norm_gain, query_weight, key_weight, value_weight, attention_output_weight, feedforward_norm_gain, up_weight, down_weight):
    length = inputs.shape[0]
    normed = low(layer_norm(inputs, norm_gain))
    query = low_back(matmul(normed, query_weight))
    key_rows = low_back(matmul(normed, key_weight))
    value_rows = low(low_back(matmul(normed, value_weight)))
    query_feat = low(feature(query))
    key_feat = low(feature(key_rows))
    attn = low(attend(query_feat.reshape(length, H, DH), key_feat.reshape(length, H, DH), value_rows.reshape(length, H, DH), seg_float))
    branch = low_back(matmul(attn, attention_output_weight))
    middle = inputs + branch
    normed_two = low(layer_norm(low(middle), feedforward_norm_gain))
    hidden_pre = low_back(matmul(normed_two, up_weight))
    hidden = low(jax.nn.silu(hidden_pre))
    ffn = low_back(matmul(hidden, down_weight))
    return middle + ffn

def reference(tokens, norm_gain, query_weight, key_weight, value_weight, attention_output_weight, feedforward_norm_gain, up_weight, down_weight, segment_ids, out_grad):
    weight_args = tuple((item.astype(jnp.float32) for item in (norm_gain, query_weight, key_weight, value_weight, attention_output_weight, feedforward_norm_gain, up_weight, down_weight)))

    def one_sequence(grad_sums, items):
        seq_tokens, seq_ids, seq_grad = items
        result, pull = jax.vjp(partial(layer, seq_ids.astype(jnp.float32)), seq_tokens.astype(jnp.float32), *weight_args)
        grads = pull(seq_grad.astype(jnp.float32))
        new_sums = tuple((total + piece for total, piece in zip(grad_sums, grads[1:])))
        return (new_sums, (result.astype(jnp.bfloat16), grads[0]))
    zero_sums = tuple((jnp.zeros_like(item) for item in weight_args))
    grad_sums, (outputs, input_grads) = lax.scan(one_sequence, zero_sums, (tokens, segment_ids, out_grad))
    return (outputs, input_grads, grad_sums[0], grad_sums[1], grad_sums[2], grad_sums[3], grad_sums[4], grad_sums[5], grad_sums[6], grad_sums[7])
```

```python
import functools

import jax
import jax.numpy as jnp
from jax import lax
from jax.experimental import pallas as pl
from jax.experimental.pallas import tpu as pltpu
from jax.sharding import PartitionSpec as P

DH = 64
BLOCK = 256
EPSILON = 1e-05
MESH = pl.DeviceIdType.MESH
F32 = jnp.float32
BF16 = jnp.bfloat16
MIB = 1 << 20

KINDS = 4
UNITS = 3


def mm(left, right, form="NN"):
    dims = {"NN": ((1,), (0,)), "NT": ((1,), (1,)), "TN": ((0,), (0,))}[form]
    return lax.dot_general(left, right, (dims, ((), ())), preferred_element_type=F32)


def loop(count, step):
    def run(i, carry):
        step(i)
        return carry

    lax.fori_loop(0, count, run, 0)


def rows_loop(total, chunk, step):
    loop(total // chunk, lambda i: step(pl.ds(pl.multiple_of(i * chunk, chunk), chunk)))


def at128(i):
    return pl.ds(pl.multiple_of(i * 128, 128), 128)


def layer_kernel(
    pairs,
    tok,
    og_in,
    wq,
    wk,
    wv,
    wo,
    wu,
    wd,
    seg,
    gain_one,
    gain_two,
    lo_out,
    ig_out,
    fin,
    gains,
    xin,
    ogs,
    w_qkv,
    w_o,
    w_u,
    w_d,
    seg_other,
    unit_one,
    unit_two,
    rstd_one,
    rstd_two,
    normed,
    normed_two,
    feat,
    val,
    mask,
    mask_t,
    seg_col,
    carry_on,
    own_s,
    own_z,
    msg_s,
    msg_z,
    buf_s,
    buf_z,
    state,
    attn,
    attn_wide,
    den_inv,
    middle,
    work,
    work_two,
    hid,
    hid_grad,
    ffn,
    norm_grad,
    middle_grad,
    middle_low,
    num_grad,
    den_grad,
    grad_s,
    grad_z,
    msg_gs,
    msg_gz,
    buf_gs,
    buf_gz,
    key_acc,
    val_acc,
    low_grads,
    lo_s,
    ig_s,
    part,
    buf_core,
    buf_y,
    buf_x,
    buf_ring,
    own_piece,
    gain_part,
    gain_buf,
    local_sem,
    send_sem,
    recv_sem,
):
    s = lax.axis_index("seq")
    h = lax.axis_index("head")
    pair, par = lax.div(s, 2), lax.rem(s, 2)
    hy, hc = lax.div(h, 2), lax.rem(h, 2)
    member = par * 4 + h
    others = pairs - 1

    ids = iter(range(10000))
    sends = []

    def peer(dp, dy, dc):
        par_to = 1 - par if dp else par
        y_to = 1 - hy if dy else hy
        c_to = 1 - hc if dc else hc
        return par_to, y_to, c_to

    def address(par_to, y_to, c_to):
        return (2 * pair + par_to, 2 * y_to + c_to)

    core, ypeer, xpeer = (address(*peer(*d)) for d in ((0, 0, 1), (0, 1, 0), (1, 0, 0)))

    def ring(d):
        to = lax.rem(pair + d, pairs)
        return to, (2 * to + par, h)

    def remote(src, dst, device):
        i = next(ids)
        return pltpu.make_async_remote_copy(
            src_ref=src,
            dst_ref=dst,
            send_sem=send_sem.at[i],
            recv_sem=recv_sem.at[i],
            device_id=device,
            device_id_type=MESH,
        )

    def start(copy):
        copy.start()
        sends.append(copy)
        return copy

    local_ids = iter(range(1000))

    def local(src, dst):
        copy = pltpu.make_async_copy(src, dst, local_sem.at[next(local_ids)])
        copy.start()
        return copy

    hcol = at128(h)
    own_tok = local(tok.at[member], xin.at[pl.ds(pl.multiple_of(par * 256, 256), 256), hcol])
    own_w = [
        [local(w, w_qkv.at[i, :, hcol]) for i, w in enumerate((wq, wk, wv))],
        [local(wo, w_o.at[hcol])],
        [local(wu, w_u.at[h])],
        [local(wd, w_d.at[h])],
    ]
    own_og = local(og_in.at[member], ogs.at[pl.ds(pl.multiple_of(par * 256, 256), 256), hcol])
    row8 = lax.broadcasted_iota(jnp.int32, (8, 128), 0)
    neutral = jnp.where(row8 == 4, -1.0, 0.0).astype(F32)
    for slot in range(2):
        buf_s[slot] = jnp.zeros((256, 128), BF16)
        buf_gs[slot] = jnp.zeros((256, 128), BF16)
        buf_z[slot] = neutral
        buf_gz[slot] = jnp.zeros((8, 128), F32)

    barrier = pltpu.get_barrier_semaphore()
    combos = [(1, 0, 0), (0, 1, 0), (1, 1, 0), (1, 0, 1), (0, 1, 1), (1, 1, 1), (0, 0, 1)]
    for d in combos:
        pl.semaphore_signal(
            barrier, inc=1, device_id=address(*peer(*d)), device_id_type=MESH
        )
    for d in range(1, pairs):
        pl.semaphore_signal(barrier, inc=1, device_id=ring(d)[1], device_id_type=MESH)
    pl.semaphore_wait(barrier, 7 + others)

    def scatter_in(src, dst):
        copies = []
        for d in combos:
            par_to, y_to, c_to = peer(*d)
            copies.append(
                start(
                    remote(
                        src.at[par_to * 4 + 2 * y_to + c_to],
                        dst.at[pl.ds(pl.multiple_of(par * 256, 256), 256), hcol],
                        address(par_to, y_to, c_to),
                    )
                )
            )
        return copies

    def scatter_out(src, dst):
        copies = []
        for d in combos:
            par_to, y_to, c_to = peer(*d)
            copies.append(
                start(
                    remote(
                        src.at[
                            pl.ds(pl.multiple_of(par_to * 256, 256), 256),
                            at128(2 * y_to + c_to),
                        ],
                        dst.at[member],
                        address(par_to, y_to, c_to),
                    )
                )
            )
        own = local(src.at[pl.ds(pl.multiple_of(par * 256, 256), 256), hcol], dst.at[member])
        return copies, own

    half256 = pl.ds(pl.multiple_of(par * 256, 256), 256)

    def view(kind, shard, half):
        if kind == 0:
            rows = (
                slice(None)
                if half is None
                else pl.ds(pl.multiple_of(half * 256, 256), 256)
            )
            return w_qkv.at[:, rows, at128(shard)]
        if kind == 1:
            if half is None:
                return w_o.at[at128(shard)]
            return w_o.at[pl.ds(pl.multiple_of(shard * 128 + half * 64, 64), 64)]
        ref = w_u if kind == 2 else w_d
        if half is None:
            return ref.at[shard]
        return ref.at[shard, pl.ds(pl.multiple_of(half * 256, 256), 256)]

    across = 2 * (1 - hy) + hc

    def weight_y(kind):
        return start(remote(view(kind, h, par), view(kind, h, par), ypeer))

    def weight_core(kind):
        return start(remote(view(kind, h, None), view(kind, h, None), core))

    def weight_x(kind):
        x = start(remote(view(kind, across, par), view(kind, across, par), xpeer))
        c = start(remote(view(kind, across, par), view(kind, across, par), core))
        return x, c

    def weight_last(kind):
        return start(remote(view(kind, across, 1 - par), view(kind, across, 1 - par), core))

    for copy in own_w[0]:
        copy.wait()
    wy = {0: weight_y(0)}
    wc = {0: weight_core(0)}
    tokens_in = scatter_in(tok, xin)
    seg_copy = start(remote(seg, seg_other, xpeer))
    for kind in (1, 2, 3):
        for copy in own_w[kind]:
            copy.wait()
        wc[kind] = weight_core(kind)
    wx, wl = {}, {}

    def forward_y(kind):
        wy[kind].wait_recv()
        wx[kind] = weight_x(kind)

    def forward_x(kind):
        wx[kind][0].wait_recv()
        wl[kind] = weight_last(kind)

    def weights_ready(kind):
        wc[kind].wait_recv()
        wx[kind][1].wait_recv()
        wl[kind].wait_recv()

    forward_y(0)
    for copy in tokens_in:
        copy.wait_recv()
    own_tok.wait()
    wy[1] = weight_y(1)
    wy[2] = weight_y(2)

    def norm_rows(source, gain, unit_ref, rstd_ref, out_ref):
        def step(r):
            x = source(r)
            center = x - jnp.mean(x, axis=-1, keepdims=True)
            scale = lax.rsqrt(jnp.mean(center * center, axis=-1, keepdims=True) + EPSILON)
            unit = center * scale
            unit_ref[r, :] = unit
            rstd_ref[r, :] = jnp.broadcast_to(scale, (unit.shape[0], 128))
            out_ref[r, :] = (unit * gain[...]).astype(BF16)

        rows_loop(512, 64, step)

    norm_rows(lambda r: xin[r, :].astype(F32), gain_one, unit_one, rstd_one, normed)

    seg_copy.wait_recv()
    own_row = seg[pl.ds(member, 1), :]
    other_row = seg_other[pl.ds(member, 1), :]
    seg_rows = (
        (own_row * (1 - par) + other_row * par).astype(F32),
        (own_row * par + other_row * (1 - par)).astype(F32),
    )
    first = lax.broadcasted_iota(jnp.int32, (256, 256), 0)
    second = lax.broadcasted_iota(jnp.int32, (256, 256), 1)
    for b in range(2):
        along = jnp.broadcast_to(seg_rows[b], (256, 256))
        down = along.T
        same = along == down
        mask[b] = jnp.where(same & (second <= first), 1.0, 0.0)
        mask_t[b] = jnp.where(same & (first <= second), 1.0, 0.0)
        seg_col[b] = down[:, :128]

    forward_x(0)
    weights_ready(0)

    def project(i):
        work[...] = mm(normed[...], w_qkv[i])

        def step(r):
            v = work[r, :]
            feat[i, r, :] = jnp.where(v > 0, v + 1.0, jnp.exp(jnp.minimum(v, 0.0))).astype(BF16)

        rows_loop(512, 64, step)

    val[...] = mm(normed[...], w_qkv[2]).astype(BF16)
    loop(2, lambda i: project(1 - i))

    lane = lax.broadcasted_iota(jnp.int32, (1, 128), 1)
    low_lanes = lane < 64
    spread = (
        lax.broadcasted_iota(jnp.int32, (128, 128), 0) // 64
        == lax.broadcasted_iota(jnp.int32, (128, 128), 1) // 64
    )

    def place(i):
        b, pr = lax.div(i, 4), lax.rem(i, 4)
        return b, pr, pl.ds(pl.multiple_of(b * 256, 256), 256), at128(pr)

    def pack(square):
        return jnp.where(low_lanes, square[:64], square[64:])

    def unpack(packed):
        zero = jnp.zeros_like(packed)
        return jnp.concatenate(
            [jnp.where(low_lanes, packed, zero), jnp.where(low_lanes, zero, packed)], axis=0
        )

    def two(rows):
        zero = jnp.zeros_like(rows)
        return jnp.concatenate(
            [jnp.where(low_lanes, rows, zero), jnp.where(low_lanes, zero, rows)], axis=0
        )

    def pick(stacked):
        return jnp.where(low_lanes, stacked[:256], stacked[256:])

    def packed_rows(pr):
        return pl.ds(pl.multiple_of(pr * 64, 64), 64)

    last_rows = [seg_col[b, pl.ds(255, 1), :] for b in range(2)]

    def own_state(i):
        b, pr, rows, cols = place(i)
        tail = seg_col[b] == seg_col[b, pl.ds(255, 1), :]
        keys = feat[1, rows, cols].astype(F32)
        keys = jnp.where(tail, keys, 0.0)
        own_s[b, packed_rows(pr), :] = pack(mm(keys.astype(BF16), val[rows, cols], "TN"))
        own_z[b, pl.ds(pr, 1), :] = jnp.sum(keys, axis=0, keepdims=True)

    own_z[...] = jnp.zeros_like(own_z)
    loop(8, own_state)
    keep_mid = jnp.where(last_rows[0] >= last_rows[1], 1.0, 0.0)
    msg_s[...] = (own_s[1] + keep_mid * own_s[0]).astype(BF16)
    msg_z[...] = jnp.where(row8 == 4, last_rows[1], own_z[1] + keep_mid * own_z[0])

    def shift(d, s_ref, z_ref, s_buf, z_buf, slot):
        to = lax.rem(pair + d + pairs, pairs)
        device = (2 * to + par, h)
        return (
            remote(s_ref, s_buf.at[slot], device),
            remote(z_ref, z_buf.at[slot], device),
        )

    forward = [shift(d, msg_s, msg_z, buf_s, buf_z, d - 1) for d in (1, 2)]
    for d, copies in zip((1, 2), forward):

        @pl.when(pair + d < pairs)
        def _():
            for copy in copies:
                copy.start()

    forward_y(1)
    forward_y(2)
    og_copies = scatter_in(og_in, ogs)
    wy[3] = weight_y(3)

    for d, copies in zip((1, 2), forward):

        @pl.when(pair >= d)
        def _():
            for copy in copies:
                copy.wait_recv()

    last_in = buf_z[0, pl.ds(4, 1), :]
    keep_in = jnp.where(buf_z[1, pl.ds(4, 1), :] >= last_in, 1.0, 0.0)
    keep_first = jnp.where(last_in >= last_rows[0], 1.0, 0.0)
    buf_z[0] = buf_z[0] + keep_in * buf_z[1]
    carry_on[0] = jnp.where(seg_col[0] == last_in, 1.0, 0.0)
    carry_on[1] = jnp.where(seg_col[1] == last_rows[0], 1.0, 0.0)

    def enter(pr):
        entering = buf_s[0, packed_rows(pr), :].astype(F32) + keep_in * buf_s[
            1, packed_rows(pr), :
        ].astype(F32)
        z_in = buf_z[0, pl.ds(pr, 1), :]
        middle_s = own_s[0, packed_rows(pr), :] + keep_first * entering
        middle_z = own_z[0, pl.ds(pr, 1), :] + keep_first * z_in
        for b, (packed, z_row) in enumerate(((entering, z_in), (middle_s, middle_z))):
            wide = jnp.where(spread, jnp.broadcast_to(z_row, (128, 128)).T, 0.0)
            state[b * 4 + pr, :, :128] = unpack(packed).astype(BF16)
            state[b * 4 + pr, :, 128:] = wide.astype(BF16)

    loop(4, enter)

    ones = jnp.ones((256, 128), BF16)

    def attend(i):
        b, pr, rows, cols = place(i)
        q, k, v = feat[0, rows, cols], feat[1, rows, cols], val[rows, cols]
        scores = mm(two(q), k, "NT")
        m = mask[b]
        low = jnp.concatenate([scores[:256] * m, scores[256:] * m], axis=0).astype(BF16)
        both = mm(low, jnp.concatenate([v, ones], axis=1))
        carried = mm(q, state[i])
        c = carry_on[b]
        numer = pick(both[:, :128]) + c * carried[:, :128]
        denom = pick(both[:, 128:]) + c * carried[:, 128:]
        inverse = 1.0 / denom
        result = numer * inverse
        den_inv[rows, cols] = inverse
        attn_wide[rows, cols] = result
        attn[rows, cols] = result.astype(BF16)

    loop(8, attend)
    forward_x(1)
    forward_x(2)
    weights_ready(1)

    work[...] = mm(attn[...], w_o[...])

    def mid_step(r):
        middle[r, :] = xin[r, :].astype(F32) + work[r, :]

    rows_loop(512, 64, mid_step)
    norm_rows(
        lambda r: middle[r, :].astype(BF16).astype(F32), gain_two, unit_two, rstd_two, normed_two
    )
    forward_y(3)
    weights_ready(2)
    for copy in og_copies:
        copy.wait_recv()
    own_og.wait()
    forward_x(3)
    weights_ready(3)

    def zero_rows(r):
        ffn[r, :] = jnp.zeros((64, 512), F32)
        norm_grad[r, :] = jnp.zeros((64, 512), F32)

    rows_loop(512, 64, zero_rows)

    def feed(i):
        jy = lax.rem(1 - hy + lax.div(i, 2), 2)
        jc = lax.rem(1 - hc + lax.rem(i, 2), 2)
        j = 2 * jy + jc
        work[...] = mm(normed_two[...], w_u[j])
        work_two[...] = mm(ogs[...], w_d[j], "NT")

        def step(r):
            v = work[r, :]
            sigma = 1.0 / (1.0 + jnp.exp(-v))
            hid[r, :] = (v * sigma).astype(BF16)
            hid_grad[r, :] = (work_two[r, :] * (sigma * (1.0 + v * (1.0 - sigma)))).astype(BF16)

        rows_loop(512, 64, step)
        part[0, jy, jc] = mm(hid[...], ogs[...], "TN").astype(BF16)
        part[1, jy, jc] = mm(normed_two[...], hid_grad[...], "TN").astype(BF16)
        ffn[...] += mm(hid[...], w_d[j])
        norm_grad[...] += mm(hid_grad[...], w_u[j], "NT")

    loop(4, feed)

    rpz = max(16, 256 // pairs)
    lane_width = 256 * 512 // pairs // rpz
    per_row = 512 // lane_width

    def piece(index):
        row = lax.div(index, per_row) * rpz
        return (
            pl.ds(pl.multiple_of(par * 256 + row, 16), rpz),
            pl.ds(pl.multiple_of(lax.rem(index, per_row) * lane_width, 128), lane_width),
        )

    def start_core(u):
        return [
            start(remote(part.at[u, jy, 1 - hc], buf_core.at[u, jy], core))
            for jy in (1 - hy, hy)
        ]

    def add_core(u, jy):
        def step(r):
            part[u, jy, hc, r, :] = (
                part[u, jy, hc, r, :].astype(F32) + buf_core[u, jy, r, :].astype(F32)
            ).astype(BF16)

        rows_loop(512, 128, step)

    def start_y(u):
        return start(remote(part.at[u, 1 - hy, hc], buf_y.at[u], ypeer))

    def add_y(u):
        def step(r):
            part[u, hy, hc, r, :] = (
                part[u, hy, hc, r, :].astype(F32) + buf_y[u, r, :].astype(F32)
            ).astype(BF16)

        rows_loop(512, 128, step)

    def start_x(u):
        rows = pl.ds(pl.multiple_of((1 - par) * 256, 256), 256)
        return start(remote(part.at[u, hy, hc, rows], buf_x.at[u], xpeer))

    def add_x(u):
        def step(r):
            rows = pl.ds(pl.multiple_of(par * 256 + r.start, 64), 64)
            part[u, hy, hc, rows, :] = (
                part[u, hy, hc, rows, :].astype(F32) + buf_x[u, r, :].astype(F32)
            ).astype(BF16)

        rows_loop(256, 64, step)

    def start_ring(u):
        copies = []
        for d in range(1, pairs):
            to, device = ring(d)
            rows, cols = piece(to)
            copies.append(
                start(remote(part.at[u, hy, hc, rows, cols], buf_ring.at[u, d - 1], device))
            )
        return copies

    def add_ring(u):
        rows, cols = piece(pair)
        total = part[u, hy, hc, rows, cols].astype(F32)
        for d in range(1, pairs):
            total = total + buf_ring[u, d - 1].astype(F32)
        own_piece[u] = total.astype(BF16)

    def start_spread(u):
        rows, cols = piece(pair)
        copies = [
            start(remote(own_piece.at[u], fin.at[u, rows, cols], ring(d)[1]))
            for d in range(1, pairs)
        ]
        return copies, local(own_piece.at[u], fin.at[u, rows, cols])

    def start_back(u):
        return start(remote(fin.at[u, half256], fin.at[u, half256], xpeer))

    core_copies = {0: start_core(0), 1: start_core(1)}

    gain_part[0] = jnp.zeros((8, 512), F32)
    row_512 = lax.broadcasted_iota(jnp.int32, (8, 512), 0)

    def norm_back(grad_ref, gain, unit_ref, rstd_ref, base, sink, row):
        def step(r):
            grad = grad_ref[r, :]
            unit = unit_ref[r, :]
            scaled = grad * gain[...]
            mean_one = jnp.mean(scaled, axis=-1, keepdims=True)
            mean_two = jnp.mean(scaled * unit, axis=-1, keepdims=True)
            rstd = rstd_ref[r, :]
            rstd = jnp.concatenate([rstd] * 4, axis=1)
            sink(r, base(r) + rstd * (scaled - mean_one - unit * mean_two))
            total = jnp.sum(grad * unit, axis=0, keepdims=True)
            gain_part[0] = gain_part[0] + jnp.where(row_512 == row, total, 0.0)

        rows_loop(512, 64, step)

    def sink_middle(r, grad):
        middle_grad[r, :] = grad
        middle_low[r, :] = grad.astype(BF16)
        lo_s[r, :] = (middle[r, :] + ffn[r, :]).astype(BF16)

    norm_back(
        norm_grad, gain_two, unit_two, rstd_two, lambda r: ogs[r, :].astype(F32), sink_middle, 1
    )

    y_copies = {}
    for u in (0, 1):
        core_copies[u][0].wait_recv()
        add_core(u, 1 - hy)
        y_copies[u] = start_y(u)
        core_copies[u][1].wait_recv()
        add_core(u, hy)

    def out_weight(j):
        part[2, lax.div(j, 2), lax.rem(j, 2), pl.ds(384, 128), :] = mm(
            attn[:, at128(j)], middle_low[...], "TN"
        ).astype(BF16)

    loop(4, out_weight)
    work[...] = mm(middle_low[...], w_o[...], "NT")

    head_ones = jnp.where(spread, 1.0, 0.0).astype(BF16)
    head_ones = jnp.concatenate([head_ones, head_ones], axis=0)
    first_lane = lax.rem(lane, 64) == 0
    second_lane = lax.rem(lane, 64) == 1

    def split(wide):
        high = wide.astype(BF16)
        return high, (wide - high.astype(F32)).astype(BF16)

    grad_z[...] = jnp.zeros_like(grad_z)

    def outer(i):
        b, pr, rows, cols = place(i)
        grad, inverse = work[rows, cols], den_inv[rows, cols]
        gnum = (grad * inverse).astype(BF16)
        high, low = split(grad * attn_wide[rows, cols])
        gden = -mm(jnp.concatenate([high, low], axis=1), head_ones) * inverse
        dhigh = gden.astype(BF16).astype(F32)
        num_grad[rows, cols] = gnum
        den_grad[rows, cols] = jnp.where(
            first_lane, dhigh, jnp.where(second_lane, gden - dhigh, 0.0)
        ).astype(BF16)
        queries = feat[0, rows, cols].astype(F32) * carry_on[b]
        grad_s[b, packed_rows(pr), :] = pack(mm(queries.astype(BF16), gnum, "TN"))
        grad_z[b, pl.ds(pr, 1), :] = jnp.sum(queries * gden, axis=0, keepdims=True)

    loop(8, outer)
    msg_gs[...] = (grad_s[0] + keep_first * grad_s[1]).astype(BF16)
    msg_gz[...] = jnp.where(row8 == 4, keep_first * keep_mid, grad_z[0] + keep_first * grad_z[1])
    backward = [shift(-d, msg_gs, msg_gz, buf_gs, buf_gz, d - 1) for d in (1, 2)]
    for d, copies in zip((1, 2), backward):

        @pl.when(pair >= d)
        def _():
            for copy in copies:
                copy.start()

    marks = jnp.where(first_lane | second_lane, 1.0, 0.0).astype(BF16)
    marks = jnp.broadcast_to(marks, (256, 128))

    def inner(i):
        b, pr, rows, cols = place(i)
        q, k, v = feat[0, rows, cols], feat[1, rows, cols], val[rows, cols]
        gnum, gden = num_grad[rows, cols], den_grad[rows, cols]
        q_two, gnum_two = two(q), two(gnum)
        grads = jnp.concatenate([gnum_two, two(gden)], axis=1)
        values = jnp.concatenate([v, marks], axis=1)
        m, mt = mask[b], mask_t[b]
        gsc = mm(grads, values, "NT")
        gsc = jnp.concatenate([gsc[:256] * m, gsc[256:] * m], axis=0).astype(BF16)
        qgrad = pick(mm(gsc, k)) + carry_on[b] * mm(
            jnp.concatenate([gnum, gden], axis=1), state[i], "NT"
        )
        low_grads[0, rows, cols] = (qgrad * jnp.minimum(q.astype(F32), 1.0)).astype(BF16)
        gsc_t = mm(values, grads, "NT")
        gsc_t = jnp.concatenate([gsc_t[:, :256] * mt, gsc_t[:, 256:] * mt], axis=1).astype(BF16)
        key_acc[rows, cols] = mm(gsc_t, q_two)
        sc_t = mm(k, q_two, "NT")
        sc_t = jnp.concatenate([sc_t[:, :256] * mt, sc_t[:, 256:] * mt], axis=1).astype(BF16)
        val_acc[rows, cols] = mm(sc_t, gnum_two)

    loop(8, inner)

    x_copies = {}
    for u in (0, 1):
        y_copies[u].wait_recv()
        add_y(u)
        x_copies[u] = start_x(u)

    for d, copies in zip((1, 2), backward):

        @pl.when(pair + d < pairs)
        def _():
            for copy in copies:
                copy.wait_recv()

    pass_on = buf_gz[0, pl.ds(4, 1), :]
    buf_gz[0] = buf_gz[0] + pass_on * buf_gz[1]

    def leave(i):
        b, pr, rows, cols = place(i)
        leaving = buf_gs[0, packed_rows(pr), :].astype(F32) + pass_on * buf_gs[
            1, packed_rows(pr), :
        ].astype(F32)
        z_leaving = buf_gz[0, pl.ds(pr, 1), :]
        first_block = (1 - b).astype(F32)
        scale = first_block * keep_mid + (1.0 - first_block)
        leaving = scale * leaving + first_block * grad_s[1, packed_rows(pr), :]
        z_leaving = scale * z_leaving + first_block * grad_z[1, pl.ds(pr, 1), :]
        square = unpack(leaving).astype(BF16)
        k, v = feat[1, rows, cols], val[rows, cols]
        tail = seg_col[b] == seg_col[b, pl.ds(255, 1), :]
        kgrad = key_acc[rows, cols] + jnp.where(tail, mm(v, square, "NT") + z_leaving, 0.0)
        low_grads[1, rows, cols] = (kgrad * jnp.minimum(k.astype(F32), 1.0)).astype(BF16)
        vgrad = val_acc[rows, cols] + jnp.where(tail, mm(k, square), 0.0)
        low_grads[2, rows, cols] = vgrad.astype(BF16)

    loop(8, leave)

    def qkv_weight(n):
        j, i = lax.div(n, 3), lax.rem(n, 3)
        part[2, lax.div(j, 2), lax.rem(j, 2), at128(i), :] = mm(
            low_grads[i, :, at128(j)], normed[...], "TN"
        ).astype(BF16)

    loop(12, qkv_weight)
    core_copies[2] = start_core(2)

    norm_grad[...] = mm(low_grads[0], w_qkv[0], "NT")
    norm_grad[...] += mm(low_grads[1], w_qkv[1], "NT")
    norm_grad[...] += mm(low_grads[2], w_qkv[2], "NT")

    core_copies[2][0].wait_recv()
    add_core(2, 1 - hy)
    y_copies[2] = start_y(2)
    core_copies[2][1].wait_recv()
    add_core(2, hy)

    def sink_input(r, grad):
        ig_s[r, :] = grad.astype(BF16)

    norm_back(norm_grad, gain_one, unit_one, rstd_one, lambda r: middle_grad[r, :], sink_input, 0)
    lo_copies, lo_own = scatter_out(lo_s, lo_out)
    ig_copies, ig_own = scatter_out(ig_s, ig_out)

    ring_copies, spread_copies, back_copies = {}, {}, {}

    def x_done(u):
        x_copies[u].wait_recv()
        add_x(u)
        ring_copies[u] = start_ring(u)

    def ring_done(u):
        for copy in ring_copies[u]:
            copy.wait_recv()
        add_ring(u)
        spread_copies[u] = start_spread(u)

    def spread_done(u):
        for copy in spread_copies[u][0]:
            copy.wait_recv()
        spread_copies[u][1].wait()
        back_copies[u] = start_back(u)

    def gain_stage(n, device):
        copy = start(remote(gain_part.at[n], gain_buf.at[n], device))
        copy.wait_recv()
        gain_part[n + 1] = gain_part[n] + gain_buf[n]

    x_done(0)
    gain_stage(0, core)
    x_done(1)
    gain_stage(1, ypeer)
    ring_done(0)
    gain_stage(2, xpeer)
    y_copies[2].wait_recv()
    add_y(2)
    x_copies[2] = start_x(2)
    ring_done(1)
    gain_copies = [
        start(remote(gain_part.at[3], gain_buf.at[2 + d], ring(d)[1])) for d in range(1, pairs)
    ]
    spread_done(0)
    x_done(2)
    spread_done(1)
    for copy in gain_copies:
        copy.wait_recv()
    total = gain_part[3]
    for d in range(1, pairs):
        total = total + gain_buf[2 + d]
    gain_part[4] = total
    gains[...] = gain_part[4, :, hcol]
    ring_done(2)
    spread_done(2)

    for u in range(UNITS):
        back_copies[u].wait_recv()
    for copy in lo_copies + ig_copies:
        copy.wait_recv()
    lo_own.wait()
    ig_own.wait()
    for copy in sends:
        copy.wait_send()
    for d in (1, 2):

        @pl.when(pair + d < pairs)
        def _():
            for copy in forward[d - 1]:
                copy.wait_send()

        @pl.when(pair >= d)
        def _():
            for copy in backward[d - 1]:
                copy.wait_send()


def widen_kernel(ig, fin, ig_o, q_o, k_o, v_o, o_o, u_o, d_o):
    ig_o[...] = ig[...].astype(F32)
    d_o[...] = fin[0].astype(F32)
    u_o[...] = fin[1].astype(F32)
    for i, out in enumerate((q_o, k_o, v_o)):
        out[...] = fin[2, i * 128 : (i + 1) * 128].astype(F32).T
    o_o[...] = fin[2, 384:].astype(F32)


def body(
    tokens,
    norm_gain,
    query_weight,
    key_weight,
    value_weight,
    attention_output_weight,
    feedforward_norm_gain,
    up_weight,
    down_weight,
    segment_ids,
    out_grad,
):
    batch, length, share = tokens.shape
    width, head_cols = query_weight.shape
    units = up_weight.shape[1]
    pairs = lax.axis_size("seq") // 2
    assert lax.axis_size("head") == 4 and batch == 8 and length == BLOCK
    assert (width, share, head_cols, units) == (512, 128, 128, 512)
    others = pairs - 1
    rpz = max(16, 256 // pairs)
    lane_width = 256 * 512 // pairs // rpz
    anywhere = pl.BlockSpec(memory_space=pl.ANY)
    vmem = pl.BlockSpec(memory_space=pltpu.VMEM)
    copies = 7 * 4 + 1 + 5 * KINDS + 8 + UNITS * (5 + 2 * others) + 3 + others
    scratch = [
        pltpu.VMEM((512, 512), BF16),
        pltpu.VMEM((512, 512), BF16),
        pltpu.VMEM((3, 512, 512), BF16),
        pltpu.VMEM((512, 512), BF16),
        pltpu.VMEM((4, 512, 512), BF16),
        pltpu.VMEM((4, 512, 512), BF16),
        pltpu.VMEM((8, 256), jnp.int32),
        pltpu.VMEM((512, 512), F32),
        pltpu.VMEM((512, 512), F32),
        pltpu.VMEM((512, 128), F32),
        pltpu.VMEM((512, 128), F32),
        pltpu.VMEM((512, 512), BF16),
        pltpu.VMEM((512, 512), BF16),
        pltpu.VMEM((2, 512, 512), BF16),
        pltpu.VMEM((512, 512), BF16),
        pltpu.VMEM((2, 256, 256), F32),
        pltpu.VMEM((2, 256, 256), F32),
        pltpu.VMEM((2, 256, 128), F32),
        pltpu.VMEM((2, 256, 128), F32),
        pltpu.VMEM((2, 256, 128), F32),
        pltpu.VMEM((2, 8, 128), F32),
        pltpu.VMEM((256, 128), BF16),
        pltpu.VMEM((8, 128), F32),
        pltpu.VMEM((2, 256, 128), BF16),
        pltpu.VMEM((2, 8, 128), F32),
        pltpu.VMEM((8, 128, 256), BF16),
        pltpu.VMEM((512, 512), BF16),
        pltpu.VMEM((512, 512), F32),
        pltpu.VMEM((512, 512), F32),
        pltpu.VMEM((512, 512), F32),
        pltpu.VMEM((512, 512), F32),
        pltpu.VMEM((512, 512), F32),
        pltpu.VMEM((512, 512), BF16),
        pltpu.VMEM((512, 512), BF16),
        pltpu.VMEM((512, 512), F32),
        pltpu.VMEM((512, 512), F32),
        pltpu.VMEM((512, 512), F32),
        pltpu.VMEM((512, 512), BF16),
        pltpu.VMEM((512, 512), BF16),
        pltpu.VMEM((512, 512), BF16),
        pltpu.VMEM((2, 256, 128), F32),
        pltpu.VMEM((2, 8, 128), F32),
        pltpu.VMEM((256, 128), BF16),
        pltpu.VMEM((8, 128), F32),
        pltpu.VMEM((2, 256, 128), BF16),
        pltpu.VMEM((2, 8, 128), F32),
        pltpu.VMEM((512, 512), F32),
        pltpu.VMEM((512, 512), F32),
        pltpu.VMEM((3, 512, 512), BF16),
        pltpu.VMEM((512, 512), BF16),
        pltpu.VMEM((512, 512), BF16),
        pltpu.VMEM((UNITS, 2, 2, 512, 512), BF16),
        pltpu.VMEM((UNITS, 2, 512, 512), BF16),
        pltpu.VMEM((UNITS, 512, 512), BF16),
        pltpu.VMEM((UNITS, 256, 512), BF16),
        pltpu.VMEM((UNITS, others, rpz, lane_width), BF16),
        pltpu.VMEM((UNITS, rpz, lane_width), BF16),
        pltpu.VMEM((5, 8, 512), F32),
        pltpu.VMEM((3 + others, 8, 512), F32),
        pltpu.SemaphoreType.DMA((16,)),
        pltpu.SemaphoreType.DMA((copies,)),
        pltpu.SemaphoreType.DMA((copies,)),
    ]
    lo, ig, fin, gains = pl.pallas_call(
        functools.partial(layer_kernel, pairs),
        out_shape=(
            jax.ShapeDtypeStruct((batch, length, share), BF16),
            jax.ShapeDtypeStruct((batch, length, share), BF16),
            jax.ShapeDtypeStruct((UNITS, 512, 512), BF16),
            jax.ShapeDtypeStruct((8, 128), F32),
        ),
        in_specs=[anywhere] * 8 + [vmem] * 3,
        out_specs=(anywhere, anywhere, anywhere, vmem),
        scratch_shapes=scratch,
        compiler_params=pltpu.CompilerParams(
            collective_id=0, has_side_effects=True, vmem_limit_bytes=56 * MIB
        ),
        cost_estimate=pl.CostEstimate(
            flops=11 * 10**9, bytes_accessed=8 * MIB, transcendentals=4 * 10**6
        ),
        name="layer",
    )(
        tokens,
        out_grad,
        query_weight,
        key_weight,
        value_weight,
        attention_output_weight,
        up_weight,
        down_weight,
        segment_ids,
        norm_gain[None],
        feedforward_norm_gain[None],
    )
    wide = pl.pallas_call(
        widen_kernel,
        out_shape=(
            jax.ShapeDtypeStruct((batch, length, share), F32),
            jax.ShapeDtypeStruct((512, 128), F32),
            jax.ShapeDtypeStruct((512, 128), F32),
            jax.ShapeDtypeStruct((512, 128), F32),
            jax.ShapeDtypeStruct((128, 512), F32),
            jax.ShapeDtypeStruct((512, 512), F32),
            jax.ShapeDtypeStruct((512, 512), F32),
        ),
        in_specs=[vmem] * 2,
        out_specs=(vmem,) * 7,
        compiler_params=pltpu.CompilerParams(vmem_limit_bytes=32 * MIB),
        name="widen",
    )(ig, fin)
    ig_w, q_w, k_w, v_w, o_w, u_w, d_w = wide
    return (lo, ig_w, gains[0], q_w, k_w, v_w, o_w, gains[1], u_w, d_w)


def solution(mesh):
    in_specs = (
        P(None, "seq", "head"),
        P(),
        P(None, "head"),
        P(None, "head"),
        P(None, "head"),
        P("head", None),
        P(),
        P(None, "head"),
        P("head", None),
        P(None, "seq"),
        P(None, "seq", "head"),
    )
    out_specs = (
        P(None, "seq", "head"),
        P(None, "seq", "head"),
        P("head"),
        P(None, "head"),
        P(None, "head"),
        P(None, "head"),
        P("head", None),
        P("head"),
        P(None, "head"),
        P("head", None),
    )
    return jax.shard_map(body, mesh=mesh, in_specs=in_specs, out_specs=out_specs, check_vma=False)
```

```python
import functools
from types import SimpleNamespace

import jax
import jax.numpy as jnp
from jax import lax
from jax.experimental import pallas as pl
from jax.experimental.pallas import tpu as pltpu
from jax.sharding import PartitionSpec as P

DH = 64
BLOCK = 256
EPSILON = 1e-05
MESH = pl.DeviceIdType.MESH
F32 = jnp.float32
BF16 = jnp.bfloat16
MIB = 1 << 20
KINDS = 4
OWNERS = 4
CHUNKS = (
    (0, 0, 512, 0, 256, True),
    (0, 0, 512, 256, 256, True),
    (1, 0, 512, 0, 256, False),
    (1, 0, 512, 256, 256, False),
    (2, 384, 128, 0, 512, True),
    (2, 0, 384, 0, 256, True),
    (2, 0, 384, 256, 256, False),
)
COMBOS = ((0, 1, 0), (0, 1, 1), (1, 1, 0), (1, 1, 1), (1, 0, 0), (1, 0, 1), (0, 0, 1))


def mm(left, right, form="NN"):
    dims = {"NN": ((1,), (0,)), "NT": ((1,), (1,)), "TN": ((0,), (0,))}[form]
    return lax.dot_general(left, right, (dims, ((), ())), preferred_element_type=F32)


def loop(count, step):
    def run(i, carry):
        step(i)
        return carry

    lax.fori_loop(0, count, run, 0)


def span(start, size, multiple=None):
    return pl.ds(pl.multiple_of(start, multiple or size), size)


def rows_loop(total, chunk, step):
    loop(total // chunk, lambda i: step(span(i * chunk, chunk)))


def at128(i):
    return span(i * 128, 128)


def layer_kernel(pairs, names, *refs):
    (tok, og_in, wq, wk, wv, wo, wu, wd, seg, gain_one, gain_two) = refs[:11]
    (lo_out, ig_out, fin, gains) = refs[11:15]
    r_ = SimpleNamespace(**dict(zip(names, refs[15:])))
    chunk_refs = refs[15 + len(names) : -3]
    local_sem, send_sem, recv_sem = refs[-3:]
    xin, ogs, w_qkv, w_o, w_u = (
        r_.xin, r_.ogs, r_.w_qkv, r_.w_o, r_.w_u,
    )
    w_d, unit_one, unit_two, rstd_one, rstd_two = (
        r_.w_d, r_.unit_one, r_.unit_two, r_.rstd_one, r_.rstd_two,
    )
    normed, normed_two, feat, val, mask = (
        r_.normed, r_.normed_two, r_.feat, r_.val, r_.mask,
    )
    seg_col, carry_on, state, scores_low, own_s = (
        r_.seg_col, r_.carry_on, r_.state, r_.scores_low, r_.own_s,
    )
    own_z, msg_s, msg_z, buf_s, buf_z = (
        r_.own_z, r_.msg_s, r_.msg_z, r_.buf_s, r_.buf_z,
    )
    grad_s, grad_z, msg_gs, msg_gz, buf_gs = (
        r_.grad_s, r_.grad_z, r_.msg_gs, r_.msg_gz, r_.buf_gs,
    )
    buf_gz, attn, attn_wide, den_inv, middle = (
        r_.buf_gz, r_.attn, r_.attn_wide, r_.den_inv, r_.middle,
    )
    work, work_two, hid, hid_grad, ffn = (
        r_.work, r_.work_two, r_.hid, r_.hid_grad, r_.ffn,
    )
    norm_grad, middle_grad, middle_low, num_grad, den_grad = (
        r_.norm_grad, r_.middle_grad, r_.middle_low, r_.num_grad, r_.den_grad,
    )
    key_acc, val_acc, low_grads, lo_s, ig_s = (
        r_.key_acc, r_.val_acc, r_.low_grads, r_.lo_s, r_.ig_s,
    )
    part, buf_core, gain_part, gain_buf, seg_other = (
        r_.part, r_.buf_core, r_.gain_part, r_.gain_buf, r_.seg_other,
    )

    s = lax.axis_index("seq")
    h = lax.axis_index("head")
    pair, par = lax.div(s, 2), lax.rem(s, 2)
    hy, hc = lax.div(h, 2), lax.rem(h, 2)
    member = par * 4 + h
    zb = lax.rem(pair, 2)

    counter = [0]
    sends = []
    local_ids = iter(range(1000))

    def take(n=1):
        counter[0] += n
        return counter[0] - n

    def guarded(cond, act):
        if cond is None:
            act()
        else:
            pl.when(cond)(act)

    def peer(dp, dy, dc):
        return (1 - par if dp else par, 1 - hy if dy else hy, 1 - hc if dc else hc)

    def address(par_to, y_to, c_to):
        return (2 * pair + par_to, 2 * y_to + c_to)

    core, ypeer, xpeer = (address(*peer(*d)) for d in ((0, 0, 1), (0, 1, 0), (1, 0, 0)))
    zpeer = (2 * (pair + 1 - 2 * zb) + par, h)

    def ring(d):
        to = lax.rem(pair + d, pairs)
        return to, (2 * to + par, h)

    def remote(src, dst, device, i=None):
        i = take() if i is None else i
        return pltpu.make_async_remote_copy(
            src_ref=src,
            dst_ref=dst,
            send_sem=send_sem.at[i],
            recv_sem=recv_sem.at[i],
            device_id=device,
            device_id_type=MESH,
        )

    def start(copy):
        copy.start()
        sends.append(copy)
        return copy

    def send(src, dst, device):
        return start(remote(src, dst, device))

    def local(src, dst):
        copy = pltpu.make_async_copy(src, dst, local_sem.at[next(local_ids)])
        copy.start()
        return copy

    def each_ring(act):
        if pairs <= 4:
            for d in range(1, pairs):
                act(d)
        else:
            loop(pairs - 1, lambda i: act(i + 1))

    hcol = at128(h)
    half256 = span(par * 256, 256)
    own_w = [
        [local(w, w_qkv.at[i, :, hcol]) for i, w in enumerate((wq, wk, wv))],
        [local(wo, w_o.at[hcol])],
        [local(wu, w_u.at[h])],
        [local(wd, w_d.at[h])],
    ]
    own_tok = local(tok.at[member], xin.at[half256, hcol])
    own_og = local(og_in.at[member], ogs.at[half256, hcol])
    row8 = lax.broadcasted_iota(jnp.int32, (8, 128), 0)
    neutral = jnp.where(row8 == 4, -1.0, 0.0).astype(F32)
    for slot in range(2):
        buf_s[slot] = jnp.zeros((256, 128), BF16)
        buf_gs[slot] = jnp.zeros((256, 128), BF16)
        buf_gz[slot] = jnp.zeros((8, 128), F32)
        for order in range(2):
            buf_z[slot, order] = neutral

    barrier = pltpu.get_barrier_semaphore()
    for d in COMBOS:
        pl.semaphore_signal(barrier, inc=1, device_id=address(*peer(*d)), device_id_type=MESH)
    each_ring(
        lambda d: pl.semaphore_signal(
            barrier, inc=1, device_id=ring(d)[1], device_id_type=MESH
        )
    )
    pl.semaphore_wait(barrier, len(COMBOS) + pairs - 1)

    def scatter_in(src, dst):
        copies = []
        for d in COMBOS:
            par_to, y_to, c_to = peer(*d)
            copies.append(
                send(
                    src.at[par_to * 4 + 2 * y_to + c_to],
                    dst.at[half256, hcol],
                    address(par_to, y_to, c_to),
                )
            )
        return copies

    def scatter_out(src, dst):
        copies = []
        for d in COMBOS:
            par_to, y_to, c_to = peer(*d)
            copies.append(
                send(
                    src.at[span(par_to * 256, 256), at128(2 * y_to + c_to)],
                    dst.at[member],
                    address(par_to, y_to, c_to),
                )
            )
        return copies, local(src.at[half256, hcol], dst.at[member])

    across = 2 * (1 - hy) + hc
    quarter = par + 2 * zb
    quarter_x = 1 - par + 2 * zb
    quarter_z = par + 2 * (1 - zb)
    quarter_far = 1 - par + 2 * (1 - zb)

    def view(kind, shard, eighth=None, eighths=2):
        rows = 32 if kind == 1 else 128
        unit = rows // 2
        if kind == 0:
            where = slice(None) if eighth is None else span(eighth * unit, unit * eighths, unit)
            return w_qkv.at[:, where, at128(shard)]
        if kind == 1:
            if eighth is None:
                return w_o.at[at128(shard)]
            return w_o.at[span(shard * 128 + eighth * unit, unit * eighths, unit)]
        ref = w_u if kind == 2 else w_d
        if eighth is None:
            return ref.at[shard]
        return ref.at[shard, span(eighth * unit, unit * eighths, unit)]

    wt = {}

    def pass_on_weight(kind, eighth, eighths, device, shard=None):
        ref = view(kind, across if shard is None else shard, eighth, eighths)
        return send(ref, ref, device)

    def weight_y(kind):
        wt[kind, "y"] = pass_on_weight(kind, 2 * quarter, 2, ypeer, h)

    def weight_core(kind):
        own = view(kind, h)
        wt[kind, "c"] = [send(own, own, core)]

    def weight_near(kind):
        wt[kind, "y"].wait_recv()
        wt[kind, "x"] = pass_on_weight(kind, 2 * quarter, 2, xpeer)
        wt[kind, "z"] = pass_on_weight(kind, 2 * quarter, 2, zpeer)
        wt[kind, "c"].append(pass_on_weight(kind, 2 * quarter, 2, core))

    def weight_far(kind):
        wt[kind, "x"].wait_recv()
        wt[kind, "z2"] = pass_on_weight(kind, 2 * quarter_x, 1, zpeer)
        wt[kind, "c"].append(pass_on_weight(kind, 2 * quarter_x, 2, core))
        wt[kind, "z"].wait_recv()
        wt[kind, "x2"] = pass_on_weight(kind, 2 * quarter_z + 1, 1, xpeer)
        wt[kind, "c"].append(pass_on_weight(kind, 2 * quarter_z, 2, core))

    def weight_last(kind):
        wt[kind, "z2"].wait_recv()
        wt[kind, "x2"].wait_recv()
        wt[kind, "c"].append(pass_on_weight(kind, 2 * quarter_far, 2, core))

    def weight_own(kind):
        wt[kind, "c"][0].wait_recv()

    def weight_ready(kind):
        for copy in wt[kind, "c"][1:]:
            copy.wait_recv()

    for copy in own_w[0]:
        copy.wait()
    weight_y(0)
    tokens_in = scatter_in(tok, xin)
    seg_copy = send(seg, seg_other, xpeer)
    weight_core(0)
    for kind in (1, 2, 3):
        for copy in own_w[kind]:
            copy.wait()
        weight_core(kind)
    weight_near(0)
    for copy in tokens_in:
        copy.wait_recv()
    own_tok.wait()
    for kind in (1, 2, 3):
        weight_y(kind)

    def norm_rows(source, gain, unit_ref, rstd_ref, out_ref):
        def step(r):
            x = source(r)
            center = x - jnp.mean(x, axis=-1, keepdims=True)
            scale = lax.rsqrt(jnp.mean(center * center, axis=-1, keepdims=True) + EPSILON)
            unit = center * scale
            unit_ref[r, :] = unit
            rstd_ref[r, :] = jnp.broadcast_to(scale, (unit.shape[0], 128))
            out_ref[r, :] = (unit * gain[...]).astype(BF16)

        rows_loop(512, 64, step)

    norm_rows(lambda r: xin[r, :].astype(F32), gain_one, unit_one, rstd_one, normed)

    seg_copy.wait_recv()
    own_row = seg[pl.ds(member, 1), :]
    other_row = seg_other[pl.ds(member, 1), :]
    seg_rows = (
        (own_row * (1 - par) + other_row * par).astype(F32),
        (own_row * par + other_row * (1 - par)).astype(F32),
    )
    first = lax.broadcasted_iota(jnp.int32, (256, 256), 0)
    second = lax.broadcasted_iota(jnp.int32, (256, 256), 1)
    for b in range(2):
        along = jnp.broadcast_to(seg_rows[b], (256, 256))
        down = along.T
        mask[b] = jnp.where((along == down) & (second <= first), 1.0, 0.0)
        seg_col[b] = down[:, :128]
    weight_far(0)
    weight_own(0)

    lane = lax.broadcasted_iota(jnp.int32, (1, 128), 1)
    low_lanes = lane < 64
    spread = (
        lax.broadcasted_iota(jnp.int32, (128, 128), 0) // 64
        == lax.broadcasted_iota(jnp.int32, (128, 128), 1) // 64
    )

    def place(i):
        b, pr = lax.div(i, 4), lax.rem(i, 4)
        return b, pr, span(b * 256, 256), at128(pr)

    def side_place(i, side):
        return place(lax.div(i, 2) * 4 + 2 * side + lax.rem(i, 2))

    def pack(square):
        return jnp.where(low_lanes, square[:64], square[64:])

    def two(rows):
        zero = jnp.zeros_like(rows)
        return jnp.concatenate(
            [jnp.where(low_lanes, rows, zero), jnp.where(low_lanes, zero, rows)], axis=0
        )

    def pick(stacked):
        return jnp.where(low_lanes, stacked[:256], stacked[256:])

    def packed_rows(pr):
        return span(pr * 64, 64)

    last_rows = [seg_col[b, pl.ds(255, 1), :] for b in range(2)]
    keep_mid = jnp.where(last_rows[0] >= last_rows[1], 1.0, 0.0)

    def project(side):
        cols = span(side * 256, 256)

        def step_kind(i):
            work[:, :256] = mm(normed[...], w_qkv[i, :, cols])

            def step(r):
                v = work[r, :256]
                feat[i, r, cols] = jnp.where(
                    v > 0, v + 1.0, jnp.exp(jnp.minimum(v, 0.0))
                ).astype(BF16)

            rows_loop(512, 64, step)

        loop(2, step_kind)
        val[:, cols] = mm(normed[...], w_qkv[2, :, cols]).astype(BF16)

    def own_state(i, side):
        b, pr, rows, cols = side_place(i, side)
        tail = seg_col[b] == seg_col[b, pl.ds(255, 1), :]
        keys = feat[1, rows, cols].astype(F32)
        keys = jnp.where(tail, keys, 0.0)
        own_s[b, packed_rows(pr), :] = pack(mm(keys.astype(BF16), val[rows, cols], "TN"))
        own_z[b, pl.ds(pr, 1), :] = jnp.sum(keys, axis=0, keepdims=True)

    def shift(d, pieces, base):
        to = lax.rem(pair + d + pairs, pairs)
        device = (2 * to + par, h)
        return [remote(src, dst, device, base + i) for i, (src, dst) in enumerate(pieces)]

    forward = {}

    def send_state(order, side):
        loop(4, lambda i: own_state(i, side))
        rows = span(side * 128, 128)
        msg_s[rows, :] = (own_s[1, rows, :] + keep_mid * own_s[0, rows, :]).astype(BF16)
        msg_z[order] = jnp.where(row8 == 4, last_rows[1], own_z[1] + keep_mid * own_z[0])
        for d in (1, 2):
            copies = shift(
                d,
                [
                    (msg_s.at[rows], buf_s.at[d - 1, rows]),
                    (msg_z.at[order], buf_z.at[d - 1, order]),
                ],
                take(2),
            )
            forward[order, d] = copies

            @pl.when(pair + d < pairs)
            def _():
                for copy in copies:
                    copy.start()

    own_z[...] = jnp.zeros_like(own_z)
    project(hy)
    send_state(0, hy)
    weight_last(0)
    og_copies = scatter_in(og_in, ogs)
    weight_near(1)
    weight_ready(0)
    project(1 - hy)
    send_state(1, 1 - hy)
    weight_near(2)
    weight_near(3)
    weight_far(1)

    ones = jnp.ones((256, 128), BF16)
    ready = {}

    def receive_state(order):
        for d in (1, 2):

            @pl.when(pair >= d)
            def _():
                for copy in forward[order, d]:
                    copy.wait_recv()

        if order == 0:
            last_in = buf_z[0, 0, pl.ds(4, 1), :]
            ready["keep_in"] = jnp.where(buf_z[1, 0, pl.ds(4, 1), :] >= last_in, 1.0, 0.0)
            ready["keep_first"] = jnp.where(last_in >= last_rows[0], 1.0, 0.0)
            carry_on[0] = jnp.where(seg_col[0] == last_in, 1.0, 0.0)
            carry_on[1] = jnp.where(seg_col[1] == last_rows[0], 1.0, 0.0)
        buf_z[0, order] = buf_z[0, order] + ready["keep_in"] * buf_z[1, order]

    def enter(order, side):
        def step(i):
            pr = 2 * side + i
            entering = buf_s[0, packed_rows(pr), :].astype(F32) + ready["keep_in"] * buf_s[
                1, packed_rows(pr), :
            ].astype(F32)
            z_in = buf_z[0, order, pl.ds(pr, 1), :]
            middle_s = own_s[0, packed_rows(pr), :] + ready["keep_first"] * entering
            middle_z = own_z[0, pl.ds(pr, 1), :] + ready["keep_first"] * z_in
            for b, (packed, z_row) in enumerate(((entering, z_in), (middle_s, middle_z))):
                wide = jnp.where(spread, jnp.broadcast_to(z_row, (128, 128)).T, 0.0)
                state[b * 4 + pr, :, :128] = two(packed).astype(BF16)
                state[b * 4 + pr, :, 128:] = wide.astype(BF16)

        loop(2, step)

    def attend(i, side):
        b, pr, rows, cols = side_place(i, side)
        q, k, v = feat[0, rows, cols], feat[1, rows, cols], val[rows, cols]
        scores = mm(two(q), k, "NT")
        m = mask[b]
        low = jnp.concatenate([scores[:256] * m, scores[256:] * m], axis=0).astype(BF16)
        scores_low[b * 4 + pr] = low
        both = mm(low, jnp.concatenate([v, ones], axis=1))
        carried = mm(q, state[b * 4 + pr])
        c = carry_on[b]
        numer = pick(both[:, :128]) + c * carried[:, :128]
        denom = pick(both[:, 128:]) + c * carried[:, 128:]
        inverse = 1.0 / denom
        result = numer * inverse
        den_inv[rows, cols] = inverse
        attn_wide[rows, cols] = result
        attn[rows, cols] = result.astype(BF16)

    for order, side in ((0, hy), (1, 1 - hy)):
        receive_state(order)
        enter(order, side)
        loop(4, lambda i: attend(i, side))
        if order == 0:
            weight_last(1)
            weight_far(2)
    keep_first = ready["keep_first"]
    weight_far(3)
    weight_own(1)
    weight_ready(1)

    work[...] = mm(attn[...], w_o[...])

    def mid_step(r):
        middle[r, :] = xin[r, :].astype(F32) + work[r, :]

    rows_loop(512, 64, mid_step)
    norm_rows(
        lambda r: middle[r, :].astype(BF16).astype(F32), gain_two, unit_two, rstd_two, normed_two
    )
    weight_last(2)
    weight_last(3)
    for copy in og_copies:
        copy.wait_recv()
    own_og.wait()
    for kind in (2, 3):
        weight_own(kind)
        weight_ready(kind)

    def core_send(view_src, view_dst):
        return send(view_src, view_dst, core)

    def add_core(u, jy, row, rows):
        def step(i):
            r = span(row + i * 64, 64)
            part[u, jy, hc, r, :] = (
                part[u, jy, hc, r, :].astype(F32) + buf_core[u, jy, r, :].astype(F32)
            ).astype(BF16)

        loop(rows // 64, step)

    owner = None if pairs == OWNERS else pair < OWNERS

    class Chunk:
        def __init__(self, n):
            self.u, self.row, self.rows, self.lane, self.lanes, self.y_first = CHUNKS[n]
            self.half = self.rows // 2
            self.piece = self.half // OWNERS
            self.buf, self.ring_buf, self.own = chunk_refs[3 * n : 3 * n + 3]
            self.cols = pl.ds(self.lane, self.lanes)
            self.devices = (ypeer, xpeer) if self.y_first else (xpeer, ypeer)
            self.ring_base = self.spread_base = None

        def rows_of(self, half, at=0, size=None):
            return span(self.row + half * self.half + at, size or self.half, 16)

        def at(self, jy, half):
            return part.at[self.u, jy, hc, self.rows_of(half), self.cols]

        def a(self):
            self.first = send(self.at(1 - hy, 1 - par), self.buf.at[0], self.devices[0])

        def b(self):
            source = (1 - hy, par) if self.y_first else (hy, 1 - par)
            self.other = send(self.at(*source), self.buf.at[1], self.devices[0])

        def mid(self):
            self.first.wait_recv()
            jy, half = (hy, 1 - par) if self.y_first else (1 - hy, par)

            def step(i):
                r = self.rows_of(half, i * self.piece, self.piece)
                got = self.buf[0, span(i * self.piece, self.piece), :].astype(F32)
                part[self.u, jy, hc, r, self.cols] = (
                    part[self.u, jy, hc, r, self.cols].astype(F32) + got
                ).astype(BF16)

            loop(OWNERS, step)
            self.second = send(self.at(jy, half), self.buf.at[2], self.devices[1])

        def ring_copy(self, d):
            to, device = ring(d)
            rows = self.rows_of(par, lax.rem(to, OWNERS) * self.piece, self.piece)
            copy = remote(
                part.at[self.u, hy, hc, rows, self.cols],
                self.ring_buf.at[d - 1],
                device,
                self.ring_base + d - 1,
            )
            return copy, None if pairs == OWNERS else to < OWNERS

        def ring(self):
            self.other.wait_recv()
            self.second.wait_recv()

            def step(i):
                r = self.rows_of(par, i * self.piece, self.piece)
                b = span(i * self.piece, self.piece)
                got = self.buf[1, b, :].astype(F32) + self.buf[2, b, :].astype(F32)
                part[self.u, hy, hc, r, self.cols] = (
                    part[self.u, hy, hc, r, self.cols].astype(F32) + got
                ).astype(BF16)

            loop(OWNERS, step)
            self.ring_base = take(pairs - 1)

            def go(d):
                copy, cond = self.ring_copy(d)
                guarded(cond, copy.start)

            each_ring(go)

        def final(self, index):
            rows = self.rows_of(par, lax.rem(index, OWNERS) * self.piece, self.piece)
            return fin.at[self.u, rows, self.cols]

        def spread_copy(self, d):
            return remote(
                self.own, self.final(pair), ring(d)[1], self.spread_base + d - 1
            )

        def spread(self):
            self.spread_base = take(pairs - 1)
            sem = local_sem.at[next(local_ids)]
            self.kept = pltpu.make_async_copy(self.own, self.final(pair), sem)

            def total():
                each_ring(lambda d: self.ring_copy(d)[0].wait_recv())
                rows = self.rows_of(par, lax.rem(pair, OWNERS) * self.piece, self.piece)
                self.own[...] = part[self.u, hy, hc, rows, self.cols]

                def more(d):
                    self.own[...] = (
                        self.own[...].astype(F32) + self.ring_buf[d - 1].astype(F32)
                    ).astype(BF16)

                if pairs == OWNERS:
                    value = part[self.u, hy, hc, rows, self.cols].astype(F32)
                    for d in range(1, pairs):
                        value = value + self.ring_buf[d - 1].astype(F32)
                    self.own[...] = value.astype(BF16)
                else:
                    each_ring(more)
                each_ring(lambda d: self.spread_copy(d).start())
                self.kept.start()

            guarded(owner, total)

        def back(self):
            def arrived(d):
                giver = lax.rem(pair - d + pairs, pairs)
                cond = None if pairs == OWNERS else giver < OWNERS
                guarded(cond, self.spread_copy(d).wait_recv)

            each_ring(arrived)
            guarded(owner, self.kept.wait)
            rows = fin.at[self.u, self.rows_of(par), self.cols]
            self.last = send(rows, rows, xpeer)

        def end(self):
            self.last.wait_recv()

        def sent(self):
            def one(d):
                copy, cond = self.ring_copy(d)
                guarded(cond, copy.wait_send)

            each_ring(one)
            guarded(owner, lambda: each_ring(lambda d: self.spread_copy(d).wait_send()))

    d0, d1, u0, u1, o0, a0, a1 = chunks = [Chunk(n) for n in range(len(CHUNKS))]

    def zero_rows(r):
        ffn[r, :] = jnp.zeros((64, 512), F32)
        norm_grad[r, :] = jnp.zeros((64, 512), F32)

    rows_loop(512, 64, zero_rows)

    def feed(jy):
        base = take()
        copy = remote(part.at[0:2, jy, 1 - hc], buf_core.at[0:2, jy], core, base)

        def one(i):
            jc = lax.rem(1 - hc + i, 2)
            j = 2 * jy + jc
            work[...] = mm(normed_two[...], w_u[j])
            work_two[...] = mm(ogs[...], w_d[j], "NT")

            def step(r):
                v = work[r, :]
                sigma = 1.0 / (1.0 + jnp.exp(-v))
                hid[r, :] = (v * sigma).astype(BF16)
                hid_grad[r, :] = (work_two[r, :] * (sigma * (1.0 + v * (1.0 - sigma)))).astype(
                    BF16
                )

            rows_loop(512, 64, step)
            part[0, jy, jc] = mm(hid[...], ogs[...], "TN").astype(BF16)
            part[1, jy, jc] = mm(normed_two[...], hid_grad[...], "TN").astype(BF16)

            @pl.when(i == 0)
            def _():
                copy.start()

            ffn[...] += mm(hid[...], w_d[j])
            norm_grad[...] += mm(hid_grad[...], w_u[j], "NT")

        loop(2, one)
        sends.append(copy)
        copy.wait_recv()
        add_core(0, jy, 0, 512)
        add_core(1, jy, 0, 512)

    feed(1 - hy)
    d0.a()
    u0.a()
    d1.a()
    u1.a()
    feed(hy)
    u0.b()
    u1.b()
    d0.b()
    d1.b()

    gain_part[0] = jnp.zeros((8, 512), F32)
    row_512 = lax.broadcasted_iota(jnp.int32, (8, 512), 0)

    def norm_back(grad_ref, gain, unit_ref, rstd_ref, base, sink, row):
        def step(r):
            grad = grad_ref[r, :]
            unit = unit_ref[r, :]
            scaled = grad * gain[...]
            mean_one = jnp.mean(scaled, axis=-1, keepdims=True)
            mean_two = jnp.mean(scaled * unit, axis=-1, keepdims=True)
            rstd = rstd_ref[r, :]
            rstd = jnp.concatenate([rstd] * 4, axis=1)
            sink(r, base(r) + rstd * (scaled - mean_one - unit * mean_two))
            total = jnp.sum(grad * unit, axis=0, keepdims=True)
            gain_part[0] = gain_part[0] + jnp.where(row_512 == row, total, 0.0)

        rows_loop(512, 64, step)

    def sink_middle(r, grad):
        middle_grad[r, :] = grad
        middle_low[r, :] = grad.astype(BF16)
        lo_s[r, :] = (middle[r, :] + ffn[r, :]).astype(BF16)

    norm_back(
        norm_grad, gain_two, unit_two, rstd_two, lambda r: ogs[r, :].astype(F32), sink_middle, 1
    )

    out_rows = pl.ds(384, 128)
    work_two[...] = mm(attn[...], middle_low[...], "TN")
    for j in range(4):
        part[2, j // 2, j % 2, out_rows, :] = work_two[j * 128 : (j + 1) * 128, :].astype(BF16)
    core_o = core_send(part.at[2, :, 1 - hc, out_rows], buf_core.at[2, :, out_rows])
    work[...] = mm(middle_low[...], w_o[...], "NT")

    head_ones = jnp.where(spread, 1.0, 0.0).astype(BF16)
    head_ones = jnp.concatenate([head_ones, head_ones], axis=0)
    first_lane = lax.rem(lane, 64) == 0
    second_lane = lax.rem(lane, 64) == 1

    def split(wide):
        high = wide.astype(BF16)
        return high, (wide - high.astype(F32)).astype(BF16)

    grad_z[...] = jnp.zeros_like(grad_z)

    def outer(i):
        b, pr, rows, cols = place(i)
        grad, inverse = work[rows, cols], den_inv[rows, cols]
        gnum = (grad * inverse).astype(BF16)
        high, low = split(grad * attn_wide[rows, cols])
        gden = -mm(jnp.concatenate([high, low], axis=1), head_ones) * inverse
        dhigh = gden.astype(BF16).astype(F32)
        num_grad[rows, cols] = gnum
        den_grad[rows, cols] = jnp.where(
            first_lane, dhigh, jnp.where(second_lane, gden - dhigh, 0.0)
        ).astype(BF16)
        queries = feat[0, rows, cols].astype(F32) * carry_on[b]
        grad_s[b, packed_rows(pr), :] = pack(mm(queries.astype(BF16), gnum, "TN"))
        grad_z[b, pl.ds(pr, 1), :] = jnp.sum(queries * gden, axis=0, keepdims=True)

    loop(8, outer)
    msg_gs[...] = (grad_s[0] + keep_first * grad_s[1]).astype(BF16)
    msg_gz[...] = jnp.where(row8 == 4, keep_first * keep_mid, grad_z[0] + keep_first * grad_z[1])
    backward = {}
    for d in (1, 2):
        pieces = [(msg_gs, buf_gs.at[d - 1]), (msg_gz, buf_gz.at[d - 1])]
        backward[d] = shift(-d, pieces, take(2))

        @pl.when(pair >= d)
        def _():
            for copy in backward[d]:
                copy.start()

    d0.mid()
    u0.mid()
    core_o.wait_recv()
    add_core(2, 0, 384, 128)
    add_core(2, 1, 384, 128)
    o0.a()
    o0.b()

    marks = jnp.where(first_lane | second_lane, 1.0, 0.0).astype(BF16)
    marks = jnp.broadcast_to(marks, (256, 128))

    def inner(i):
        b, pr, rows, cols = place(i)
        q, k, v = feat[0, rows, cols], feat[1, rows, cols], val[rows, cols]
        gnum, gden = num_grad[rows, cols], den_grad[rows, cols]
        gnum_two = two(gnum)
        grads = jnp.concatenate([gnum_two, two(gden)], axis=1)
        values = jnp.concatenate([v, marks], axis=1)
        m = mask[b]
        gsc = mm(grads, values, "NT")
        gsc = jnp.concatenate([gsc[:256] * m, gsc[256:] * m], axis=0).astype(BF16)
        qgrad = pick(mm(gsc, k)) + carry_on[b] * mm(
            jnp.concatenate([gnum, gden], axis=1), state[i], "NT"
        )
        low_grads[0, rows, cols] = (qgrad * jnp.minimum(q.astype(F32), 1.0)).astype(BF16)
        key_acc[rows, cols] = mm(gsc, two(q), "TN")
        val_acc[rows, cols] = mm(scores_low[i], gnum_two, "TN")

    loop(8, inner)

    d1.mid()
    u1.mid()
    o0.mid()
    for d in (1, 2):

        @pl.when(pair + d < pairs)
        def _():
            for copy in backward[d]:
                copy.wait_recv()

    pass_on = buf_gz[0, pl.ds(4, 1), :]
    buf_gz[0] = buf_gz[0] + pass_on * buf_gz[1]

    def leave(i):
        b, pr, rows, cols = place(i)
        leaving = buf_gs[0, packed_rows(pr), :].astype(F32) + pass_on * buf_gs[
            1, packed_rows(pr), :
        ].astype(F32)
        z_leaving = buf_gz[0, pl.ds(pr, 1), :]
        first_block = (1 - b).astype(F32)
        scale = first_block * keep_mid + (1.0 - first_block)
        leaving = scale * leaving + first_block * grad_s[1, packed_rows(pr), :]
        z_leaving = scale * z_leaving + first_block * grad_z[1, pl.ds(pr, 1), :]
        square = two(leaving).astype(BF16)
        k, v = feat[1, rows, cols], val[rows, cols]
        tail = seg_col[b] == seg_col[b, pl.ds(255, 1), :]
        kgrad = key_acc[rows, cols] + jnp.where(tail, mm(v, square, "NT") + z_leaving, 0.0)
        low_grads[1, rows, cols] = (kgrad * jnp.minimum(k.astype(F32), 1.0)).astype(BF16)
        vgrad = val_acc[rows, cols] + jnp.where(tail, mm(k, square), 0.0)
        low_grads[2, rows, cols] = vgrad.astype(BF16)

    loop(8, leave)

    def qkv_weight(i):
        work[...] = mm(low_grads[i], normed[...], "TN")
        for j in range(4):
            part[2, j // 2, j % 2, at128(i), :] = work[j * 128 : (j + 1) * 128, :].astype(BF16)

    loop(3, qkv_weight)
    qkv_rows = pl.ds(0, 384)
    core_a = [
        core_send(part.at[2, jy, 1 - hc, qkv_rows], buf_core.at[2, jy, qkv_rows])
        for jy in (1 - hy, hy)
    ]
    norm_grad[...] = mm(low_grads[0], w_qkv[0], "NT")
    core_a[0].wait_recv()
    add_core(2, 1 - hy, 0, 384)
    a0.a()
    a1.a()
    core_a[1].wait_recv()
    add_core(2, hy, 0, 384)
    a1.b()
    a0.b()
    d0.ring()
    u0.ring()
    norm_grad[...] += mm(low_grads[1], w_qkv[1], "NT")
    norm_grad[...] += mm(low_grads[2], w_qkv[2], "NT")
    lo_copies, lo_own = scatter_out(lo_s, lo_out)

    def sink_input(r, grad):
        ig_s[r, :] = grad.astype(BF16)

    norm_back(norm_grad, gain_one, unit_one, rstd_one, lambda r: middle_grad[r, :], sink_input, 0)

    def gain_stage(n, device):
        copy = send(gain_part.at[n], gain_buf.at[n], device)
        copy.wait_recv()
        gain_part[n + 1] = gain_part[n] + gain_buf[n]

    a0.mid()
    a1.mid()
    d1.ring()
    u1.ring()
    o0.ring()
    d0.spread()
    u0.spread()
    ig_copies, ig_own = scatter_out(ig_s, ig_out)
    a0.ring()
    a1.ring()
    gain_stage(0, core)
    d1.spread()
    u1.spread()
    o0.spread()
    d0.back()
    u0.back()
    gain_stage(1, ypeer)
    a0.spread()
    a1.spread()
    gain_stage(2, xpeer)
    gain_base = take(pairs - 1)

    def gain_copy(d):
        return remote(gain_part.at[3], gain_buf.at[2 + d], ring(d)[1], gain_base + d - 1)

    each_ring(lambda d: gain_copy(d).start())
    d1.back()
    u1.back()
    o0.back()
    a0.back()
    a1.back()
    each_ring(lambda d: gain_copy(d).wait_recv())
    gain_part[4] = gain_part[3]

    def add_gain(d):
        gain_part[4] = gain_part[4] + gain_buf[2 + d]

    each_ring(add_gain)
    gains[...] = gain_part[4, :, hcol]

    for chunk in chunks:
        chunk.end()
    for copy in lo_copies + ig_copies:
        copy.wait_recv()
    lo_own.wait()
    ig_own.wait()
    for copy in sends:
        copy.wait_send()
    for chunk in chunks:
        chunk.sent()
    each_ring(lambda d: gain_copy(d).wait_send())
    for d in (1, 2):

        @pl.when(pair + d < pairs)
        def _():
            for order in range(2):
                for copy in forward[order, d]:
                    copy.wait_send()

        @pl.when(pair >= d)
        def _():
            for copy in backward[d]:
                copy.wait_send()


def widen_kernel(lo, ig, fin_d, fin_u, fin_a, gains, lo_o, ig_o, q_o, k_o, v_o, o_o, u_o, d_o, g_o, f_o):
    step = pl.program_id(0)
    lo_o[...] = lo[...]
    ig_o[...] = ig[...].astype(F32)
    d_o[...] = fin_d[0].astype(F32)
    u_o[...] = fin_u[0].astype(F32)
    for i, out in enumerate((q_o, k_o, v_o)):

        @pl.when(step == i)
        def _():
            out[...] = fin_a[0].astype(F32).T

    @pl.when(step == 3)
    def _():
        o_o[...] = fin_a[0].astype(F32)

    g_o[...] = gains[0]
    f_o[...] = gains[1]


def body(
    tokens,
    norm_gain,
    query_weight,
    key_weight,
    value_weight,
    attention_output_weight,
    feedforward_norm_gain,
    up_weight,
    down_weight,
    segment_ids,
    out_grad,
):
    batch, length, share = tokens.shape
    width, head_cols = query_weight.shape
    units = up_weight.shape[1]
    pairs = lax.axis_size("seq") // 2
    assert lax.axis_size("head") == 4 and batch == 8 and length == BLOCK
    assert (width, share, head_cols, units) == (512, 128, 128, 512)
    assert pairs >= OWNERS and pairs % 2 == 0
    others = pairs - 1
    anywhere = pl.BlockSpec(memory_space=pl.ANY)
    vmem = pl.BlockSpec(memory_space=pltpu.VMEM)
    copies = 7 * 4 + 1 + 10 * KINDS + 8 + 4 + 5 + len(CHUNKS) * (4 + 2 * others) + 3 + others
    square = (512, 512)
    buffers = dict(
        xin=(square, BF16),
        ogs=(square, BF16),
        w_qkv=((3, 512, 512), BF16),
        w_o=(square, BF16),
        w_u=((4, 512, 512), BF16),
        w_d=((4, 512, 512), BF16),
        seg_other=((8, 256), jnp.int32),
        unit_one=(square, F32),
        unit_two=(square, F32),
        rstd_one=((512, 128), F32),
        rstd_two=((512, 128), F32),
        normed=(square, BF16),
        normed_two=(square, BF16),
        feat=((2, 512, 512), BF16),
        val=(square, BF16),
        mask=((2, 256, 256), F32),
        seg_col=((2, 256, 128), F32),
        carry_on=((2, 256, 128), F32),
        own_s=((2, 256, 128), F32),
        own_z=((2, 8, 128), F32),
        msg_s=((256, 128), BF16),
        msg_z=((2, 8, 128), F32),
        buf_s=((2, 256, 128), BF16),
        buf_z=((2, 2, 8, 128), F32),
        state=((8, 128, 256), BF16),
        scores_low=((8, 512, 256), BF16),
        attn=(square, BF16),
        attn_wide=(square, F32),
        den_inv=(square, F32),
        middle=(square, F32),
        work=(square, F32),
        work_two=(square, F32),
        hid=(square, BF16),
        hid_grad=(square, BF16),
        ffn=(square, F32),
        norm_grad=(square, F32),
        middle_grad=(square, F32),
        middle_low=(square, BF16),
        num_grad=(square, BF16),
        den_grad=(square, BF16),
        grad_s=((2, 256, 128), F32),
        grad_z=((2, 8, 128), F32),
        msg_gs=((256, 128), BF16),
        msg_gz=((8, 128), F32),
        buf_gs=((2, 256, 128), BF16),
        buf_gz=((2, 8, 128), F32),
        key_acc=(square, F32),
        val_acc=(square, F32),
        low_grads=((3, 512, 512), BF16),
        lo_s=(square, BF16),
        ig_s=(square, BF16),
        part=((3, 2, 2, 512, 512), BF16),
        buf_core=((3, 2, 512, 512), BF16),
        gain_part=((5, 8, 512), F32),
        gain_buf=((3 + others, 8, 512), F32),
    )
    shapes = list(buffers.values())
    for _, _, rows, _, lanes, _ in CHUNKS:
        piece = rows // 2 // OWNERS
        shapes.append(((3, rows // 2, lanes), BF16))
        shapes.append(((others, piece, lanes), BF16))
        shapes.append(((piece, lanes), BF16))
    scratch = [pltpu.VMEM(*spec) for spec in shapes]
    scratch += [
        pltpu.SemaphoreType.DMA((8 + 2 + len(CHUNKS),)),
        pltpu.SemaphoreType.DMA((copies,)),
        pltpu.SemaphoreType.DMA((copies,)),
    ]
    lo, ig, fin, gains = pl.pallas_call(
        functools.partial(layer_kernel, pairs, list(buffers)),
        out_shape=(
            jax.ShapeDtypeStruct((batch, length, share), BF16),
            jax.ShapeDtypeStruct((batch, length, share), BF16),
            jax.ShapeDtypeStruct((3, 512, 512), BF16),
            jax.ShapeDtypeStruct((8, 128), F32),
        ),
        in_specs=[anywhere] * 8 + [vmem] * 3,
        out_specs=(anywhere, anywhere, anywhere, vmem),
        scratch_shapes=scratch,
        compiler_params=pltpu.CompilerParams(
            collective_id=0, has_side_effects=True, vmem_limit_bytes=58 * MIB
        ),
        cost_estimate=pl.CostEstimate(
            flops=11 * 10**9, bytes_accessed=8 * MIB, transcendentals=4 * 10**6
        ),
        name="layer",
    )(
        tokens,
        out_grad,
        query_weight,
        key_weight,
        value_weight,
        attention_output_weight,
        up_weight,
        down_weight,
        segment_ids,
        norm_gain[None],
        feedforward_norm_gain[None],
    )

    def whole(shape):
        return pl.BlockSpec(shape, lambda g: (0,) * len(shape))

    def rows_block(u):
        return pl.BlockSpec((1, 128, 512), lambda g: (u, g, 0))

    tok_block = pl.BlockSpec((batch // 4, length, share), lambda g: (g, 0, 0))
    wide_block = pl.BlockSpec((128, 512), lambda g: (g, 0))
    lo, ig, q_w, k_w, v_w, o_w, u_w, d_w, g_one, g_two = pl.pallas_call(
        widen_kernel,
        grid=(4,),
        out_shape=(
            jax.ShapeDtypeStruct((batch, length, share), BF16),
            jax.ShapeDtypeStruct((batch, length, share), F32),
            jax.ShapeDtypeStruct((512, 128), F32),
            jax.ShapeDtypeStruct((512, 128), F32),
            jax.ShapeDtypeStruct((512, 128), F32),
            jax.ShapeDtypeStruct((128, 512), F32),
            jax.ShapeDtypeStruct((512, 512), F32),
            jax.ShapeDtypeStruct((512, 512), F32),
            jax.ShapeDtypeStruct((128,), F32),
            jax.ShapeDtypeStruct((128,), F32),
        ),
        in_specs=[
            tok_block,
            tok_block,
            rows_block(0),
            rows_block(1),
            rows_block(2),
            whole((8, 128)),
        ],
        out_specs=(
            tok_block,
            tok_block,
            whole((512, 128)),
            whole((512, 128)),
            whole((512, 128)),
            whole((128, 512)),
            wide_block,
            wide_block,
            whole((128,)),
            whole((128,)),
        ),
        compiler_params=pltpu.CompilerParams(vmem_limit_bytes=58 * MIB),
        name="widen",
    )(lo, ig, fin, fin, fin, gains)
    return (lo, ig, g_one, q_w, k_w, v_w, o_w, g_two, u_w, d_w)


def solution(mesh):
    in_specs = (
        P(None, "seq", "head"),
        P(),
        P(None, "head"),
        P(None, "head"),
        P(None, "head"),
        P("head", None),
        P(),
        P(None, "head"),
        P("head", None),
        P(None, "seq"),
        P(None, "seq", "head"),
    )
    out_specs = (
        P(None, "seq", "head"),
        P(None, "seq", "head"),
        P("head"),
        P(None, "head"),
        P(None, "head"),
        P(None, "head"),
        P("head", None),
        P("head"),
        P(None, "head"),
        P("head", None),
    )
    return jax.shard_map(body, mesh=mesh, in_specs=in_specs, out_specs=out_specs, check_vma=False)
```

```python
import functools
from types import SimpleNamespace

import jax
import jax.numpy as jnp
from jax import lax
from jax.experimental import pallas as pl
from jax.experimental.pallas import tpu as pltpu
from jax.sharding import PartitionSpec as P

DH = 64
BLOCK = 256
EPSILON = 1e-05
MESH = pl.DeviceIdType.MESH
F32 = jnp.float32
BF16 = jnp.bfloat16
MIB = 1 << 20
KINDS = 4
OWNERS = 4
CHUNKS = (
    (0, 0, 512, 0, 256, True),
    (0, 0, 512, 256, 256, True),
    (1, 0, 512, 0, 256, False),
    (1, 0, 512, 256, 256, True),
    (2, 384, 128, 0, 512, True),
    (2, 0, 384, 0, 256, True),
    (2, 0, 384, 256, 256, False),
)
COMBOS = ((0, 1, 0), (0, 1, 1), (1, 1, 0), (1, 1, 1), (1, 0, 0), (1, 0, 1), (0, 0, 1))


def mm(left, right, form="NN"):
    dims = {"NN": ((1,), (0,)), "NT": ((1,), (1,)), "TN": ((0,), (0,))}[form]
    return lax.dot_general(left, right, (dims, ((), ())), preferred_element_type=F32)


def loop(count, step):
    def run(i, carry):
        step(i)
        return carry

    lax.fori_loop(0, count, run, 0)


def span(start, size, multiple=None):
    return pl.ds(pl.multiple_of(start, multiple or size), size)


def rows_loop(total, chunk, step):
    loop(total // chunk, lambda i: step(span(i * chunk, chunk)))


def at128(i):
    return span(i * 128, 128)


def layer_kernel(pairs, names, *refs):
    (tok, og_in, wq, wk, wv, wo, wu, wd, seg, gain_one, gain_two) = refs[:11]
    (lo_out, ig_out, fin, gains) = refs[11:15]
    r_ = SimpleNamespace(**dict(zip(names, refs[15:])))
    chunk_refs = refs[15 + len(names) : -3]
    local_sem, send_sem, recv_sem = refs[-3:]
    xin, ogs, w_qkv, w_o, w_u = (
        r_.xin, r_.ogs, r_.w_qkv, r_.w_o, r_.w_u,
    )
    w_d, unit_one, unit_two, rstd_one, rstd_two = (
        r_.w_d, r_.unit_one, r_.unit_two, r_.rstd_one, r_.rstd_two,
    )
    normed, normed_two, feat, val, mask = (
        r_.normed, r_.normed_two, r_.feat, r_.val, r_.mask,
    )
    seg_col, carry_on, state, scores_low, own_s = (
        r_.seg_col, r_.carry_on, r_.state, r_.scores_low, r_.own_s,
    )
    own_z, msg_s, msg_z, buf_s, buf_z = (
        r_.own_z, r_.msg_s, r_.msg_z, r_.buf_s, r_.buf_z,
    )
    grad_s, grad_z, msg_gs, msg_gz, buf_gs = (
        r_.grad_s, r_.grad_z, r_.msg_gs, r_.msg_gz, r_.buf_gs,
    )
    buf_gz, attn, attn_wide, den_inv, middle = (
        r_.buf_gz, r_.attn, r_.attn_wide, r_.den_inv, r_.middle,
    )
    work, work_two, hid, hid_grad, ffn = (
        r_.work, r_.work_two, r_.hid, r_.hid_grad, r_.ffn,
    )
    norm_grad, middle_grad, middle_low, num_grad, den_grad = (
        r_.norm_grad, r_.middle_grad, r_.middle_low, r_.num_grad, r_.den_grad,
    )
    key_acc, val_acc, low_grads, lo_s, ig_s = (
        r_.key_acc, r_.val_acc, r_.low_grads, r_.lo_s, r_.ig_s,
    )
    gain_sum = r_.gain_sum
    part, buf_core, gain_part, gain_buf, seg_other = (
        r_.part, r_.buf_core, r_.gain_part, r_.gain_buf, r_.seg_other,
    )

    s = lax.axis_index("seq")
    h = lax.axis_index("head")
    pair, par = lax.div(s, 2), lax.rem(s, 2)
    hy, hc = lax.div(h, 2), lax.rem(h, 2)
    member = par * 4 + h
    zb = lax.rem(pair, 2)

    counter = [0]
    sends = []
    local_ids = iter(range(1000))

    def take(n=1):
        counter[0] += n
        return counter[0] - n

    def guarded(cond, act):
        if cond is None:
            act()
        else:
            pl.when(cond)(act)

    def peer(dp, dy, dc):
        return (1 - par if dp else par, 1 - hy if dy else hy, 1 - hc if dc else hc)

    def address(par_to, y_to, c_to):
        return (2 * pair + par_to, 2 * y_to + c_to)

    core, ypeer, xpeer = (address(*peer(*d)) for d in ((0, 0, 1), (0, 1, 0), (1, 0, 0)))
    zpeer = (2 * (pair + 1 - 2 * zb) + par, h)

    def ring(d):
        to = lax.rem(pair + d, pairs)
        return to, (2 * to + par, h)

    def remote(src, dst, device, i=None):
        i = take() if i is None else i
        return pltpu.make_async_remote_copy(
            src_ref=src,
            dst_ref=dst,
            send_sem=send_sem.at[i],
            recv_sem=recv_sem.at[i],
            device_id=device,
            device_id_type=MESH,
        )

    def start(copy):
        copy.start()
        sends.append(copy)
        return copy

    def send(src, dst, device):
        return start(remote(src, dst, device))

    def local(src, dst):
        copy = pltpu.make_async_copy(src, dst, local_sem.at[next(local_ids)])
        copy.start()
        return copy

    def each_ring(act):
        if pairs <= 4:
            for d in range(1, pairs):
                act(d)
        else:
            loop(pairs - 1, lambda i: act(i + 1))

    hcol = at128(h)
    half256 = span(par * 256, 256)
    own_w = [
        [local(w, w_qkv.at[i, :, hcol]) for i, w in enumerate((wq, wk, wv))],
        [local(wo, w_o.at[hcol])],
        [local(wu, w_u.at[h])],
        [local(wd, w_d.at[h])],
    ]
    own_tok = local(tok.at[member], xin.at[half256, hcol])
    own_og = local(og_in.at[member], ogs.at[half256, hcol])
    row8 = lax.broadcasted_iota(jnp.int32, (8, 128), 0)
    neutral = jnp.where(row8 == 4, -1.0, 0.0).astype(F32)
    for slot in range(2):
        buf_s[slot] = jnp.zeros((256, 128), BF16)
        buf_gs[slot] = jnp.zeros((256, 128), BF16)
        buf_gz[slot] = jnp.zeros((8, 128), F32)
        for order in range(2):
            buf_z[slot, order] = neutral

    barrier = pltpu.get_barrier_semaphore()
    for d in COMBOS:
        pl.semaphore_signal(barrier, inc=1, device_id=address(*peer(*d)), device_id_type=MESH)
    each_ring(
        lambda d: pl.semaphore_signal(
            barrier, inc=1, device_id=ring(d)[1], device_id_type=MESH
        )
    )
    pl.semaphore_wait(barrier, len(COMBOS) + pairs - 1)

    def scatter_in(src, dst, combos=COMBOS):
        copies = []
        for d in combos:
            par_to, y_to, c_to = peer(*d)
            copies.append(
                send(
                    src.at[par_to * 4 + 2 * y_to + c_to],
                    dst.at[half256, hcol],
                    address(par_to, y_to, c_to),
                )
            )
        return copies

    def scatter_out(src, dst, combos):
        copies = []
        for d in combos:
            par_to, y_to, c_to = peer(*d)
            copies.append(
                send(
                    src.at[span(par_to * 256, 256), at128(2 * y_to + c_to)],
                    dst.at[member],
                    address(par_to, y_to, c_to),
                )
            )
        return copies

    across = 2 * (1 - hy) + hc
    quarter = par + 2 * zb
    quarter_x = 1 - par + 2 * zb

    def view(kind, shard, eighth=None, eighths=2):
        rows = 32 if kind == 1 else 128
        unit = rows // 2
        if kind == 0:
            where = slice(None) if eighth is None else span(eighth * unit, unit * eighths, unit)
            return w_qkv.at[:, where, at128(shard)]
        if kind == 1:
            if eighth is None:
                return w_o.at[at128(shard)]
            return w_o.at[span(shard * 128 + eighth * unit, unit * eighths, unit)]
        ref = w_u if kind == 2 else w_d
        if eighth is None:
            return ref.at[shard]
        return ref.at[shard, span(eighth * unit, unit * eighths, unit)]

    wt = {}

    def pass_on_weight(kind, eighth, eighths, device, shard=None):
        ref = view(kind, across if shard is None else shard, eighth, eighths)
        return send(ref, ref, device)

    def weight_y(kind):
        wt[kind, "y"] = pass_on_weight(kind, 2 * quarter, 2, ypeer, h)

    def weight_core(kind):
        own = view(kind, h)
        wt[kind, "c"] = [send(own, own, core)]

    def weight_near(kind):
        wt[kind, "y"].wait_recv()
        wt[kind, "x"] = pass_on_weight(kind, 2 * quarter, 2, xpeer)
        wt[kind, "z"] = pass_on_weight(kind, 2 * quarter, 2, zpeer)

    def weight_far(kind):
        wt[kind, "x"].wait_recv()
        wt[kind, "far"] = pass_on_weight(kind, 2 * quarter_x, 2, zpeer)
        wt[kind, "c"].append(pass_on_weight(kind, 4 * zb, 4, core))

    def weight_last(kind):
        wt[kind, "z"].wait_recv()
        wt[kind, "far"].wait_recv()
        wt[kind, "c"].append(pass_on_weight(kind, 4 * (1 - zb), 4, core))

    def weight_own(kind):
        wt[kind, "c"][0].wait_recv()

    def weight_ready(kind):
        for copy in wt[kind, "c"][1:]:
            copy.wait_recv()

    for copy in own_w[0]:
        copy.wait()
    weight_y(0)
    tokens_in = scatter_in(tok, xin)
    seg_copy = send(seg, seg_other, xpeer)
    weight_core(0)
    for kind in (1, 2, 3):
        for copy in own_w[kind]:
            copy.wait()
        weight_y(kind)
    for kind in (1, 2, 3):
        weight_core(kind)
    weight_near(0)
    og_copies = scatter_in(og_in, ogs)
    for copy in tokens_in:
        copy.wait_recv()
    own_tok.wait()
    weight_far(0)

    def norm_rows(source, gain, unit_ref, rstd_ref, out_ref):
        def step(r):
            x = source(r)
            center = x - jnp.mean(x, axis=-1, keepdims=True)
            scale = lax.rsqrt(jnp.mean(center * center, axis=-1, keepdims=True) + EPSILON)
            unit = center * scale
            unit_ref[r, :] = unit
            rstd_ref[r, :] = jnp.broadcast_to(scale, (unit.shape[0], 128))
            out_ref[r, :] = (unit * gain[...]).astype(BF16)

        rows_loop(512, 64, step)

    norm_rows(lambda r: xin[r, :].astype(F32), gain_one, unit_one, rstd_one, normed)

    seg_copy.wait_recv()
    own_row = seg[pl.ds(member, 1), :]
    other_row = seg_other[pl.ds(member, 1), :]
    seg_rows = (
        (own_row * (1 - par) + other_row * par).astype(F32),
        (own_row * par + other_row * (1 - par)).astype(F32),
    )
    first = lax.broadcasted_iota(jnp.int32, (256, 256), 0)
    second = lax.broadcasted_iota(jnp.int32, (256, 256), 1)
    for b in range(2):
        along = jnp.broadcast_to(seg_rows[b], (256, 256))
        down = along.T
        mask[b] = jnp.where((along == down) & (second <= first), 1.0, 0.0)
        seg_col[b] = down[:, :128]
    weight_own(0)

    lane = lax.broadcasted_iota(jnp.int32, (1, 128), 1)
    low_lanes = lane < 64
    spread = (
        lax.broadcasted_iota(jnp.int32, (128, 128), 0) // 64
        == lax.broadcasted_iota(jnp.int32, (128, 128), 1) // 64
    )

    def place(i):
        b, pr = lax.div(i, 4), lax.rem(i, 4)
        return b, pr, span(b * 256, 256), at128(pr)

    def side_place(i, side):
        return place(lax.div(i, 2) * 4 + 2 * side + lax.rem(i, 2))

    def pack(square):
        return jnp.where(low_lanes, square[:64], square[64:])

    def two(rows):
        zero = jnp.zeros_like(rows)
        return jnp.concatenate(
            [jnp.where(low_lanes, rows, zero), jnp.where(low_lanes, zero, rows)], axis=0
        )

    def pick(stacked):
        return jnp.where(low_lanes, stacked[:256], stacked[256:])

    def packed_rows(pr):
        return span(pr * 64, 64)

    last_rows = [seg_col[b, pl.ds(255, 1), :] for b in range(2)]
    keep_mid = jnp.where(last_rows[0] >= last_rows[1], 1.0, 0.0)

    def project(side):
        cols = span(side * 256, 256)

        def step_kind(i):
            work[:, :256] = mm(normed[...], w_qkv[i, :, cols])

            def step(r):
                v = work[r, :256]
                feat[i, r, cols] = jnp.where(
                    v > 0, v + 1.0, jnp.exp(jnp.minimum(v, 0.0))
                ).astype(BF16)

            rows_loop(512, 64, step)

        loop(2, step_kind)
        val[:, cols] = mm(normed[...], w_qkv[2, :, cols]).astype(BF16)

    def own_state(i, side):
        b, pr, rows, cols = side_place(i, side)
        tail = seg_col[b] == seg_col[b, pl.ds(255, 1), :]
        keys = feat[1, rows, cols].astype(F32)
        keys = jnp.where(tail, keys, 0.0)
        own_s[b, packed_rows(pr), :] = pack(mm(keys.astype(BF16), val[rows, cols], "TN"))
        own_z[b, pl.ds(pr, 1), :] = jnp.sum(keys, axis=0, keepdims=True)

    def shift(d, pieces, base):
        to = lax.rem(pair + d + pairs, pairs)
        device = (2 * to + par, h)
        return [remote(src, dst, device, base + i) for i, (src, dst) in enumerate(pieces)]

    forward = {}

    def send_state(order, side):
        loop(4, lambda i: own_state(i, side))
        rows = span(side * 128, 128)
        msg_s[rows, :] = (own_s[1, rows, :] + keep_mid * own_s[0, rows, :]).astype(BF16)
        msg_z[order] = jnp.where(row8 == 4, last_rows[1], own_z[1] + keep_mid * own_z[0])
        for d in (1, 2):
            copies = shift(
                d,
                [
                    (msg_s.at[rows], buf_s.at[d - 1, rows]),
                    (msg_z.at[order], buf_z.at[d - 1, order]),
                ],
                take(2),
            )
            forward[order, d] = copies

            @pl.when(pair + d < pairs)
            def _():
                for copy in copies:
                    copy.start()

    own_z[...] = jnp.zeros_like(own_z)
    project(hy)
    send_state(0, hy)
    weight_near(1)
    weight_last(0)
    weight_near(2)
    weight_ready(0)
    project(1 - hy)
    send_state(1, 1 - hy)
    weight_far(1)
    weight_near(3)

    ones = jnp.ones((256, 128), BF16)
    ready = {}

    def receive_state(order):
        for d in (1, 2):

            @pl.when(pair >= d)
            def _():
                for copy in forward[order, d]:
                    copy.wait_recv()

        if order == 0:
            last_in = buf_z[0, 0, pl.ds(4, 1), :]
            ready["keep_in"] = jnp.where(buf_z[1, 0, pl.ds(4, 1), :] >= last_in, 1.0, 0.0)
            ready["keep_first"] = jnp.where(last_in >= last_rows[0], 1.0, 0.0)
            carry_on[0] = jnp.where(seg_col[0] == last_in, 1.0, 0.0)
            carry_on[1] = jnp.where(seg_col[1] == last_rows[0], 1.0, 0.0)
        buf_z[0, order] = buf_z[0, order] + ready["keep_in"] * buf_z[1, order]

    def enter(order, side):
        def step(i):
            pr = 2 * side + i
            entering = buf_s[0, packed_rows(pr), :].astype(F32) + ready["keep_in"] * buf_s[
                1, packed_rows(pr), :
            ].astype(F32)
            z_in = buf_z[0, order, pl.ds(pr, 1), :]
            middle_s = own_s[0, packed_rows(pr), :] + ready["keep_first"] * entering
            middle_z = own_z[0, pl.ds(pr, 1), :] + ready["keep_first"] * z_in
            for b, (packed, z_row) in enumerate(((entering, z_in), (middle_s, middle_z))):
                wide = jnp.where(spread, jnp.broadcast_to(z_row, (128, 128)).T, 0.0)
                state[b * 4 + pr, :, :128] = two(packed).astype(BF16)
                state[b * 4 + pr, :, 128:] = wide.astype(BF16)

        loop(2, step)

    def attend(i, side):
        b, pr, rows, cols = side_place(i, side)
        q, k, v = feat[0, rows, cols], feat[1, rows, cols], val[rows, cols]
        scores = mm(two(q), k, "NT")
        m = mask[b]
        low = jnp.concatenate([scores[:256] * m, scores[256:] * m], axis=0).astype(BF16)
        scores_low[b * 4 + pr] = low
        both = mm(low, jnp.concatenate([v, ones], axis=1))
        carried = mm(q, state[b * 4 + pr])
        c = carry_on[b]
        numer = pick(both[:, :128]) + c * carried[:, :128]
        denom = pick(both[:, 128:]) + c * carried[:, 128:]
        inverse = 1.0 / denom
        result = numer * inverse
        den_inv[rows, cols] = inverse
        attn_wide[rows, cols] = result
        attn[rows, cols] = result.astype(BF16)

    receive_state(0)
    enter(0, hy)
    loop(4, lambda i: attend(i, hy))
    weight_far(2)
    receive_state(1)
    enter(1, 1 - hy)
    weight_last(1)
    loop(4, lambda i: attend(i, 1 - hy))
    keep_first = ready["keep_first"]
    weight_own(1)
    weight_ready(1)

    weight_far(3)
    work[...] = mm(attn[...], w_o[...])

    def mid_step(r):
        middle[r, :] = xin[r, :].astype(F32) + work[r, :]

    rows_loop(512, 64, mid_step)
    norm_rows(
        lambda r: middle[r, :].astype(BF16).astype(F32), gain_two, unit_two, rstd_two, normed_two
    )
    for copy in og_copies:
        copy.wait_recv()
    own_og.wait()
    weight_own(2)
    weight_own(3)

    def core_send(view_src, view_dst):
        return send(view_src, view_dst, core)

    def add_core(u, jy, row, rows):
        def step(i):
            r = span(row + i * 64, 64)
            part[u, jy, hc, r, :] = (
                part[u, jy, hc, r, :].astype(F32) + buf_core[u, jy, r, :].astype(F32)
            ).astype(BF16)

        loop(rows // 64, step)

    owner = None if pairs == OWNERS else pair < OWNERS

    class Chunk:
        def __init__(self, n):
            self.u, self.row, self.rows, self.lane, self.lanes, self.y_first = CHUNKS[n]
            self.half = self.rows // 2
            self.piece = self.half // OWNERS
            self.buf, self.ring_buf, self.own = chunk_refs[3 * n : 3 * n + 3]
            self.cols = pl.ds(self.lane, self.lanes)
            self.devices = (ypeer, xpeer) if self.y_first else (xpeer, ypeer)
            self.ring_base = self.spread_base = None

        def rows_of(self, half, at=0, size=None):
            return span(self.row + half * self.half + at, size or self.half, 16)

        def at(self, jy, half):
            return part.at[self.u, jy, hc, self.rows_of(half), self.cols]

        def a(self):
            self.first = send(self.at(1 - hy, 1 - par), self.buf.at[0], self.devices[0])

        def b(self):
            source = (1 - hy, par) if self.y_first else (hy, 1 - par)
            self.other = send(self.at(*source), self.buf.at[1], self.devices[0])

        def mid(self):
            self.first.wait_recv()
            jy, half = (hy, 1 - par) if self.y_first else (1 - hy, par)

            def step(i):
                r = self.rows_of(half, i * self.piece, self.piece)
                got = self.buf[0, span(i * self.piece, self.piece), :].astype(F32)
                part[self.u, jy, hc, r, self.cols] = (
                    part[self.u, jy, hc, r, self.cols].astype(F32) + got
                ).astype(BF16)

            loop(OWNERS, step)
            self.second = send(self.at(jy, half), self.buf.at[2], self.devices[1])

        def ring_copy(self, d):
            to, device = ring(d)
            rows = self.rows_of(par, lax.rem(to, OWNERS) * self.piece, self.piece)
            copy = remote(
                part.at[self.u, hy, hc, rows, self.cols],
                self.ring_buf.at[d - 1],
                device,
                self.ring_base + d - 1,
            )
            return copy, None if pairs == OWNERS else to < OWNERS

        def ring(self):
            self.other.wait_recv()
            self.second.wait_recv()

            def step(i):
                r = self.rows_of(par, i * self.piece, self.piece)
                b = span(i * self.piece, self.piece)
                got = self.buf[1, b, :].astype(F32) + self.buf[2, b, :].astype(F32)
                part[self.u, hy, hc, r, self.cols] = (
                    part[self.u, hy, hc, r, self.cols].astype(F32) + got
                ).astype(BF16)

            loop(OWNERS, step)
            self.ring_base = take(pairs - 1)

            def go(d):
                copy, cond = self.ring_copy(d)
                guarded(cond, copy.start)

            each_ring(go)

        def final(self, index):
            rows = self.rows_of(par, lax.rem(index, OWNERS) * self.piece, self.piece)
            return fin.at[self.u, rows, self.cols]

        def spread_copy(self, d):
            return remote(
                self.own, self.final(pair), ring(d)[1], self.spread_base + d - 1
            )

        def spread(self):
            self.spread_base = take(pairs - 1)
            sem = local_sem.at[next(local_ids)]
            self.kept = pltpu.make_async_copy(self.own, self.final(pair), sem)

            def total():
                each_ring(lambda d: self.ring_copy(d)[0].wait_recv())
                rows = self.rows_of(par, lax.rem(pair, OWNERS) * self.piece, self.piece)
                self.own[...] = part[self.u, hy, hc, rows, self.cols]

                def more(d):
                    self.own[...] = (
                        self.own[...].astype(F32) + self.ring_buf[d - 1].astype(F32)
                    ).astype(BF16)

                if pairs == OWNERS:
                    value = part[self.u, hy, hc, rows, self.cols].astype(F32)
                    for d in range(1, pairs):
                        value = value + self.ring_buf[d - 1].astype(F32)
                    self.own[...] = value.astype(BF16)
                else:
                    each_ring(more)
                each_ring(lambda d: self.spread_copy(d).start())
                self.kept.start()

            guarded(owner, total)

        def back(self):
            def arrived(d):
                giver = lax.rem(pair - d + pairs, pairs)
                cond = None if pairs == OWNERS else giver < OWNERS
                guarded(cond, self.spread_copy(d).wait_recv)

            each_ring(arrived)
            guarded(owner, self.kept.wait)
            rows = fin.at[self.u, self.rows_of(par), self.cols]
            self.last = send(rows, rows, xpeer)

        def end(self):
            self.last.wait_recv()

        def sent(self):
            def one(d):
                copy, cond = self.ring_copy(d)
                guarded(cond, copy.wait_send)

            each_ring(one)
            guarded(owner, lambda: each_ring(lambda d: self.spread_copy(d).wait_send()))

    d0, d1, u0, u1, o0, a0, a1 = chunks = [Chunk(n) for n in range(len(CHUNKS))]

    def zero_rows(r):
        ffn[r, :] = jnp.zeros((64, 512), F32)
        norm_grad[r, :] = jnp.zeros((64, 512), F32)

    rows_loop(512, 64, zero_rows)

    def feed(jc, jy):
        j = 2 * jy + jc
        work[...] = mm(normed_two[...], w_u[j])
        work_two[...] = mm(ogs[...], w_d[j], "NT")

        def step(r):
            v = work[r, :]
            sigma = 1.0 / (1.0 + jnp.exp(-v))
            hid[r, :] = (v * sigma).astype(BF16)
            hid_grad[r, :] = (work_two[r, :] * (sigma * (1.0 + v * (1.0 - sigma)))).astype(BF16)

        rows_loop(512, 64, step)
        part[0, jy, jc] = mm(hid[...], ogs[...], "TN").astype(BF16)
        part[1, jy, jc] = mm(normed_two[...], hid_grad[...], "TN").astype(BF16)

    def feed_on(jc, jy):
        j = 2 * jy + jc
        ffn[...] += mm(hid[...], w_d[j])
        norm_grad[...] += mm(hid_grad[...], w_u[j], "NT")

    def core_feed(jy):
        return core_send(part.at[0:2, jy, 1 - hc], buf_core.at[0:2, jy])

    def core_fed(copy, jy):
        copy.wait_recv()
        add_core(0, jy, 0, 512)
        add_core(1, jy, 0, 512)

    feed(1 - hc, hy)
    core_f = core_feed(hy)
    feed_on(1 - hc, hy)
    weight_last(2)
    feed(hc, hy)
    core_fed(core_f, hy)
    u0.b()
    weight_last(3)
    feed_on(hc, hy)
    weight_ready(2)
    weight_ready(3)
    feed(1 - hc, 1 - hy)
    core_f = core_feed(1 - hy)
    feed_on(1 - hc, 1 - hy)
    feed(hc, 1 - hy)
    core_fed(core_f, 1 - hy)
    for chunk in (d0, d1):
        chunk.a()
        chunk.b()
    u0.a()
    u1.a()
    u1.b()
    feed_on(hc, 1 - hy)

    gain_part[0] = jnp.zeros((8, 512), F32)
    row_512 = lax.broadcasted_iota(jnp.int32, (8, 512), 0)

    def norm_back(grad_ref, gain, unit_ref, rstd_ref, base, sink, row):
        def step(r):
            grad = grad_ref[r, :]
            unit = unit_ref[r, :]
            scaled = grad * gain[...]
            mean_one = jnp.mean(scaled, axis=-1, keepdims=True)
            mean_two = jnp.mean(scaled * unit, axis=-1, keepdims=True)
            rstd = rstd_ref[r, :]
            rstd = jnp.concatenate([rstd] * 4, axis=1)
            sink(r, base(r) + rstd * (scaled - mean_one - unit * mean_two))
            total = jnp.sum(grad * unit, axis=0, keepdims=True)
            gain_part[0] = gain_part[0] + jnp.where(row_512 == row, total, 0.0)

        rows_loop(512, 64, step)

    def sink_middle(r, grad):
        middle_grad[r, :] = grad
        middle_low[r, :] = grad.astype(BF16)
        lo_s[r, :] = (middle[r, :] + ffn[r, :]).astype(BF16)

    norm_back(
        norm_grad, gain_two, unit_two, rstd_two, lambda r: ogs[r, :].astype(F32), sink_middle, 1
    )

    lo_copies = scatter_out(lo_s, lo_out, COMBOS[4:])
    lo_own = local(lo_s.at[half256, hcol], lo_out.at[member])
    out_rows = pl.ds(384, 128)
    work_two[...] = mm(attn[...], middle_low[...], "TN")
    for j in range(4):
        part[2, j // 2, j % 2, out_rows, :] = work_two[j * 128 : (j + 1) * 128, :].astype(BF16)
    core_o = core_send(part.at[2, :, 1 - hc, out_rows], buf_core.at[2, :, out_rows])
    work[...] = mm(middle_low[...], w_o[...], "NT")

    head_ones = jnp.where(spread, 1.0, 0.0).astype(BF16)
    head_ones = jnp.concatenate([head_ones, head_ones], axis=0)
    first_lane = lax.rem(lane, 64) == 0
    second_lane = lax.rem(lane, 64) == 1

    def split(wide):
        high = wide.astype(BF16)
        return high, (wide - high.astype(F32)).astype(BF16)

    grad_z[...] = jnp.zeros_like(grad_z)

    def outer(i):
        b, pr, rows, cols = place(i)
        grad, inverse = work[rows, cols], den_inv[rows, cols]
        gnum = (grad * inverse).astype(BF16)
        high, low = split(grad * attn_wide[rows, cols])
        gden = -mm(jnp.concatenate([high, low], axis=1), head_ones) * inverse
        dhigh = gden.astype(BF16).astype(F32)
        num_grad[rows, cols] = gnum
        den_grad[rows, cols] = jnp.where(
            first_lane, dhigh, jnp.where(second_lane, gden - dhigh, 0.0)
        ).astype(BF16)
        queries = feat[0, rows, cols].astype(F32) * carry_on[b]
        grad_s[b, packed_rows(pr), :] = pack(mm(queries.astype(BF16), gnum, "TN"))
        grad_z[b, pl.ds(pr, 1), :] = jnp.sum(queries * gden, axis=0, keepdims=True)

    loop(8, outer)
    msg_gs[...] = (grad_s[0] + keep_first * grad_s[1]).astype(BF16)
    msg_gz[...] = jnp.where(row8 == 4, keep_first * keep_mid, grad_z[0] + keep_first * grad_z[1])
    backward = {}
    for d in (1, 2):
        pieces = [(msg_gs, buf_gs.at[d - 1]), (msg_gz, buf_gz.at[d - 1])]
        backward[d] = shift(-d, pieces, take(2))

        @pl.when(pair >= d)
        def _():
            for copy in backward[d]:
                copy.start()

    marks = jnp.where(first_lane | second_lane, 1.0, 0.0).astype(BF16)
    marks = jnp.broadcast_to(marks, (256, 128))

    def inner(i):
        b, pr, rows, cols = place(i)
        q, k, v = feat[0, rows, cols], feat[1, rows, cols], val[rows, cols]
        gnum, gden = num_grad[rows, cols], den_grad[rows, cols]
        gnum_two = two(gnum)
        grads = jnp.concatenate([gnum_two, two(gden)], axis=1)
        values = jnp.concatenate([v, marks], axis=1)
        m = mask[b]
        gsc = mm(grads, values, "NT")
        gsc = jnp.concatenate([gsc[:256] * m, gsc[256:] * m], axis=0).astype(BF16)
        qgrad = pick(mm(gsc, k)) + carry_on[b] * mm(
            jnp.concatenate([gnum, gden], axis=1), state[i], "NT"
        )
        low_grads[0, rows, cols] = (qgrad * jnp.minimum(q.astype(F32), 1.0)).astype(BF16)
        key_acc[rows, cols] = mm(gsc, two(q), "TN")
        val_acc[rows, cols] = mm(scores_low[i], gnum_two, "TN")

    loop(4, inner)
    d0.mid()
    u0.mid()
    core_o.wait_recv()
    add_core(2, 0, 384, 128)
    add_core(2, 1, 384, 128)
    loop(4, lambda i: inner(4 + i))

    d1.mid()
    o0.a()
    o0.b()
    for d in (1, 2):

        @pl.when(pair + d < pairs)
        def _():
            for copy in backward[d]:
                copy.wait_recv()

    pass_on = buf_gz[0, pl.ds(4, 1), :]
    buf_gz[0] = buf_gz[0] + pass_on * buf_gz[1]

    def leave(i):
        b, pr, rows, cols = place(i)
        leaving = buf_gs[0, packed_rows(pr), :].astype(F32) + pass_on * buf_gs[
            1, packed_rows(pr), :
        ].astype(F32)
        z_leaving = buf_gz[0, pl.ds(pr, 1), :]
        first_block = (1 - b).astype(F32)
        scale = first_block * keep_mid + (1.0 - first_block)
        leaving = scale * leaving + first_block * grad_s[1, packed_rows(pr), :]
        z_leaving = scale * z_leaving + first_block * grad_z[1, pl.ds(pr, 1), :]
        square = two(leaving).astype(BF16)
        k, v = feat[1, rows, cols], val[rows, cols]
        tail = seg_col[b] == seg_col[b, pl.ds(255, 1), :]
        kgrad = key_acc[rows, cols] + jnp.where(tail, mm(v, square, "NT") + z_leaving, 0.0)
        low_grads[1, rows, cols] = (kgrad * jnp.minimum(k.astype(F32), 1.0)).astype(BF16)
        vgrad = val_acc[rows, cols] + jnp.where(tail, mm(k, square), 0.0)
        low_grads[2, rows, cols] = vgrad.astype(BF16)

    loop(8, leave)

    d0.ring()
    def qkv_weight(i):
        work[...] = mm(low_grads[i], normed[...], "TN")
        for j in range(4):
            part[2, j // 2, j % 2, at128(i), :] = work[j * 128 : (j + 1) * 128, :].astype(BF16)

    loop(3, qkv_weight)
    qkv_rows = pl.ds(0, 384)
    core_a = [
        core_send(part.at[2, jy, 1 - hc, qkv_rows], buf_core.at[2, jy, qkv_rows])
        for jy in (1 - hy, hy)
    ]
    norm_grad[...] = mm(low_grads[0], w_qkv[0], "NT")
    core_a[0].wait_recv()
    add_core(2, 1 - hy, 0, 384)
    a0.a()
    a1.a()
    core_a[1].wait_recv()
    add_core(2, hy, 0, 384)
    a0.b()
    a1.b()
    norm_grad[...] += mm(low_grads[1], w_qkv[1], "NT")
    norm_grad[...] += mm(low_grads[2], w_qkv[2], "NT")
    u1.mid()

    def sink_input(r, grad):
        ig_s[r, :] = grad.astype(BF16)

    norm_back(norm_grad, gain_one, unit_one, rstd_one, lambda r: middle_grad[r, :], sink_input, 0)

    def gain_start():
        copies = []
        for n, d in enumerate(COMBOS):
            par_to, y_to, c_to = peer(*d)
            copies.append(
                send(
                    gain_part.at[0, :, at128(2 * y_to + c_to)],
                    gain_buf.at[n],
                    address(par_to, y_to, c_to),
                )
            )
        return copies

    gain_base = take(pairs - 1)

    def gain_copy(d):
        return remote(gain_sum.at[0], gain_buf.at[6 + d], ring(d)[1], gain_base + d - 1)

    def gain_middle(copies):
        for copy in copies:
            copy.wait_recv()
        total = gain_part[0, :, hcol]
        for n in range(len(COMBOS)):
            total = total + gain_buf[n]
        gain_sum[0] = total
        each_ring(lambda d: gain_copy(d).start())

    def gain_end():
        each_ring(lambda d: gain_copy(d).wait_recv())
        gain_sum[1] = gain_sum[0]

        def add_gain(d):
            gain_sum[1] = gain_sum[1] + gain_buf[6 + d]

        each_ring(add_gain)
        gains[...] = gain_sum[1]

    gain_copies = gain_start()
    d1.ring()
    d0.spread()
    u0.ring()
    u1.ring()
    o0.mid()
    d1.spread()
    d0.back()
    a0.mid()
    a1.mid()
    o0.ring()
    u0.spread()
    a0.ring()
    a1.ring()
    lo_copies += scatter_out(lo_s, lo_out, COMBOS[:4])
    ig_copies = scatter_out(ig_s, ig_out, COMBOS)
    ig_own = local(ig_s.at[half256, hcol], ig_out.at[member])
    d1.back()
    u1.spread()
    gain_middle(gain_copies)
    o0.spread()
    u0.back()
    a0.spread()
    a1.spread()
    u1.back()
    o0.back()
    a0.back()
    a1.back()
    gain_end()

    for chunk in chunks:
        chunk.end()
    for copy in lo_copies + ig_copies:
        copy.wait_recv()
    lo_own.wait()
    ig_own.wait()
    for copy in sends:
        copy.wait_send()
    for chunk in chunks:
        chunk.sent()
    each_ring(lambda d: gain_copy(d).wait_send())
    for d in (1, 2):

        @pl.when(pair + d < pairs)
        def _():
            for order in range(2):
                for copy in forward[order, d]:
                    copy.wait_send()

        @pl.when(pair >= d)
        def _():
            for copy in backward[d]:
                copy.wait_send()


def widen_kernel(lo, ig, fin, gains, *refs):
    lo_o, ig_o, q_o, k_o, v_o, o_o, u_o, d_o, g_o, f_o = refs[:10]
    ig_b, fin_b, lo_b, ig_w, fin_w, qkv_w, sem_in, sem_out = refs[10:]
    parts = []
    for u in (0, 1, 2):
        for half in range(2):
            rows = pl.ds(half * 256, 256)
            parts.append((fin.at[u, rows], fin_b.at[u, rows], u, half))
    for quarter in range(4):
        rows = pl.ds(quarter * 2, 2)
        parts.append((ig.at[rows], ig_b.at[rows], 3, quarter))
    for half in range(2):
        rows = pl.ds(half * 4, 4)
        parts.append((lo.at[rows], lo_b.at[rows], 4, half))
    arriving = [
        pltpu.make_async_copy(source, into, sem_in.at[n])
        for n, (source, into, _, _) in enumerate(parts)
    ]
    for copy in arriving:
        copy.start()
    g_o[...] = gains[0]
    f_o[...] = gains[1]
    leaving = []

    def leave(source, out):
        copy = pltpu.make_async_copy(source, out, sem_out.at[len(leaving)])
        copy.start()
        leaving.append(copy)

    for copy, (_, _, u, n) in zip(arriving, parts, strict=True):
        copy.wait()
        if u == 4:
            rows = pl.ds(n * 4, 4)
            leave(lo_b.at[rows], lo_o.at[rows])
        elif u == 3:
            rows = pl.ds(n * 2, 2)
            ig_w[rows] = ig_b[rows].astype(F32)
            leave(ig_w.at[rows], ig_o.at[rows])
        elif u < 2:
            rows = pl.ds(n * 256, 256)
            fin_w[u, rows] = fin_b[u, rows].astype(F32)
            leave(fin_w.at[u, rows], (d_o, u_o)[u].at[rows])
        else:
            for i in (2 * n, 2 * n + 1):
                rows = pl.ds(i * 128, 128)
                if i < 3:
                    qkv_w[i] = fin_b[2, rows].astype(F32).T
                    leave(qkv_w.at[i], (q_o, k_o, v_o)[i])
                else:
                    fin_w[2, pl.ds(0, 128)] = fin_b[2, rows].astype(F32)
                    leave(fin_w.at[2, pl.ds(0, 128)], o_o)
    for copy in leaving:
        copy.wait()


def body(
    tokens,
    norm_gain,
    query_weight,
    key_weight,
    value_weight,
    attention_output_weight,
    feedforward_norm_gain,
    up_weight,
    down_weight,
    segment_ids,
    out_grad,
):
    batch, length, share = tokens.shape
    width, head_cols = query_weight.shape
    units = up_weight.shape[1]
    pairs = lax.axis_size("seq") // 2
    assert lax.axis_size("head") == 4 and batch == 8 and length == BLOCK
    assert (width, share, head_cols, units) == (512, 128, 128, 512)
    assert pairs >= OWNERS and pairs % 2 == 0
    others = pairs - 1
    anywhere = pl.BlockSpec(memory_space=pl.ANY)
    vmem = pl.BlockSpec(memory_space=pltpu.VMEM)
    copies = 7 * 4 + 1 + 7 * KINDS + 8 + 4 + 5 + len(CHUNKS) * (4 + 2 * others) + 7 + others
    square = (512, 512)
    buffers = dict(
        xin=(square, BF16),
        ogs=(square, BF16),
        w_qkv=((3, 512, 512), BF16),
        w_o=(square, BF16),
        w_u=((4, 512, 512), BF16),
        w_d=((4, 512, 512), BF16),
        seg_other=((8, 256), jnp.int32),
        unit_one=(square, F32),
        unit_two=(square, F32),
        rstd_one=((512, 128), F32),
        rstd_two=((512, 128), F32),
        normed=(square, BF16),
        normed_two=(square, BF16),
        feat=((2, 512, 512), BF16),
        val=(square, BF16),
        mask=((2, 256, 256), F32),
        seg_col=((2, 256, 128), F32),
        carry_on=((2, 256, 128), F32),
        own_s=((2, 256, 128), F32),
        own_z=((2, 8, 128), F32),
        msg_s=((256, 128), BF16),
        msg_z=((2, 8, 128), F32),
        buf_s=((2, 256, 128), BF16),
        buf_z=((2, 2, 8, 128), F32),
        state=((8, 128, 256), BF16),
        scores_low=((8, 512, 256), BF16),
        attn=(square, BF16),
        attn_wide=(square, F32),
        den_inv=(square, F32),
        middle=(square, F32),
        work=(square, F32),
        work_two=(square, F32),
        hid=(square, BF16),
        hid_grad=(square, BF16),
        ffn=(square, F32),
        norm_grad=(square, F32),
        middle_grad=(square, F32),
        middle_low=(square, BF16),
        num_grad=(square, BF16),
        den_grad=(square, BF16),
        grad_s=((2, 256, 128), F32),
        grad_z=((2, 8, 128), F32),
        msg_gs=((256, 128), BF16),
        msg_gz=((8, 128), F32),
        buf_gs=((2, 256, 128), BF16),
        buf_gz=((2, 8, 128), F32),
        key_acc=(square, F32),
        val_acc=(square, F32),
        low_grads=((3, 512, 512), BF16),
        lo_s=(square, BF16),
        ig_s=(square, BF16),
        part=((3, 2, 2, 512, 512), BF16),
        buf_core=((3, 2, 512, 512), BF16),
        gain_part=((1, 8, 512), F32),
        gain_sum=((2, 8, 128), F32),
        gain_buf=((7 + others, 8, 128), F32),
    )
    shapes = list(buffers.values())
    for _, _, rows, _, lanes, _ in CHUNKS:
        piece = rows // 2 // OWNERS
        shapes.append(((3, rows // 2, lanes), BF16))
        shapes.append(((others, piece, lanes), BF16))
        shapes.append(((piece, lanes), BF16))
    scratch = [pltpu.VMEM(*spec) for spec in shapes]
    scratch += [
        pltpu.SemaphoreType.DMA((8 + 2 + len(CHUNKS),)),
        pltpu.SemaphoreType.DMA((copies,)),
        pltpu.SemaphoreType.DMA((copies,)),
    ]
    lo, ig, fin, gains = pl.pallas_call(
        functools.partial(layer_kernel, pairs, list(buffers)),
        out_shape=(
            jax.ShapeDtypeStruct((batch, length, share), BF16),
            jax.ShapeDtypeStruct((batch, length, share), BF16),
            jax.ShapeDtypeStruct((3, 512, 512), BF16),
            jax.ShapeDtypeStruct((8, 128), F32),
        ),
        in_specs=[anywhere] * 8 + [vmem] * 3,
        out_specs=(anywhere, anywhere, anywhere, vmem),
        scratch_shapes=scratch,
        compiler_params=pltpu.CompilerParams(
            collective_id=0, has_side_effects=True, vmem_limit_bytes=58 * MIB
        ),
        cost_estimate=pl.CostEstimate(
            flops=11 * 10**9, bytes_accessed=8 * MIB, transcendentals=4 * 10**6
        ),
        name="layer",
    )(
        tokens,
        out_grad,
        query_weight,
        key_weight,
        value_weight,
        attention_output_weight,
        up_weight,
        down_weight,
        segment_ids,
        norm_gain[None],
        feedforward_norm_gain[None],
    )

    lo, ig, q_w, k_w, v_w, o_w, u_w, d_w, g_one, g_two = pl.pallas_call(
        widen_kernel,
        out_shape=(
            jax.ShapeDtypeStruct((batch, length, share), BF16),
            jax.ShapeDtypeStruct((batch, length, share), F32),
            jax.ShapeDtypeStruct((512, 128), F32),
            jax.ShapeDtypeStruct((512, 128), F32),
            jax.ShapeDtypeStruct((512, 128), F32),
            jax.ShapeDtypeStruct((128, 512), F32),
            jax.ShapeDtypeStruct((512, 512), F32),
            jax.ShapeDtypeStruct((512, 512), F32),
            jax.ShapeDtypeStruct((128,), F32),
            jax.ShapeDtypeStruct((128,), F32),
        ),
        in_specs=[anywhere] * 3 + [vmem],
        out_specs=(anywhere,) * 8 + (vmem,) * 2,
        scratch_shapes=[
            pltpu.VMEM((batch, length, share), BF16),
            pltpu.VMEM((3, 512, 512), BF16),
            pltpu.VMEM((batch, length, share), BF16),
            pltpu.VMEM((batch, length, share), F32),
            pltpu.VMEM((3, 512, 512), F32),
            pltpu.VMEM((3, 512, 128), F32),
            pltpu.SemaphoreType.DMA((12,)),
            pltpu.SemaphoreType.DMA((14,)),
        ],
        compiler_params=pltpu.CompilerParams(vmem_limit_bytes=58 * MIB),
        name="widen",
    )(lo, ig, fin, gains)
    return (lo, ig, g_one, q_w, k_w, v_w, o_w, g_two, u_w, d_w)


def solution(mesh):
    in_specs = (
        P(None, "seq", "head"),
        P(),
        P(None, "head"),
        P(None, "head"),
        P(None, "head"),
        P("head", None),
        P(),
        P(None, "head"),
        P("head", None),
        P(None, "seq"),
        P(None, "seq", "head"),
    )
    out_specs = (
        P(None, "seq", "head"),
        P(None, "seq", "head"),
        P("head"),
        P(None, "head"),
        P(None, "head"),
        P(None, "head"),
        P("head", None),
        P("head"),
        P(None, "head"),
        P("head", None),
    )
    return jax.shard_map(body, mesh=mesh, in_specs=in_specs, out_specs=out_specs, check_vma=False)
```

```python
import functools
from types import SimpleNamespace

import jax
import jax.numpy as jnp
from jax import lax
from jax.experimental import pallas as pl
from jax.experimental.pallas import tpu as pltpu
from jax.sharding import PartitionSpec as P

DH = 64
BLOCK = 256
EPSILON = 1e-05
MESH = pl.DeviceIdType.MESH
F32 = jnp.float32
BF16 = jnp.bfloat16
MIB = 1 << 20
KINDS = 4
OWNERS = 4
CHUNKS = (
    (0, 0, 512, 0, 256, True, False),
    (0, 0, 512, 256, 256, False, False),
    (1, 0, 512, 0, 256, False, False),
    (1, 0, 512, 256, 256, False, False),
    (2, 384, 128, 0, 512, True, False),
    (2, 0, 384, 0, 256, True, False),
    (2, 0, 384, 256, 256, True, True),
)
COMBOS = ((0, 1, 0), (0, 1, 1), (1, 1, 0), (1, 1, 1), (1, 0, 0), (1, 0, 1), (0, 0, 1))


def mm(left, right, form="NN"):
    dims = {"NN": ((1,), (0,)), "NT": ((1,), (1,)), "TN": ((0,), (0,))}[form]
    return lax.dot_general(left, right, (dims, ((), ())), preferred_element_type=F32)


def loop(count, step):
    def run(i, carry):
        step(i)
        return carry

    lax.fori_loop(0, count, run, 0)


def span(start, size, multiple=None):
    return pl.ds(pl.multiple_of(start, multiple or size), size)


def rows_loop(total, chunk, step):
    loop(total // chunk, lambda i: step(span(i * chunk, chunk)))


def at128(i):
    return span(i * 128, 128)


def layer_kernel(pairs, names, *refs):
    (tok, og_in, wq, wk, wv, wo, wu, wd, seg, gain_one, gain_two) = refs[:11]
    (lo_out, ig_out, fin, gains) = refs[11:15]
    r_ = SimpleNamespace(**dict(zip(names, refs[15:])))
    chunk_refs = refs[15 + len(names) : -3]
    local_sem, send_sem, recv_sem = refs[-3:]
    xin, ogs, w_qkv, w_o, w_u = (
        r_.xin, r_.ogs, r_.w_qkv, r_.w_o, r_.w_u,
    )
    w_d, unit_one, unit_two, rstd_one, rstd_two = (
        r_.w_d, r_.unit_one, r_.unit_two, r_.rstd_one, r_.rstd_two,
    )
    normed, normed_two, feat, val, mask = (
        r_.normed, r_.normed_two, r_.feat, r_.val, r_.mask,
    )
    seg_col, carry_on, state, scores_low, own_s = (
        r_.seg_col, r_.carry_on, r_.state, r_.scores_low, r_.own_s,
    )
    own_z, msg_s, msg_z, buf_s, buf_z = (
        r_.own_z, r_.msg_s, r_.msg_z, r_.buf_s, r_.buf_z,
    )
    grad_s, grad_z, msg_gs, msg_gz, buf_gs = (
        r_.grad_s, r_.grad_z, r_.msg_gs, r_.msg_gz, r_.buf_gs,
    )
    buf_gz, attn, attn_wide, den_inv, middle = (
        r_.buf_gz, r_.attn, r_.attn_wide, r_.den_inv, r_.middle,
    )
    work, work_two, hid, hid_grad, ffn = (
        r_.work, r_.work_two, r_.hid, r_.hid_grad, r_.ffn,
    )
    norm_grad, middle_grad, middle_low, num_grad, den_grad = (
        r_.norm_grad, r_.middle_grad, r_.middle_low, r_.num_grad, r_.den_grad,
    )
    key_acc, val_acc, low_grads, lo_s, ig_s = (
        r_.key_acc, r_.val_acc, r_.low_grads, r_.lo_s, r_.ig_s,
    )
    gain_sum = r_.gain_sum
    part, buf_core, gain_part, gain_buf, seg_other = (
        r_.part, r_.buf_core, r_.gain_part, r_.gain_buf, r_.seg_other,
    )

    s = lax.axis_index("seq")
    h = lax.axis_index("head")
    pair, par = lax.div(s, 2), lax.rem(s, 2)
    hy, hc = lax.div(h, 2), lax.rem(h, 2)
    member = par * 4 + h
    zb = lax.rem(pair, 2)

    counter = [0]
    sends = []
    local_ids = iter(range(1000))

    def take(n=1):
        counter[0] += n
        return counter[0] - n

    def guarded(cond, act):
        if cond is None:
            act()
        else:
            pl.when(cond)(act)

    def peer(dp, dy, dc):
        return (1 - par if dp else par, 1 - hy if dy else hy, 1 - hc if dc else hc)

    def address(par_to, y_to, c_to):
        return (2 * pair + par_to, 2 * y_to + c_to)

    core, ypeer, xpeer = (address(*peer(*d)) for d in ((0, 0, 1), (0, 1, 0), (1, 0, 0)))
    zpeer = (2 * (pair + 1 - 2 * zb) + par, h)

    def ring(d):
        to = lax.rem(pair + d, pairs)
        return to, (2 * to + par, h)

    def remote(src, dst, device, i=None):
        i = take() if i is None else i
        return pltpu.make_async_remote_copy(
            src_ref=src,
            dst_ref=dst,
            send_sem=send_sem.at[i],
            recv_sem=recv_sem.at[i],
            device_id=device,
            device_id_type=MESH,
        )

    def start(copy):
        copy.start()
        sends.append(copy)
        return copy

    def send(src, dst, device):
        return start(remote(src, dst, device))

    def local(src, dst):
        copy = pltpu.make_async_copy(src, dst, local_sem.at[next(local_ids)])
        copy.start()
        return copy

    def each_ring(act):
        if pairs <= 4:
            for d in range(1, pairs):
                act(d)
        else:
            loop(pairs - 1, lambda i: act(i + 1))

    hcol = at128(h)
    half256 = span(par * 256, 256)
    own_w = [
        [local(w, w_qkv.at[i, :, hcol]) for i, w in enumerate((wq, wk, wv))],
        [local(wo, w_o.at[hcol])],
        [local(wu, w_u.at[h])],
        [local(wd, w_d.at[h])],
    ]
    own_tok = local(tok.at[member], xin.at[half256, hcol])
    own_og = local(og_in.at[member], ogs.at[half256, hcol])
    row8 = lax.broadcasted_iota(jnp.int32, (8, 128), 0)
    neutral = jnp.where(row8 == 4, -1.0, 0.0).astype(F32)
    for slot in range(2):
        buf_s[slot] = jnp.zeros((256, 128), BF16)
        buf_gs[slot] = jnp.zeros((256, 128), BF16)
        buf_gz[slot] = jnp.zeros((8, 128), F32)
        for order in range(2):
            buf_z[slot, order] = neutral

    barrier = pltpu.get_barrier_semaphore()
    for d in COMBOS:
        pl.semaphore_signal(barrier, inc=1, device_id=address(*peer(*d)), device_id_type=MESH)
    each_ring(
        lambda d: pl.semaphore_signal(
            barrier, inc=1, device_id=ring(d)[1], device_id_type=MESH
        )
    )
    pl.semaphore_wait(barrier, len(COMBOS) + pairs - 1)

    def scatter_in(src, dst, combos=COMBOS):
        copies = []
        for d in combos:
            par_to, y_to, c_to = peer(*d)
            copies.append(
                send(
                    src.at[par_to * 4 + 2 * y_to + c_to],
                    dst.at[half256, hcol],
                    address(par_to, y_to, c_to),
                )
            )
        return copies

    def scatter_out(src, dst, combos):
        copies = []
        for d in combos:
            par_to, y_to, c_to = peer(*d)
            copies.append(
                send(
                    src.at[span(par_to * 256, 256), at128(2 * y_to + c_to)],
                    dst.at[member],
                    address(par_to, y_to, c_to),
                )
            )
        return copies

    across = 2 * (1 - hy) + hc
    quarter = par + 2 * zb
    quarter_x = 1 - par + 2 * zb

    def view(kind, shard, eighth=None, eighths=2):
        rows = 32 if kind == 1 else 128
        unit = rows // 2
        if kind == 0:
            where = slice(None) if eighth is None else span(eighth * unit, unit * eighths, unit)
            return w_qkv.at[:, where, at128(shard)]
        if kind == 1:
            if eighth is None:
                return w_o.at[at128(shard)]
            return w_o.at[span(shard * 128 + eighth * unit, unit * eighths, unit)]
        ref = w_u if kind == 2 else w_d
        if eighth is None:
            return ref.at[shard]
        return ref.at[shard, span(eighth * unit, unit * eighths, unit)]

    wt = {}

    def pass_on_weight(kind, eighth, eighths, device, shard=None):
        ref = view(kind, across if shard is None else shard, eighth, eighths)
        return send(ref, ref, device)

    def weight_y(kind):
        wt[kind, "y"] = pass_on_weight(kind, 2 * quarter, 2, ypeer, h)

    def weight_core(kind):
        own = view(kind, h)
        wt[kind, "c"] = [send(own, own, core)]

    def weight_near(kind):
        wt[kind, "y"].wait_recv()
        wt[kind, "x"] = pass_on_weight(kind, 2 * quarter, 2, xpeer)
        wt[kind, "z"] = pass_on_weight(kind, 2 * quarter, 2, zpeer)

    def weight_far(kind):
        wt[kind, "x"].wait_recv()
        wt[kind, "far"] = pass_on_weight(kind, 2 * quarter_x, 2, zpeer)
        wt[kind, "c"].append(pass_on_weight(kind, 4 * zb, 4, core))

    def weight_last(kind):
        wt[kind, "z"].wait_recv()
        wt[kind, "far"].wait_recv()
        wt[kind, "c"].append(pass_on_weight(kind, 4 * (1 - zb), 4, core))

    def weight_own(kind):
        wt[kind, "c"][0].wait_recv()

    def weight_ready(kind):
        for copy in wt[kind, "c"][1:]:
            copy.wait_recv()

    for copy in own_w[0]:
        copy.wait()
    weight_y(0)
    tokens_in = scatter_in(tok, xin)
    seg_copy = send(seg, seg_other, xpeer)
    weight_core(0)
    for kind in (1, 2, 3):
        for copy in own_w[kind]:
            copy.wait()
        weight_y(kind)
    for kind in (1, 2, 3):
        weight_core(kind)
    weight_near(0)
    og_copies = scatter_in(og_in, ogs)
    for copy in tokens_in:
        copy.wait_recv()
    own_tok.wait()
    weight_far(0)

    def norm_rows(source, gain, unit_ref, rstd_ref, out_ref):
        def step(r):
            x = source(r)
            center = x - jnp.mean(x, axis=-1, keepdims=True)
            scale = lax.rsqrt(jnp.mean(center * center, axis=-1, keepdims=True) + EPSILON)
            unit = center * scale
            unit_ref[r, :] = unit
            rstd_ref[r, :] = jnp.broadcast_to(scale, (unit.shape[0], 128))
            out_ref[r, :] = (unit * gain[...]).astype(BF16)

        rows_loop(512, 64, step)

    norm_rows(lambda r: xin[r, :].astype(F32), gain_one, unit_one, rstd_one, normed)

    seg_copy.wait_recv()
    own_row = seg[pl.ds(member, 1), :]
    other_row = seg_other[pl.ds(member, 1), :]
    seg_rows = (
        (own_row * (1 - par) + other_row * par).astype(F32),
        (own_row * par + other_row * (1 - par)).astype(F32),
    )
    first = lax.broadcasted_iota(jnp.int32, (256, 256), 0)
    second = lax.broadcasted_iota(jnp.int32, (256, 256), 1)
    for b in range(2):
        along = jnp.broadcast_to(seg_rows[b], (256, 256))
        down = along.T
        mask[b] = jnp.where((along == down) & (second <= first), 1.0, 0.0)
        seg_col[b] = down[:, :128]
    weight_own(0)

    lane = lax.broadcasted_iota(jnp.int32, (1, 128), 1)
    low_lanes = lane < 64
    spread = (
        lax.broadcasted_iota(jnp.int32, (128, 128), 0) // 64
        == lax.broadcasted_iota(jnp.int32, (128, 128), 1) // 64
    )

    def place(i):
        b, pr = lax.div(i, 4), lax.rem(i, 4)
        return b, pr, span(b * 256, 256), at128(pr)

    def side_place(i, side):
        return place(lax.div(i, 2) * 4 + 2 * side + lax.rem(i, 2))

    def pack(square):
        return jnp.where(low_lanes, square[:64], square[64:])

    def two(rows):
        zero = jnp.zeros_like(rows)
        return jnp.concatenate(
            [jnp.where(low_lanes, rows, zero), jnp.where(low_lanes, zero, rows)], axis=0
        )

    def pick(stacked):
        return jnp.where(low_lanes, stacked[:256], stacked[256:])

    def packed_rows(pr):
        return span(pr * 64, 64)

    last_rows = [seg_col[b, pl.ds(255, 1), :] for b in range(2)]
    keep_mid = jnp.where(last_rows[0] >= last_rows[1], 1.0, 0.0)

    def project(side):
        cols = span(side * 256, 256)

        def step_kind(i):
            work[:, :256] = mm(normed[...], w_qkv[i, :, cols])

            def step(r):
                v = work[r, :256]
                feat[i, r, cols] = jnp.where(
                    v > 0, v + 1.0, jnp.exp(jnp.minimum(v, 0.0))
                ).astype(BF16)

            rows_loop(512, 64, step)

        loop(2, step_kind)
        val[:, cols] = mm(normed[...], w_qkv[2, :, cols]).astype(BF16)

    def own_state(i, side):
        b, pr, rows, cols = side_place(i, side)
        tail = seg_col[b] == seg_col[b, pl.ds(255, 1), :]
        keys = feat[1, rows, cols].astype(F32)
        keys = jnp.where(tail, keys, 0.0)
        own_s[b, packed_rows(pr), :] = pack(mm(keys.astype(BF16), val[rows, cols], "TN"))
        own_z[b, pl.ds(pr, 1), :] = jnp.sum(keys, axis=0, keepdims=True)

    def shift(d, pieces, base):
        to = lax.rem(pair + d + pairs, pairs)
        device = (2 * to + par, h)
        return [remote(src, dst, device, base + i) for i, (src, dst) in enumerate(pieces)]

    forward = {}

    def send_state(order, side):
        loop(4, lambda i: own_state(i, side))
        rows = span(side * 128, 128)
        msg_s[rows, :] = (own_s[1, rows, :] + keep_mid * own_s[0, rows, :]).astype(BF16)
        msg_z[order] = jnp.where(row8 == 4, last_rows[1], own_z[1] + keep_mid * own_z[0])
        for d in (1, 2):
            copies = shift(
                d,
                [
                    (msg_s.at[rows], buf_s.at[d - 1, rows]),
                    (msg_z.at[order], buf_z.at[d - 1, order]),
                ],
                take(2),
            )
            forward[order, d] = copies

            @pl.when(pair + d < pairs)
            def _():
                for copy in copies:
                    copy.start()

    own_z[...] = jnp.zeros_like(own_z)
    project(hy)
    send_state(0, hy)
    weight_near(1)
    weight_last(0)
    weight_near(2)
    weight_ready(0)
    project(1 - hy)
    send_state(1, 1 - hy)
    weight_far(1)
    weight_near(3)

    ones = jnp.ones((256, 128), BF16)
    ready = {}

    def receive_state(order):
        for d in (1, 2):

            @pl.when(pair >= d)
            def _():
                for copy in forward[order, d]:
                    copy.wait_recv()

        if order == 0:
            last_in = buf_z[0, 0, pl.ds(4, 1), :]
            ready["keep_in"] = jnp.where(buf_z[1, 0, pl.ds(4, 1), :] >= last_in, 1.0, 0.0)
            ready["keep_first"] = jnp.where(last_in >= last_rows[0], 1.0, 0.0)
            carry_on[0] = jnp.where(seg_col[0] == last_in, 1.0, 0.0)
            carry_on[1] = jnp.where(seg_col[1] == last_rows[0], 1.0, 0.0)
        buf_z[0, order] = buf_z[0, order] + ready["keep_in"] * buf_z[1, order]

    def enter(order, side):
        def step(i):
            pr = 2 * side + i
            entering = buf_s[0, packed_rows(pr), :].astype(F32) + ready["keep_in"] * buf_s[
                1, packed_rows(pr), :
            ].astype(F32)
            z_in = buf_z[0, order, pl.ds(pr, 1), :]
            middle_s = own_s[0, packed_rows(pr), :] + ready["keep_first"] * entering
            middle_z = own_z[0, pl.ds(pr, 1), :] + ready["keep_first"] * z_in
            for b, (packed, z_row) in enumerate(((entering, z_in), (middle_s, middle_z))):
                wide = jnp.where(spread, jnp.broadcast_to(z_row, (128, 128)).T, 0.0)
                state[b * 4 + pr, :, :128] = two(packed).astype(BF16)
                state[b * 4 + pr, :, 128:] = wide.astype(BF16)

        loop(2, step)

    def attend(i, side):
        b, pr, rows, cols = side_place(i, side)
        q, k, v = feat[0, rows, cols], feat[1, rows, cols], val[rows, cols]
        scores = mm(two(q), k, "NT")
        m = mask[b]
        low = jnp.concatenate([scores[:256] * m, scores[256:] * m], axis=0).astype(BF16)
        scores_low[b * 4 + pr] = low
        both = mm(low, jnp.concatenate([v, ones], axis=1))
        carried = mm(q, state[b * 4 + pr])
        c = carry_on[b]
        numer = pick(both[:, :128]) + c * carried[:, :128]
        denom = pick(both[:, 128:]) + c * carried[:, 128:]
        inverse = 1.0 / denom
        result = numer * inverse
        den_inv[rows, cols] = inverse
        attn_wide[rows, cols] = result
        attn[rows, cols] = result.astype(BF16)

    receive_state(0)
    enter(0, hy)
    loop(4, lambda i: attend(i, hy))
    weight_far(2)
    receive_state(1)
    enter(1, 1 - hy)
    weight_last(1)
    loop(4, lambda i: attend(i, 1 - hy))
    keep_first = ready["keep_first"]
    weight_own(1)
    weight_ready(1)

    weight_far(3)
    work[...] = mm(attn[...], w_o[...])

    def mid_step(r):
        middle[r, :] = xin[r, :].astype(F32) + work[r, :]

    rows_loop(512, 64, mid_step)
    norm_rows(
        lambda r: middle[r, :].astype(BF16).astype(F32), gain_two, unit_two, rstd_two, normed_two
    )
    for copy in og_copies:
        copy.wait_recv()
    own_og.wait()
    weight_own(2)
    weight_own(3)

    def core_send(view_src, view_dst):
        return send(view_src, view_dst, core)

    def add_core(u, jy, row, rows):
        def step(i):
            r = span(row + i * 64, 64)
            part[u, jy, hc, r, :] = (
                part[u, jy, hc, r, :].astype(F32) + buf_core[u, jy, r, :].astype(F32)
            ).astype(BF16)

        loop(rows // 64, step)

    owner = None if pairs == OWNERS else pair < OWNERS

    class Chunk:
        def __init__(self, n):
            self.u, self.row, self.rows, self.lane, self.lanes = CHUNKS[n][:5]
            self.y_first, self.x_then_z = CHUNKS[n][5:]
            self.half = self.rows // 2
            self.piece = self.half // OWNERS
            self.buf, self.ring_buf, self.own, self.own_x = chunk_refs[4 * n : 4 * n + 4]
            self.cols = pl.ds(self.lane, self.lanes)
            self.devices = (ypeer, xpeer) if self.y_first else (xpeer, ypeer)
            self.ring_base = self.spread_base = None

        def rows_of(self, half, at=0, size=None):
            return span(self.row + half * self.half + at, size or self.half, 16)

        def at(self, jy, half):
            return part.at[self.u, jy, hc, self.rows_of(half), self.cols]

        def a(self):
            self.first = send(self.at(1 - hy, 1 - par), self.buf.at[0], self.devices[0])

        def b(self):
            source = (1 - hy, par) if self.y_first else (hy, 1 - par)
            self.other = send(self.at(*source), self.buf.at[1], self.devices[0])

        def mid(self):
            self.first.wait_recv()
            jy, half = (hy, 1 - par) if self.y_first else (1 - hy, par)

            def step(i):
                r = self.rows_of(half, i * self.piece, self.piece)
                got = self.buf[0, span(i * self.piece, self.piece), :].astype(F32)
                part[self.u, jy, hc, r, self.cols] = (
                    part[self.u, jy, hc, r, self.cols].astype(F32) + got
                ).astype(BF16)

            loop(OWNERS, step)
            self.second = send(self.at(jy, half), self.buf.at[2], self.devices[1])

        def ring_copy(self, d):
            to, device = ring(d)
            rows = self.rows_of(par, lax.rem(to, OWNERS) * self.piece, self.piece)
            copy = remote(
                part.at[self.u, hy, hc, rows, self.cols],
                self.ring_buf.at[d - 1],
                device,
                self.ring_base + d - 1,
            )
            return copy, None if pairs == OWNERS else to < OWNERS

        def ring(self):
            self.other.wait_recv()
            self.second.wait_recv()

            def step(i):
                r = self.rows_of(par, i * self.piece, self.piece)
                b = span(i * self.piece, self.piece)
                got = self.buf[1, b, :].astype(F32) + self.buf[2, b, :].astype(F32)
                part[self.u, hy, hc, r, self.cols] = (
                    part[self.u, hy, hc, r, self.cols].astype(F32) + got
                ).astype(BF16)

            loop(OWNERS, step)
            self.ring_base = take(pairs - 1)

            def go(d):
                copy, cond = self.ring_copy(d)
                guarded(cond, copy.start)

            each_ring(go)

        def final(self, index, half=par):
            rows = self.rows_of(half, lax.rem(index, OWNERS) * self.piece, self.piece)
            return fin.at[self.u, rows, self.cols]

        def spread_copy(self, d):
            return remote(
                self.own, self.final(pair), ring(d)[1], self.spread_base + d - 1
            )

        def spread(self):
            self.spread_base = take(pairs - 1)
            sem = local_sem.at[next(local_ids)]
            self.kept = pltpu.make_async_copy(self.own, self.final(pair), sem)
            if self.x_then_z:
                self.across = remote(self.own, self.own_x, xpeer)
                self.spread_x_base = take(pairs - 1)
                sem = local_sem.at[next(local_ids)]
                self.kept_x = pltpu.make_async_copy(self.own_x, self.final(pair, 1 - par), sem)

            def total():
                each_ring(lambda d: self.ring_copy(d)[0].wait_recv())
                rows = self.rows_of(par, lax.rem(pair, OWNERS) * self.piece, self.piece)
                self.own[...] = part[self.u, hy, hc, rows, self.cols]

                def more(d):
                    self.own[...] = (
                        self.own[...].astype(F32) + self.ring_buf[d - 1].astype(F32)
                    ).astype(BF16)

                if pairs == OWNERS:
                    value = part[self.u, hy, hc, rows, self.cols].astype(F32)
                    for d in range(1, pairs):
                        value = value + self.ring_buf[d - 1].astype(F32)
                    self.own[...] = value.astype(BF16)
                else:
                    each_ring(more)
                if self.x_then_z:
                    self.across.start()
                each_ring(lambda d: self.spread_copy(d).start())
                self.kept.start()

            guarded(owner, total)

        def spread_x_copy(self, d):
            return remote(
                self.own_x,
                self.final(pair, 1 - par),
                ring(d)[1],
                self.spread_x_base + d - 1,
            )

        def arrived(self, copy_of):
            def one(d):
                giver = lax.rem(pair - d + pairs, pairs)
                cond = None if pairs == OWNERS else giver < OWNERS
                guarded(cond, copy_of(d).wait_recv)

            each_ring(one)

        def back(self):
            if self.x_then_z:

                def pass_on():
                    self.across.wait_recv()
                    each_ring(lambda d: self.spread_x_copy(d).start())
                    self.kept_x.start()

                guarded(owner, pass_on)
                return
            self.arrived(self.spread_copy)
            guarded(owner, self.kept.wait)
            rows = fin.at[self.u, self.rows_of(par), self.cols]
            self.last = send(rows, rows, xpeer)

        def end(self):
            if self.x_then_z:
                self.arrived(self.spread_copy)
                self.arrived(self.spread_x_copy)
                guarded(owner, self.kept.wait)
                guarded(owner, self.kept_x.wait)
            else:
                self.last.wait_recv()

        def sent(self):
            def one(d):
                copy, cond = self.ring_copy(d)
                guarded(cond, copy.wait_send)

            each_ring(one)
            guarded(owner, lambda: each_ring(lambda d: self.spread_copy(d).wait_send()))
            if self.x_then_z:
                guarded(owner, self.across.wait_send)
                guarded(owner, lambda: each_ring(lambda d: self.spread_x_copy(d).wait_send()))

    lo_copies, ig_copies = [], []
    d0, d1, u0, u1, o0, a0, a1 = chunks = [Chunk(n) for n in range(len(CHUNKS))]

    def zero_rows(r):
        ffn[r, :] = jnp.zeros((64, 512), F32)
        norm_grad[r, :] = jnp.zeros((64, 512), F32)

    rows_loop(512, 64, zero_rows)

    def feed(jc, jy):
        j = 2 * jy + jc
        work[...] = mm(normed_two[...], w_u[j])
        work_two[...] = mm(ogs[...], w_d[j], "NT")

        def step(r):
            v = work[r, :]
            sigma = 1.0 / (1.0 + jnp.exp(-v))
            hid[r, :] = (v * sigma).astype(BF16)
            hid_grad[r, :] = (work_two[r, :] * (sigma * (1.0 + v * (1.0 - sigma)))).astype(BF16)

        rows_loop(512, 64, step)
        part[0, jy, jc] = mm(hid[...], ogs[...], "TN").astype(BF16)
        part[1, jy, jc] = mm(normed_two[...], hid_grad[...], "TN").astype(BF16)

    def feed_on(jc, jy):
        j = 2 * jy + jc
        ffn[...] += mm(hid[...], w_d[j])
        norm_grad[...] += mm(hid_grad[...], w_u[j], "NT")

    def core_feed(jy):
        return core_send(part.at[0:2, jy, 1 - hc], buf_core.at[0:2, jy])

    def core_fed(copy, jy):
        copy.wait_recv()
        add_core(0, jy, 0, 512)
        add_core(1, jy, 0, 512)

    feed(1 - hc, hy)
    core_f = core_feed(hy)
    feed_on(1 - hc, hy)
    weight_last(2)
    feed(hc, hy)
    core_fed(core_f, hy)
    weight_last(3)
    u1.b()
    u0.b()
    feed_on(hc, hy)
    weight_ready(2)
    weight_ready(3)
    feed(1 - hc, 1 - hy)
    core_f = core_feed(1 - hy)
    feed_on(1 - hc, 1 - hy)
    feed(hc, 1 - hy)
    core_fed(core_f, 1 - hy)
    u1.a()
    feed_on(hc, 1 - hy)

    u0.a()
    gain_part[0] = jnp.zeros((8, 512), F32)
    row_512 = lax.broadcasted_iota(jnp.int32, (8, 512), 0)

    def norm_back(grad_ref, gain, unit_ref, rstd_ref, base, sink, row):
        def step(r):
            grad = grad_ref[r, :]
            unit = unit_ref[r, :]
            scaled = grad * gain[...]
            mean_one = jnp.mean(scaled, axis=-1, keepdims=True)
            mean_two = jnp.mean(scaled * unit, axis=-1, keepdims=True)
            rstd = rstd_ref[r, :]
            rstd = jnp.concatenate([rstd] * 4, axis=1)
            sink(r, base(r) + rstd * (scaled - mean_one - unit * mean_two))
            total = jnp.sum(grad * unit, axis=0, keepdims=True)
            gain_part[0] = gain_part[0] + jnp.where(row_512 == row, total, 0.0)

        rows_loop(512, 64, step)

    def sink_middle(r, grad):
        middle_grad[r, :] = grad
        middle_low[r, :] = grad.astype(BF16)
        lo_s[r, :] = (middle[r, :] + ffn[r, :]).astype(BF16)

    norm_back(
        norm_grad, gain_two, unit_two, rstd_two, lambda r: ogs[r, :].astype(F32), sink_middle, 1
    )

    d1.b()
    d0.a()
    lo_own = local(lo_s.at[half256, hcol], lo_out.at[member])
    out_rows = pl.ds(384, 128)
    work_two[...] = mm(attn[...], middle_low[...], "TN")
    for j in range(4):
        part[2, j // 2, j % 2, out_rows, :] = work_two[j * 128 : (j + 1) * 128, :].astype(BF16)
    core_o = core_send(part.at[2, :, 1 - hc, out_rows], buf_core.at[2, :, out_rows])
    work[...] = mm(middle_low[...], w_o[...], "NT")

    head_ones = jnp.where(spread, 1.0, 0.0).astype(BF16)
    head_ones = jnp.concatenate([head_ones, head_ones], axis=0)
    first_lane = lax.rem(lane, 64) == 0
    second_lane = lax.rem(lane, 64) == 1

    def split(wide):
        high = wide.astype(BF16)
        return high, (wide - high.astype(F32)).astype(BF16)

    grad_z[...] = jnp.zeros_like(grad_z)

    def outer(i):
        b, pr, rows, cols = place(i)
        grad, inverse = work[rows, cols], den_inv[rows, cols]
        gnum = (grad * inverse).astype(BF16)
        high, low = split(grad * attn_wide[rows, cols])
        gden = -mm(jnp.concatenate([high, low], axis=1), head_ones) * inverse
        dhigh = gden.astype(BF16).astype(F32)
        num_grad[rows, cols] = gnum
        den_grad[rows, cols] = jnp.where(
            first_lane, dhigh, jnp.where(second_lane, gden - dhigh, 0.0)
        ).astype(BF16)
        queries = feat[0, rows, cols].astype(F32) * carry_on[b]
        grad_s[b, packed_rows(pr), :] = pack(mm(queries.astype(BF16), gnum, "TN"))
        grad_z[b, pl.ds(pr, 1), :] = jnp.sum(queries * gden, axis=0, keepdims=True)

    loop(8, outer)
    msg_gs[...] = (grad_s[0] + keep_first * grad_s[1]).astype(BF16)
    msg_gz[...] = jnp.where(row8 == 4, keep_first * keep_mid, grad_z[0] + keep_first * grad_z[1])
    backward = {}
    for d in (1, 2):
        pieces = [(msg_gs, buf_gs.at[d - 1]), (msg_gz, buf_gz.at[d - 1])]
        backward[d] = shift(-d, pieces, take(2))

        @pl.when(pair >= d)
        def _():
            for copy in backward[d]:
                copy.start()

    u1.mid()

    marks = jnp.where(first_lane | second_lane, 1.0, 0.0).astype(BF16)
    marks = jnp.broadcast_to(marks, (256, 128))

    def inner(i):
        b, pr, rows, cols = place(i)
        q, k, v = feat[0, rows, cols], feat[1, rows, cols], val[rows, cols]
        gnum, gden = num_grad[rows, cols], den_grad[rows, cols]
        gnum_two = two(gnum)
        grads = jnp.concatenate([gnum_two, two(gden)], axis=1)
        values = jnp.concatenate([v, marks], axis=1)
        m = mask[b]
        gsc = mm(grads, values, "NT")
        gsc = jnp.concatenate([gsc[:256] * m, gsc[256:] * m], axis=0).astype(BF16)
        qgrad = pick(mm(gsc, k)) + carry_on[b] * mm(
            jnp.concatenate([gnum, gden], axis=1), state[i], "NT"
        )
        low_grads[0, rows, cols] = (qgrad * jnp.minimum(q.astype(F32), 1.0)).astype(BF16)
        key_acc[rows, cols] = mm(gsc, two(q), "TN")
        val_acc[rows, cols] = mm(scores_low[i], gnum_two, "TN")

    loop(4, inner)
    d0.b()
    core_o.wait_recv()
    add_core(2, 0, 384, 128)
    add_core(2, 1, 384, 128)
    d0.mid()
    loop(4, lambda i: inner(4 + i))

    d1.a()
    u1.ring()
    for d in (1, 2):

        @pl.when(pair + d < pairs)
        def _():
            for copy in backward[d]:
                copy.wait_recv()

    pass_on = buf_gz[0, pl.ds(4, 1), :]
    buf_gz[0] = buf_gz[0] + pass_on * buf_gz[1]

    o0.a()
    def leave(i):
        b, pr, rows, cols = place(i)
        leaving = buf_gs[0, packed_rows(pr), :].astype(F32) + pass_on * buf_gs[
            1, packed_rows(pr), :
        ].astype(F32)
        z_leaving = buf_gz[0, pl.ds(pr, 1), :]
        first_block = (1 - b).astype(F32)
        scale = first_block * keep_mid + (1.0 - first_block)
        leaving = scale * leaving + first_block * grad_s[1, packed_rows(pr), :]
        z_leaving = scale * z_leaving + first_block * grad_z[1, pl.ds(pr, 1), :]
        square = two(leaving).astype(BF16)
        k, v = feat[1, rows, cols], val[rows, cols]
        tail = seg_col[b] == seg_col[b, pl.ds(255, 1), :]
        kgrad = key_acc[rows, cols] + jnp.where(tail, mm(v, square, "NT") + z_leaving, 0.0)
        low_grads[1, rows, cols] = (kgrad * jnp.minimum(k.astype(F32), 1.0)).astype(BF16)
        vgrad = val_acc[rows, cols] + jnp.where(tail, mm(k, square), 0.0)
        low_grads[2, rows, cols] = vgrad.astype(BF16)

    loop(8, leave)

    u0.mid()
    lo_copies += scatter_out(lo_s, lo_out, COMBOS[4:])
    d0.ring()
    def qkv_weight(i):
        work[...] = mm(low_grads[i], normed[...], "TN")
        for j in range(4):
            part[2, j // 2, j % 2, at128(i), :] = work[j * 128 : (j + 1) * 128, :].astype(BF16)

    loop(3, qkv_weight)
    qkv_rows = pl.ds(0, 384)
    core_a = [
        core_send(part.at[2, jy, 1 - hc, qkv_rows], buf_core.at[2, jy, qkv_rows])
        for jy in (1 - hy, hy)
    ]
    norm_grad[...] = mm(low_grads[0], w_qkv[0], "NT")
    o0.b()
    u1.spread()
    core_a[0].wait_recv()
    add_core(2, 1 - hy, 0, 384)
    core_a[1].wait_recv()
    add_core(2, hy, 0, 384)
    a0.a()
    a0.b()
    norm_grad[...] += mm(low_grads[1], w_qkv[1], "NT")
    u0.ring()
    o0.mid()
    norm_grad[...] += mm(low_grads[2], w_qkv[2], "NT")

    def sink_input(r, grad):
        ig_s[r, :] = grad.astype(BF16)

    norm_back(norm_grad, gain_one, unit_one, rstd_one, lambda r: middle_grad[r, :], sink_input, 0)

    def gain_start():
        copies = []
        for n, d in enumerate(COMBOS):
            par_to, y_to, c_to = peer(*d)
            copies.append(
                send(
                    gain_part.at[0, :, at128(2 * y_to + c_to)],
                    gain_buf.at[n],
                    address(par_to, y_to, c_to),
                )
            )
        return copies

    gain_base = take(pairs - 1)

    def gain_copy(d):
        return remote(gain_sum.at[0], gain_buf.at[6 + d], ring(d)[1], gain_base + d - 1)

    def gain_middle(copies):
        for copy in copies:
            copy.wait_recv()
        total = gain_part[0, :, hcol]
        for n in range(len(COMBOS)):
            total = total + gain_buf[n]
        gain_sum[0] = total
        each_ring(lambda d: gain_copy(d).start())

    def gain_end():
        each_ring(lambda d: gain_copy(d).wait_recv())
        gain_sum[1] = gain_sum[0]

        def add_gain(d):
            gain_sum[1] = gain_sum[1] + gain_buf[6 + d]

        each_ring(add_gain)
        gains[...] = gain_sum[1]

    d0.spread()
    a1.a()
    ig_copies += scatter_out(ig_s, ig_out, COMBOS[4:])
    d1.mid()
    a0.mid()
    u1.back()
    ig_copies += scatter_out(ig_s, ig_out, COMBOS[:4])
    o0.ring()
    gain_copies = gain_start()
    ig_own = local(ig_s.at[half256, hcol], ig_out.at[member])
    a1.mid()
    a0.ring()
    d0.back()
    u0.spread()
    o0.spread()
    a1.b()
    d1.ring()
    u0.back()
    a0.spread()
    lo_copies += scatter_out(lo_s, lo_out, COMBOS[:4])
    a1.ring()
    d1.spread()
    a0.back()
    a1.spread()
    gain_middle(gain_copies)
    o0.back()
    d1.back()
    a1.back()
    gain_end()

    for chunk in chunks:
        chunk.end()
    for copy in lo_copies + ig_copies:
        copy.wait_recv()
    lo_own.wait()
    ig_own.wait()
    for copy in sends:
        copy.wait_send()
    for chunk in chunks:
        chunk.sent()
    each_ring(lambda d: gain_copy(d).wait_send())
    for d in (1, 2):

        @pl.when(pair + d < pairs)
        def _():
            for order in range(2):
                for copy in forward[order, d]:
                    copy.wait_send()

        @pl.when(pair >= d)
        def _():
            for copy in backward[d]:
                copy.wait_send()


def widen_kernel(lo, ig, fin, gains, *refs):
    lo_o, ig_o, q_o, k_o, v_o, o_o, u_o, d_o, g_o, f_o = refs[:10]
    ig_b, fin_b, lo_b, ig_w, fin_w, qkv_w, sem_in, sem_out = refs[10:]
    parts = []
    for u in (0, 1, 2):
        for half in range(2):
            rows = pl.ds(half * 256, 256)
            parts.append((fin.at[u, rows], fin_b.at[u, rows], u, half))
    for quarter in range(4):
        rows = pl.ds(quarter * 2, 2)
        parts.append((ig.at[rows], ig_b.at[rows], 3, quarter))
    for half in range(2):
        rows = pl.ds(half * 4, 4)
        parts.append((lo.at[rows], lo_b.at[rows], 4, half))
    arriving = [
        pltpu.make_async_copy(source, into, sem_in.at[n])
        for n, (source, into, _, _) in enumerate(parts)
    ]
    for copy in arriving:
        copy.start()
    g_o[...] = gains[0]
    f_o[...] = gains[1]
    leaving = []

    def leave(source, out):
        copy = pltpu.make_async_copy(source, out, sem_out.at[len(leaving)])
        copy.start()
        leaving.append(copy)

    for copy, (_, _, u, n) in zip(arriving, parts, strict=True):
        copy.wait()
        if u == 4:
            rows = pl.ds(n * 4, 4)
            leave(lo_b.at[rows], lo_o.at[rows])
        elif u == 3:
            rows = pl.ds(n * 2, 2)
            ig_w[rows] = ig_b[rows].astype(F32)
            leave(ig_w.at[rows], ig_o.at[rows])
        elif u < 2:
            rows = pl.ds(n * 256, 256)
            fin_w[u, rows] = fin_b[u, rows].astype(F32)
            leave(fin_w.at[u, rows], (d_o, u_o)[u].at[rows])
        else:
            for i in (2 * n, 2 * n + 1):
                rows = pl.ds(i * 128, 128)
                if i < 3:
                    qkv_w[i] = fin_b[2, rows].astype(F32).T
                    leave(qkv_w.at[i], (q_o, k_o, v_o)[i])
                else:
                    fin_w[2, pl.ds(0, 128)] = fin_b[2, rows].astype(F32)
                    leave(fin_w.at[2, pl.ds(0, 128)], o_o)
    for copy in leaving:
        copy.wait()


def body(
    tokens,
    norm_gain,
    query_weight,
    key_weight,
    value_weight,
    attention_output_weight,
    feedforward_norm_gain,
    up_weight,
    down_weight,
    segment_ids,
    out_grad,
):
    batch, length, share = tokens.shape
    width, head_cols = query_weight.shape
    units = up_weight.shape[1]
    pairs = lax.axis_size("seq") // 2
    assert lax.axis_size("head") == 4 and batch == 8 and length == BLOCK
    assert (width, share, head_cols, units) == (512, 128, 128, 512)
    assert pairs >= OWNERS and pairs % 2 == 0
    others = pairs - 1
    anywhere = pl.BlockSpec(memory_space=pl.ANY)
    vmem = pl.BlockSpec(memory_space=pltpu.VMEM)
    copies = 7 * 4 + 1 + 7 * KINDS + 8 + 4 + 5 + len(CHUNKS) * (4 + 3 * others) + 7 + others
    square = (512, 512)
    buffers = dict(
        xin=(square, BF16),
        ogs=(square, BF16),
        w_qkv=((3, 512, 512), BF16),
        w_o=(square, BF16),
        w_u=((4, 512, 512), BF16),
        w_d=((4, 512, 512), BF16),
        seg_other=((8, 256), jnp.int32),
        unit_one=(square, F32),
        unit_two=(square, F32),
        rstd_one=((512, 128), F32),
        rstd_two=((512, 128), F32),
        normed=(square, BF16),
        normed_two=(square, BF16),
        feat=((2, 512, 512), BF16),
        val=(square, BF16),
        mask=((2, 256, 256), F32),
        seg_col=((2, 256, 128), F32),
        carry_on=((2, 256, 128), F32),
        own_s=((2, 256, 128), F32),
        own_z=((2, 8, 128), F32),
        msg_s=((256, 128), BF16),
        msg_z=((2, 8, 128), F32),
        buf_s=((2, 256, 128), BF16),
        buf_z=((2, 2, 8, 128), F32),
        state=((8, 128, 256), BF16),
        scores_low=((8, 512, 256), BF16),
        attn=(square, BF16),
        attn_wide=(square, F32),
        den_inv=(square, F32),
        middle=(square, F32),
        work=(square, F32),
        work_two=(square, F32),
        hid=(square, BF16),
        hid_grad=(square, BF16),
        ffn=(square, F32),
        norm_grad=(square, F32),
        middle_grad=(square, F32),
        middle_low=(square, BF16),
        num_grad=(square, BF16),
        den_grad=(square, BF16),
        grad_s=((2, 256, 128), F32),
        grad_z=((2, 8, 128), F32),
        msg_gs=((256, 128), BF16),
        msg_gz=((8, 128), F32),
        buf_gs=((2, 256, 128), BF16),
        buf_gz=((2, 8, 128), F32),
        key_acc=(square, F32),
        val_acc=(square, F32),
        low_grads=((3, 512, 512), BF16),
        lo_s=(square, BF16),
        ig_s=(square, BF16),
        part=((3, 2, 2, 512, 512), BF16),
        buf_core=((3, 2, 512, 512), BF16),
        gain_part=((1, 8, 512), F32),
        gain_sum=((2, 8, 128), F32),
        gain_buf=((7 + others, 8, 128), F32),
    )
    shapes = list(buffers.values())
    for _, _, rows, _, lanes, _, _ in CHUNKS:
        piece = rows // 2 // OWNERS
        shapes.append(((3, rows // 2, lanes), BF16))
        shapes.append(((others, piece, lanes), BF16))
        shapes.append(((piece, lanes), BF16))
        shapes.append(((piece, lanes), BF16))
    scratch = [pltpu.VMEM(*spec) for spec in shapes]
    scratch += [
        pltpu.SemaphoreType.DMA((8 + 2 + 2 * len(CHUNKS),)),
        pltpu.SemaphoreType.DMA((copies,)),
        pltpu.SemaphoreType.DMA((copies,)),
    ]
    lo, ig, fin, gains = pl.pallas_call(
        functools.partial(layer_kernel, pairs, list(buffers)),
        out_shape=(
            jax.ShapeDtypeStruct((batch, length, share), BF16),
            jax.ShapeDtypeStruct((batch, length, share), BF16),
            jax.ShapeDtypeStruct((3, 512, 512), BF16),
            jax.ShapeDtypeStruct((8, 128), F32),
        ),
        in_specs=[anywhere] * 8 + [vmem] * 3,
        out_specs=(anywhere, anywhere, anywhere, vmem),
        scratch_shapes=scratch,
        compiler_params=pltpu.CompilerParams(
            collective_id=0, has_side_effects=True, vmem_limit_bytes=58 * MIB
        ),
        cost_estimate=pl.CostEstimate(
            flops=11 * 10**9, bytes_accessed=8 * MIB, transcendentals=4 * 10**6
        ),
        name="layer",
    )(
        tokens,
        out_grad,
        query_weight,
        key_weight,
        value_weight,
        attention_output_weight,
        up_weight,
        down_weight,
        segment_ids,
        norm_gain[None],
        feedforward_norm_gain[None],
    )

    lo, ig, q_w, k_w, v_w, o_w, u_w, d_w, g_one, g_two = pl.pallas_call(
        widen_kernel,
        out_shape=(
            jax.ShapeDtypeStruct((batch, length, share), BF16),
            jax.ShapeDtypeStruct((batch, length, share), F32),
            jax.ShapeDtypeStruct((512, 128), F32),
            jax.ShapeDtypeStruct((512, 128), F32),
            jax.ShapeDtypeStruct((512, 128), F32),
            jax.ShapeDtypeStruct((128, 512), F32),
            jax.ShapeDtypeStruct((512, 512), F32),
            jax.ShapeDtypeStruct((512, 512), F32),
            jax.ShapeDtypeStruct((128,), F32),
            jax.ShapeDtypeStruct((128,), F32),
        ),
        in_specs=[anywhere] * 3 + [vmem],
        out_specs=(anywhere,) * 8 + (vmem,) * 2,
        scratch_shapes=[
            pltpu.VMEM((batch, length, share), BF16),
            pltpu.VMEM((3, 512, 512), BF16),
            pltpu.VMEM((batch, length, share), BF16),
            pltpu.VMEM((batch, length, share), F32),
            pltpu.VMEM((3, 512, 512), F32),
            pltpu.VMEM((3, 512, 128), F32),
            pltpu.SemaphoreType.DMA((12,)),
            pltpu.SemaphoreType.DMA((14,)),
        ],
        compiler_params=pltpu.CompilerParams(vmem_limit_bytes=58 * MIB),
        name="widen",
    )(lo, ig, fin, gains)
    return (lo, ig, g_one, q_w, k_w, v_w, o_w, g_two, u_w, d_w)


def solution(mesh):
    in_specs = (
        P(None, "seq", "head"),
        P(),
        P(None, "head"),
        P(None, "head"),
        P(None, "head"),
        P("head", None),
        P(),
        P(None, "head"),
        P("head", None),
        P(None, "seq"),
        P(None, "seq", "head"),
    )
    out_specs = (
        P(None, "seq", "head"),
        P(None, "seq", "head"),
        P("head"),
        P(None, "head"),
        P(None, "head"),
        P(None, "head"),
        P("head", None),
        P("head"),
        P(None, "head"),
        P("head", None),
    )
    return jax.shard_map(body, mesh=mesh, in_specs=in_specs, out_specs=out_specs, check_vma=False)
```

```python
import functools
from types import SimpleNamespace

import jax
import jax.numpy as jnp
from jax import lax
from jax.experimental import pallas as pl
from jax.experimental.pallas import tpu as pltpu
from jax.sharding import PartitionSpec as P

DH = 64
BLOCK = 256
EPSILON = 1e-05
MESH = pl.DeviceIdType.MESH
F32 = jnp.float32
BF16 = jnp.bfloat16
MIB = 1 << 20
KINDS = 4
OWNERS = 4
CHUNKS = (
    (0, 0, 512, 0, 256, True, True),
    (0, 0, 512, 256, 256, True, False),
    (1, 0, 512, 0, 256, False, False),
    (1, 0, 512, 256, 256, False, False),
    (2, 384, 128, 0, 512, False, False),
    (2, 0, 384, 0, 256, False, False),
    (2, 0, 384, 256, 256, True, False),
)
COMBOS = ((0, 1, 0), (0, 1, 1), (1, 1, 0), (1, 1, 1), (1, 0, 0), (1, 0, 1), (0, 0, 1))


def mm(left, right, form="NN"):
    dims = {"NN": ((1,), (0,)), "NT": ((1,), (1,)), "TN": ((0,), (0,))}[form]
    return lax.dot_general(left, right, (dims, ((), ())), preferred_element_type=F32)


def loop(count, step, unroll=1):
    def run(i, carry):
        step(i)
        return carry

    lax.fori_loop(0, count, run, 0, unroll=unroll)


def span(start, size, multiple=None):
    return pl.ds(pl.multiple_of(start, multiple or size), size)


def rows_loop(total, chunk, step):
    loop(total // chunk, lambda i: step(span(i * chunk, chunk)))


def at128(i):
    return span(i * 128, 128)


def layer_kernel(pairs, names, *refs):
    (tok, og_in, wq, wk, wv, wo, wu, wd, seg, gain_one, gain_two) = refs[:11]
    (lo_out, ig_out, fin, gains) = refs[11:15]
    r_ = SimpleNamespace(**dict(zip(names, refs[15:])))
    chunk_refs = refs[15 + len(names) : -3]
    local_sem, send_sem, recv_sem = refs[-3:]
    xin, ogs, w_qkv, w_o, w_u = (
        r_.xin, r_.ogs, r_.w_qkv, r_.w_o, r_.w_u,
    )
    w_d, unit_one, unit_two, rstd_one, rstd_two = (
        r_.w_d, r_.unit_one, r_.unit_two, r_.rstd_one, r_.rstd_two,
    )
    normed, normed_two, feat, val, mask = (
        r_.normed, r_.normed_two, r_.feat, r_.val, r_.mask,
    )
    seg_col, carry_on, state, scores_low, own_s = (
        r_.seg_col, r_.carry_on, r_.state, r_.scores_low, r_.own_s,
    )
    own_z, msg_s, msg_z, buf_s, buf_z = (
        r_.own_z, r_.msg_s, r_.msg_z, r_.buf_s, r_.buf_z,
    )
    grad_s, grad_z, msg_gs, msg_gz, buf_gs = (
        r_.grad_s, r_.grad_z, r_.msg_gs, r_.msg_gz, r_.buf_gs,
    )
    buf_gz, attn, attn_wide, den_inv, middle = (
        r_.buf_gz, r_.attn, r_.attn_wide, r_.den_inv, r_.middle,
    )
    work, work_two, hid, hid_grad, ffn = (
        r_.work, r_.work_two, r_.hid, r_.hid_grad, r_.ffn,
    )
    norm_grad, middle_grad, middle_low, num_grad, den_grad = (
        r_.norm_grad, r_.middle_grad, r_.middle_low, r_.num_grad, r_.den_grad,
    )
    key_acc, val_acc, low_grads, lo_s, ig_s = (
        r_.key_acc, r_.val_acc, r_.low_grads, r_.lo_s, r_.ig_s,
    )
    gain_sum = r_.gain_sum
    part, buf_core, gain_part, gain_buf, seg_other = (
        r_.part, r_.buf_core, r_.gain_part, r_.gain_buf, r_.seg_other,
    )

    s = lax.axis_index("seq")
    h = lax.axis_index("head")
    pair, par = lax.div(s, 2), lax.rem(s, 2)
    hy, hc = lax.div(h, 2), lax.rem(h, 2)
    member = par * 4 + h
    zb = lax.rem(pair, 2)

    counter = [0]
    sends = []
    local_ids = iter(range(1000))

    def take(n=1):
        counter[0] += n
        return counter[0] - n

    def guarded(cond, act):
        if cond is None:
            act()
        else:
            pl.when(cond)(act)

    def peer(dp, dy, dc):
        return (1 - par if dp else par, 1 - hy if dy else hy, 1 - hc if dc else hc)

    def address(par_to, y_to, c_to):
        return (2 * pair + par_to, 2 * y_to + c_to)

    core, ypeer, xpeer = (address(*peer(*d)) for d in ((0, 0, 1), (0, 1, 0), (1, 0, 0)))
    zpeer = (2 * (pair + 1 - 2 * zb) + par, h)

    def ring(d):
        to = lax.rem(pair + d, pairs)
        return to, (2 * to + par, h)

    def remote(src, dst, device, i=None):
        i = take() if i is None else i
        return pltpu.make_async_remote_copy(
            src_ref=src,
            dst_ref=dst,
            send_sem=send_sem.at[i],
            recv_sem=recv_sem.at[i],
            device_id=device,
            device_id_type=MESH,
        )

    def start(copy):
        copy.start()
        sends.append(copy)
        return copy

    def send(src, dst, device):
        return start(remote(src, dst, device))

    def local(src, dst):
        copy = pltpu.make_async_copy(src, dst, local_sem.at[next(local_ids)])
        copy.start()
        return copy

    def each_ring(act):
        if pairs <= 4:
            for d in range(1, pairs):
                act(d)
        else:
            loop(pairs - 1, lambda i: act(i + 1))

    hcol = at128(h)
    half256 = span(par * 256, 256)
    own_w = [
        [local(w, w_qkv.at[i, :, hcol]) for i, w in enumerate((wq, wk, wv))],
        [local(wo, w_o.at[hcol])],
        [local(wu, w_u.at[h])],
        [local(wd, w_d.at[h])],
    ]
    own_tok = local(tok.at[member], xin.at[half256, hcol])
    own_og = local(og_in.at[member], ogs.at[half256, hcol])
    row8 = lax.broadcasted_iota(jnp.int32, (8, 128), 0)
    neutral = jnp.where(row8 == 4, -1.0, 0.0).astype(F32)
    for slot in range(2):
        buf_s[slot] = jnp.zeros((256, 128), BF16)
        buf_gs[slot] = jnp.zeros((256, 128), BF16)
        buf_gz[slot] = jnp.zeros((8, 128), F32)
        for order in range(2):
            buf_z[slot, order] = neutral

    barrier = pltpu.get_barrier_semaphore()
    for d in COMBOS:
        pl.semaphore_signal(barrier, inc=1, device_id=address(*peer(*d)), device_id_type=MESH)
    each_ring(
        lambda d: pl.semaphore_signal(
            barrier, inc=1, device_id=ring(d)[1], device_id_type=MESH
        )
    )
    pl.semaphore_wait(barrier, len(COMBOS) + pairs - 1)

    def scatter_in(src, dst, combos=COMBOS):
        copies = []
        for d in combos:
            par_to, y_to, c_to = peer(*d)
            copies.append(
                send(
                    src.at[par_to * 4 + 2 * y_to + c_to],
                    dst.at[half256, hcol],
                    address(par_to, y_to, c_to),
                )
            )
        return copies

    def scatter_out(src, dst, combos):
        copies = []
        for d in combos:
            par_to, y_to, c_to = peer(*d)
            copies.append(
                send(
                    src.at[span(par_to * 256, 256), at128(2 * y_to + c_to)],
                    dst.at[member],
                    address(par_to, y_to, c_to),
                )
            )
        return copies

    across = 2 * (1 - hy) + hc
    quarter = par + 2 * zb
    quarter_x = 1 - par + 2 * zb

    def view(kind, shard, eighth=None, eighths=2):
        rows = 32 if kind == 1 else 128
        unit = rows // 2
        if kind == 0:
            where = slice(None) if eighth is None else span(eighth * unit, unit * eighths, unit)
            return w_qkv.at[:, where, at128(shard)]
        if kind == 1:
            if eighth is None:
                return w_o.at[at128(shard)]
            return w_o.at[span(shard * 128 + eighth * unit, unit * eighths, unit)]
        ref = w_u if kind == 2 else w_d
        if eighth is None:
            return ref.at[shard]
        return ref.at[shard, span(eighth * unit, unit * eighths, unit)]

    wt = {}

    def pass_on_weight(kind, eighth, eighths, device, shard=None):
        ref = view(kind, across if shard is None else shard, eighth, eighths)
        return send(ref, ref, device)

    def weight_y(kind):
        wt[kind, "y"] = pass_on_weight(kind, 2 * quarter, 2, ypeer, h)

    def weight_core(kind):
        own = view(kind, h)
        wt[kind, "own"] = send(own, own, core)
        wt[kind, "c"] = []

    def weight_near(kind):
        wt[kind, "y"].wait_recv()
        wt[kind, "x"] = pass_on_weight(kind, 2 * quarter, 2, xpeer)
        wt[kind, "z"] = pass_on_weight(kind, 2 * quarter, 2, zpeer)

    def weight_far(kind):
        wt[kind, "x"].wait_recv()
        wt[kind, "far"] = pass_on_weight(kind, 2 * quarter_x, 2, zpeer)
        wt[kind, "c"].append(pass_on_weight(kind, 4 * zb, 4, core))

    def weight_last(kind):
        wt[kind, "z"].wait_recv()
        wt[kind, "far"].wait_recv()
        wt[kind, "c"].append(pass_on_weight(kind, 4 * (1 - zb), 4, core))

    def weight_own(kind):
        wt[kind, "own"].wait_recv()

    def weight_ready(kind):
        for copy in wt[kind, "c"]:
            copy.wait_recv()

    for copies in own_w:
        for copy in copies:
            copy.wait()
    seg_copy = send(seg, seg_other, xpeer)
    tokens_in, og_copies = [], []
    weight_y(0)
    tokens_in += scatter_in(tok, xin, COMBOS[0:2])
    tokens_in += scatter_in(tok, xin, COMBOS[2:4])
    tokens_in += scatter_in(tok, xin, COMBOS[4:])
    weight_core(0)
    weight_y(1)
    weight_y(2)
    weight_y(3)
    weight_core(1)
    weight_core(2)
    weight_core(3)
    weight_near(0)
    og_copies += scatter_in(og_in, ogs, COMBOS[0:2])
    og_copies += scatter_in(og_in, ogs, COMBOS[2:4])
    og_copies += scatter_in(og_in, ogs, COMBOS[4:])
    for copy in tokens_in:
        copy.wait_recv()
    own_tok.wait()

    def norm_rows(source, gain, unit_ref, rstd_ref, out_ref):
        def step(r):
            x = source(r)
            center = x - jnp.mean(x, axis=-1, keepdims=True)
            scale = lax.rsqrt(jnp.mean(center * center, axis=-1, keepdims=True) + EPSILON)
            unit = center * scale
            unit_ref[r, :] = unit
            rstd_ref[r, :] = jnp.broadcast_to(scale, (unit.shape[0], 128))
            out_ref[r, :] = (unit * gain[...]).astype(BF16)

        rows_loop(512, 64, step)

    norm_rows(lambda r: xin[r, :].astype(F32), gain_one, unit_one, rstd_one, normed)

    weight_far(0)
    seg_copy.wait_recv()
    own_row = seg[pl.ds(member, 1), :]
    other_row = seg_other[pl.ds(member, 1), :]
    seg_rows = (
        (own_row * (1 - par) + other_row * par).astype(F32),
        (own_row * par + other_row * (1 - par)).astype(F32),
    )
    first = lax.broadcasted_iota(jnp.int32, (256, 256), 0)
    second = lax.broadcasted_iota(jnp.int32, (256, 256), 1)
    for b in range(2):
        along = jnp.broadcast_to(seg_rows[b], (256, 256))
        down = along.T
        mask[b] = jnp.where((along == down) & (second <= first), 1.0, 0.0)
        seg_col[b] = down[:, :128]
    weight_own(0)
    lane = lax.broadcasted_iota(jnp.int32, (1, 128), 1)
    low_lanes = lane < 64
    spread = (
        lax.broadcasted_iota(jnp.int32, (128, 128), 0) // 64
        == lax.broadcasted_iota(jnp.int32, (128, 128), 1) // 64
    )

    def place(i):
        b, pr = lax.div(i, 4), lax.rem(i, 4)
        return b, pr, span(b * 256, 256), at128(pr)

    def side_place(i, side):
        return place(lax.div(i, 2) * 4 + 2 * side + lax.rem(i, 2))

    def pack(square):
        return jnp.where(low_lanes, square[:64], square[64:])

    def two(rows):
        zero = jnp.zeros_like(rows)
        return jnp.concatenate(
            [jnp.where(low_lanes, rows, zero), jnp.where(low_lanes, zero, rows)], axis=0
        )

    def pick(stacked):
        return jnp.where(low_lanes, stacked[:256], stacked[256:])

    def packed_rows(pr):
        return span(pr * 64, 64)

    last_rows = [seg_col[b, pl.ds(255, 1), :] for b in range(2)]
    keep_mid = jnp.where(last_rows[0] >= last_rows[1], 1.0, 0.0)

    def project(side):
        cols = span(side * 256, 256)

        def step_kind(i):
            work[:, :256] = mm(normed[...], w_qkv[i, :, cols])

            def step(r):
                v = work[r, :256]
                feat[i, r, cols] = jnp.where(
                    v > 0, v + 1.0, jnp.exp(jnp.minimum(v, 0.0))
                ).astype(BF16)

            rows_loop(512, 64, step)

        loop(2, step_kind)
        val[:, cols] = mm(normed[...], w_qkv[2, :, cols]).astype(BF16)

    def own_state(i, side):
        b, pr, rows, cols = side_place(i, side)
        tail = seg_col[b] == seg_col[b, pl.ds(255, 1), :]
        keys = feat[1, rows, cols].astype(F32)
        keys = jnp.where(tail, keys, 0.0)
        own_s[b, packed_rows(pr), :] = pack(mm(keys.astype(BF16), val[rows, cols], "TN"))
        own_z[b, pl.ds(pr, 1), :] = jnp.sum(keys, axis=0, keepdims=True)

    def shift(d, pieces, base):
        to = lax.rem(pair + d + pairs, pairs)
        device = (2 * to + par, h)
        return [remote(src, dst, device, base + i) for i, (src, dst) in enumerate(pieces)]

    forward = {}

    def make_state(order, side):
        loop(4, lambda i: own_state(i, side), 2)
        rows = span(side * 128, 128)
        msg_s[rows, :] = (own_s[1, rows, :] + keep_mid * own_s[0, rows, :]).astype(BF16)
        msg_z[order] = jnp.where(row8 == 4, last_rows[1], own_z[1] + keep_mid * own_z[0])

    def send_state(order, side):
        rows = span(side * 128, 128)
        for d in (1, 2):
            copies = shift(
                d,
                [
                    (msg_s.at[rows], buf_s.at[d - 1, rows]),
                    (msg_z.at[order], buf_z.at[d - 1, order]),
                ],
                take(2),
            )
            forward[order, d] = copies

            @pl.when(pair + d < pairs)
            def _():
                for copy in copies:
                    copy.start()

    own_z[...] = jnp.zeros_like(own_z)
    project(hy)
    make_state(0, hy)
    send_state(0, hy)
    weight_near(1)
    weight_last(0)
    weight_near(2)
    weight_ready(0)
    project(1 - hy)
    make_state(1, 1 - hy)
    send_state(1, 1 - hy)
    weight_far(1)
    weight_near(3)

    ones = jnp.ones((256, 128), BF16)
    ready = {}

    def receive_state(order):
        for d in (1, 2):

            @pl.when(pair >= d)
            def _():
                for copy in forward[order, d]:
                    copy.wait_recv()

        if order == 0:
            last_in = buf_z[0, 0, pl.ds(4, 1), :]
            ready["keep_in"] = jnp.where(buf_z[1, 0, pl.ds(4, 1), :] >= last_in, 1.0, 0.0)
            ready["keep_first"] = jnp.where(last_in >= last_rows[0], 1.0, 0.0)
            carry_on[0] = jnp.where(seg_col[0] == last_in, 1.0, 0.0)
            carry_on[1] = jnp.where(seg_col[1] == last_rows[0], 1.0, 0.0)
        buf_z[0, order] = buf_z[0, order] + ready["keep_in"] * buf_z[1, order]

    def enter(order, side):
        def step(i):
            pr = 2 * side + i
            entering = buf_s[0, packed_rows(pr), :].astype(F32) + ready["keep_in"] * buf_s[
                1, packed_rows(pr), :
            ].astype(F32)
            z_in = buf_z[0, order, pl.ds(pr, 1), :]
            middle_s = own_s[0, packed_rows(pr), :] + ready["keep_first"] * entering
            middle_z = own_z[0, pl.ds(pr, 1), :] + ready["keep_first"] * z_in
            for b, (packed, z_row) in enumerate(((entering, z_in), (middle_s, middle_z))):
                wide = jnp.where(spread, jnp.broadcast_to(z_row, (128, 128)).T, 0.0)
                state[b * 4 + pr, :, :128] = two(packed).astype(BF16)
                state[b * 4 + pr, :, 128:] = wide.astype(BF16)

        loop(2, step)

    def attend(i, side):
        b, pr, rows, cols = side_place(i, side)
        q, k, v = feat[0, rows, cols], feat[1, rows, cols], val[rows, cols]
        scores = mm(two(q), k, "NT")
        m = mask[b]
        low = jnp.concatenate([scores[:256] * m, scores[256:] * m], axis=0).astype(BF16)
        scores_low[b * 4 + pr] = low
        both = mm(low, jnp.concatenate([v, ones], axis=1))
        carried = mm(q, state[b * 4 + pr])
        c = carry_on[b]
        numer = pick(both[:, :128]) + c * carried[:, :128]
        denom = pick(both[:, 128:]) + c * carried[:, 128:]
        inverse = 1.0 / denom
        result = numer * inverse
        den_inv[rows, cols] = inverse
        attn_wide[rows, cols] = result
        attn[rows, cols] = result.astype(BF16)

    receive_state(0)
    enter(0, hy)
    loop(4, lambda i: attend(i, hy), 2)
    weight_far(2)
    receive_state(1)
    enter(1, 1 - hy)
    weight_last(1)
    loop(4, lambda i: attend(i, 1 - hy), 2)
    keep_first = ready["keep_first"]
    weight_own(1)
    weight_ready(1)
    weight_far(3)
    work[...] = mm(attn[...], w_o[...])

    def mid_step(r):
        middle[r, :] = xin[r, :].astype(F32) + work[r, :]

    rows_loop(512, 64, mid_step)
    norm_rows(
        lambda r: middle[r, :].astype(BF16).astype(F32), gain_two, unit_two, rstd_two, normed_two
    )
    for copy in og_copies:
        copy.wait_recv()
    own_og.wait()
    weight_own(2)
    weight_own(3)

    def core_send(view_src, view_dst):
        return send(view_src, view_dst, core)

    def add_core(u, jy, row, rows):
        def step(i):
            r = span(row + i * 64, 64)
            part[u, jy, hc, r, :] = (
                part[u, jy, hc, r, :].astype(F32) + buf_core[u, jy, r, :].astype(F32)
            ).astype(BF16)

        loop(rows // 64, step)

    owner = None if pairs == OWNERS else pair < OWNERS

    class Chunk:
        def __init__(self, n):
            self.u, self.row, self.rows, self.lane, self.lanes = CHUNKS[n][:5]
            self.y_first, self.x_then_z = CHUNKS[n][5:]
            self.half = self.rows // 2
            self.piece = self.half // OWNERS
            self.buf, self.ring_buf, self.own, self.own_x = chunk_refs[4 * n : 4 * n + 4]
            self.cols = pl.ds(self.lane, self.lanes)
            self.devices = (ypeer, xpeer) if self.y_first else (xpeer, ypeer)
            self.ring_base = self.spread_base = None

        def rows_of(self, half, at=0, size=None):
            return span(self.row + half * self.half + at, size or self.half, 16)

        def at(self, jy, half):
            return part.at[self.u, jy, hc, self.rows_of(half), self.cols]

        def a(self):
            self.first = send(self.at(1 - hy, 1 - par), self.buf.at[0], self.devices[0])

        def b(self):
            source = (1 - hy, par) if self.y_first else (hy, 1 - par)
            self.other = send(self.at(*source), self.buf.at[1], self.devices[0])

        def mid(self):
            self.first.wait_recv()
            jy, half = (hy, 1 - par) if self.y_first else (1 - hy, par)

            def step(i):
                r = self.rows_of(half, i * self.piece, self.piece)
                got = self.buf[0, span(i * self.piece, self.piece), :].astype(F32)
                part[self.u, jy, hc, r, self.cols] = (
                    part[self.u, jy, hc, r, self.cols].astype(F32) + got
                ).astype(BF16)

            loop(OWNERS, step)
            self.second = send(self.at(jy, half), self.buf.at[2], self.devices[1])

        def ring_copy(self, d):
            to, device = ring(d)
            rows = self.rows_of(par, lax.rem(to, OWNERS) * self.piece, self.piece)
            copy = remote(
                part.at[self.u, hy, hc, rows, self.cols],
                self.ring_buf.at[d - 1],
                device,
                self.ring_base + d - 1,
            )
            return copy, None if pairs == OWNERS else to < OWNERS

        def ring(self):
            self.other.wait_recv()
            self.second.wait_recv()

            def step(i):
                r = self.rows_of(par, i * self.piece, self.piece)
                b = span(i * self.piece, self.piece)
                got = self.buf[1, b, :].astype(F32) + self.buf[2, b, :].astype(F32)
                part[self.u, hy, hc, r, self.cols] = (
                    part[self.u, hy, hc, r, self.cols].astype(F32) + got
                ).astype(BF16)

            loop(OWNERS, step)
            self.ring_base = take(pairs - 1)

            def go(d):
                copy, cond = self.ring_copy(d)
                guarded(cond, copy.start)

            each_ring(go)

        def final(self, index, half=par):
            rows = self.rows_of(half, lax.rem(index, OWNERS) * self.piece, self.piece)
            return fin.at[self.u, rows, self.cols]

        def spread_copy(self, d):
            return remote(
                self.own, self.final(pair), ring(d)[1], self.spread_base + d - 1
            )

        def spread(self):
            self.spread_base = take(pairs - 1)
            sem = local_sem.at[next(local_ids)]
            self.kept = pltpu.make_async_copy(self.own, self.final(pair), sem)
            if self.x_then_z:
                self.across = remote(self.own, self.own_x, xpeer)
                self.spread_x_base = take(pairs - 1)
                sem = local_sem.at[next(local_ids)]
                self.kept_x = pltpu.make_async_copy(self.own_x, self.final(pair, 1 - par), sem)

            def total():
                each_ring(lambda d: self.ring_copy(d)[0].wait_recv())
                rows = self.rows_of(par, lax.rem(pair, OWNERS) * self.piece, self.piece)
                self.own[...] = part[self.u, hy, hc, rows, self.cols]

                def more(d):
                    self.own[...] = (
                        self.own[...].astype(F32) + self.ring_buf[d - 1].astype(F32)
                    ).astype(BF16)

                if pairs == OWNERS:
                    value = part[self.u, hy, hc, rows, self.cols].astype(F32)
                    for d in range(1, pairs):
                        value = value + self.ring_buf[d - 1].astype(F32)
                    self.own[...] = value.astype(BF16)
                else:
                    each_ring(more)
                if self.x_then_z:
                    self.across.start()
                each_ring(lambda d: self.spread_copy(d).start())
                self.kept.start()

            guarded(owner, total)

        def spread_x_copy(self, d):
            return remote(
                self.own_x,
                self.final(pair, 1 - par),
                ring(d)[1],
                self.spread_x_base + d - 1,
            )

        def arrived(self, copy_of):
            def one(d):
                giver = lax.rem(pair - d + pairs, pairs)
                cond = None if pairs == OWNERS else giver < OWNERS
                guarded(cond, copy_of(d).wait_recv)

            each_ring(one)

        def back(self):
            if self.x_then_z:

                def pass_on():
                    self.across.wait_recv()
                    each_ring(lambda d: self.spread_x_copy(d).start())
                    self.kept_x.start()

                guarded(owner, pass_on)
                return
            self.arrived(self.spread_copy)
            guarded(owner, self.kept.wait)
            rows = fin.at[self.u, self.rows_of(par), self.cols]
            self.last = send(rows, rows, xpeer)

        def end(self):
            if self.x_then_z:
                self.arrived(self.spread_copy)
                self.arrived(self.spread_x_copy)
                guarded(owner, self.kept.wait)
                guarded(owner, self.kept_x.wait)
            else:
                self.last.wait_recv()

        def sent(self):
            def one(d):
                copy, cond = self.ring_copy(d)
                guarded(cond, copy.wait_send)

            each_ring(one)
            guarded(owner, lambda: each_ring(lambda d: self.spread_copy(d).wait_send()))
            if self.x_then_z:
                guarded(owner, self.across.wait_send)
                guarded(owner, lambda: each_ring(lambda d: self.spread_x_copy(d).wait_send()))

    lo_copies, ig_copies = [], []
    d0, d1, u0, u1, o0, a0, a1 = chunks = [Chunk(n) for n in range(len(CHUNKS))]

    def zero_rows(r):
        ffn[r, :] = jnp.zeros((64, 512), F32)
        norm_grad[r, :] = jnp.zeros((64, 512), F32)

    rows_loop(512, 64, zero_rows)

    def feed(jc, jy):
        j = 2 * jy + jc
        work[...] = mm(normed_two[...], w_u[j])
        work_two[...] = mm(ogs[...], w_d[j], "NT")

        def step(r):
            v = work[r, :]
            sigma = 1.0 / (1.0 + jnp.exp(-v))
            hid[r, :] = (v * sigma).astype(BF16)
            hid_grad[r, :] = (work_two[r, :] * (sigma * (1.0 + v * (1.0 - sigma)))).astype(BF16)

        rows_loop(512, 64, step)
        part[0, jy, jc] = mm(hid[...], ogs[...], "TN").astype(BF16)
        part[1, jy, jc] = mm(normed_two[...], hid_grad[...], "TN").astype(BF16)

    def feed_on(jc, jy):
        j = 2 * jy + jc
        ffn[...] += mm(hid[...], w_d[j])
        norm_grad[...] += mm(hid_grad[...], w_u[j], "NT")

    def core_feed(jy):
        return core_send(part.at[0:2, jy, 1 - hc], buf_core.at[0:2, jy])

    def core_fed(copy, jy):
        copy.wait_recv()
        add_core(0, jy, 0, 512)
        add_core(1, jy, 0, 512)

    feed(1 - hc, hy)
    core_f = core_feed(hy)
    feed_on(1 - hc, hy)
    feed(hc, hy)
    core_fed(core_f, hy)
    weight_last(2)
    weight_last(3)
    u0.b()
    feed_on(hc, hy)
    weight_ready(2)
    weight_ready(3)
    u1.b()
    feed(1 - hc, 1 - hy)
    core_f = core_feed(1 - hy)
    feed_on(1 - hc, 1 - hy)
    feed(hc, 1 - hy)
    core_fed(core_f, 1 - hy)
    u0.a()
    d1.a()
    feed_on(hc, 1 - hy)

    gain_part[0] = jnp.zeros((8, 512), F32)
    row_512 = lax.broadcasted_iota(jnp.int32, (8, 512), 0)

    def norm_back(grad_ref, gain, unit_ref, rstd_ref, base, sink, row):
        def step(r):
            grad = grad_ref[r, :]
            unit = unit_ref[r, :]
            scaled = grad * gain[...]
            mean_one = jnp.mean(scaled, axis=-1, keepdims=True)
            mean_two = jnp.mean(scaled * unit, axis=-1, keepdims=True)
            rstd = rstd_ref[r, :]
            rstd = jnp.concatenate([rstd] * 4, axis=1)
            sink(r, base(r) + rstd * (scaled - mean_one - unit * mean_two))
            total = jnp.sum(grad * unit, axis=0, keepdims=True)
            gain_part[0] = gain_part[0] + jnp.where(row_512 == row, total, 0.0)

        rows_loop(512, 64, step)

    def sink_middle(r, grad):
        middle_grad[r, :] = grad
        middle_low[r, :] = grad.astype(BF16)
        lo_s[r, :] = (middle[r, :] + ffn[r, :]).astype(BF16)

    norm_back(
        norm_grad, gain_two, unit_two, rstd_two, lambda r: ogs[r, :].astype(F32), sink_middle, 1
    )

    d0.a()
    lo_own = local(lo_s.at[half256, hcol], lo_out.at[member])
    out_rows = pl.ds(384, 128)
    work_two[...] = mm(attn[...], middle_low[...], "TN")
    for j in range(4):
        part[2, j // 2, j % 2, out_rows, :] = work_two[j * 128 : (j + 1) * 128, :].astype(BF16)
    core_o = core_send(part.at[2, :, 1 - hc, out_rows], buf_core.at[2, :, out_rows])
    work[...] = mm(middle_low[...], w_o[...], "NT")

    u1.a()
    head_ones = jnp.where(spread, 1.0, 0.0).astype(BF16)
    head_ones = jnp.concatenate([head_ones, head_ones], axis=0)
    first_lane = lax.rem(lane, 64) == 0
    second_lane = lax.rem(lane, 64) == 1

    def split(wide):
        high = wide.astype(BF16)
        return high, (wide - high.astype(F32)).astype(BF16)

    grad_z[...] = jnp.zeros_like(grad_z)

    def outer(i):
        b, pr, rows, cols = place(i)
        grad, inverse = work[rows, cols], den_inv[rows, cols]
        gnum = (grad * inverse).astype(BF16)
        high, low = split(grad * attn_wide[rows, cols])
        gden = -mm(jnp.concatenate([high, low], axis=1), head_ones) * inverse
        dhigh = gden.astype(BF16).astype(F32)
        num_grad[rows, cols] = gnum
        den_grad[rows, cols] = jnp.where(
            first_lane, dhigh, jnp.where(second_lane, gden - dhigh, 0.0)
        ).astype(BF16)
        queries = feat[0, rows, cols].astype(F32) * carry_on[b]
        grad_s[b, packed_rows(pr), :] = pack(mm(queries.astype(BF16), gnum, "TN"))
        grad_z[b, pl.ds(pr, 1), :] = jnp.sum(queries * gden, axis=0, keepdims=True)

    loop(8, outer, 2)
    lo_copies += scatter_out(lo_s, lo_out, COMBOS[4:])
    msg_gs[...] = (grad_s[0] + keep_first * grad_s[1]).astype(BF16)
    msg_gz[...] = jnp.where(row8 == 4, keep_first * keep_mid, grad_z[0] + keep_first * grad_z[1])
    backward = {}
    for d in (1, 2):
        pieces = [(msg_gs, buf_gs.at[d - 1]), (msg_gz, buf_gz.at[d - 1])]
        backward[d] = shift(-d, pieces, take(2))

        @pl.when(pair >= d)
        def _():
            for copy in backward[d]:
                copy.start()

    d1.mid()
    u0.mid()

    marks = jnp.where(first_lane | second_lane, 1.0, 0.0).astype(BF16)
    marks = jnp.broadcast_to(marks, (256, 128))

    def inner(i):
        b, pr, rows, cols = place(i)
        q, k, v = feat[0, rows, cols], feat[1, rows, cols], val[rows, cols]
        gnum, gden = num_grad[rows, cols], den_grad[rows, cols]
        gnum_two = two(gnum)
        grads = jnp.concatenate([gnum_two, two(gden)], axis=1)
        values = jnp.concatenate([v, marks], axis=1)
        m = mask[b]
        gsc = mm(grads, values, "NT")
        gsc = jnp.concatenate([gsc[:256] * m, gsc[256:] * m], axis=0).astype(BF16)
        qgrad = pick(mm(gsc, k)) + carry_on[b] * mm(
            jnp.concatenate([gnum, gden], axis=1), state[i], "NT"
        )
        low_grads[0, rows, cols] = (qgrad * jnp.minimum(q.astype(F32), 1.0)).astype(BF16)
        key_acc[rows, cols] = mm(gsc, two(q), "TN")
        val_acc[rows, cols] = mm(scores_low[i], gnum_two, "TN")

    loop(4, inner, 2)
    core_o.wait_recv()
    add_core(2, 0, 384, 128)
    add_core(2, 1, 384, 128)
    u1.mid()
    d0.b()
    d1.b()
    loop(4, lambda i: inner(4 + i), 2)

    u0.ring()
    o0.a()
    d0.mid()
    o0.b()
    for d in (1, 2):

        @pl.when(pair + d < pairs)
        def _():
            for copy in backward[d]:
                copy.wait_recv()

    pass_on = buf_gz[0, pl.ds(4, 1), :]
    buf_gz[0] = buf_gz[0] + pass_on * buf_gz[1]

    def leave(i):
        b, pr, rows, cols = place(i)
        leaving = buf_gs[0, packed_rows(pr), :].astype(F32) + pass_on * buf_gs[
            1, packed_rows(pr), :
        ].astype(F32)
        z_leaving = buf_gz[0, pl.ds(pr, 1), :]
        first_block = (1 - b).astype(F32)
        scale = first_block * keep_mid + (1.0 - first_block)
        leaving = scale * leaving + first_block * grad_s[1, packed_rows(pr), :]
        z_leaving = scale * z_leaving + first_block * grad_z[1, pl.ds(pr, 1), :]
        square = two(leaving).astype(BF16)
        k, v = feat[1, rows, cols], val[rows, cols]
        tail = seg_col[b] == seg_col[b, pl.ds(255, 1), :]
        kgrad = key_acc[rows, cols] + jnp.where(tail, mm(v, square, "NT") + z_leaving, 0.0)
        low_grads[1, rows, cols] = (kgrad * jnp.minimum(k.astype(F32), 1.0)).astype(BF16)
        vgrad = val_acc[rows, cols] + jnp.where(tail, mm(k, square), 0.0)
        low_grads[2, rows, cols] = vgrad.astype(BF16)

    loop(8, leave, 2)

    u1.ring()
    def qkv_weight(i):
        work[...] = mm(low_grads[i], normed[...], "TN")
        for j in range(4):
            part[2, j // 2, j % 2, at128(i), :] = work[j * 128 : (j + 1) * 128, :].astype(BF16)

    loop(3, qkv_weight)
    qkv_rows = pl.ds(0, 384)
    core_a = [
        core_send(part.at[2, jy, 1 - hc, qkv_rows], buf_core.at[2, jy, qkv_rows])
        for jy in (1 - hy, hy)
    ]
    norm_grad[...] = mm(low_grads[0], w_qkv[0], "NT")
    core_a[0].wait_recv()
    add_core(2, 1 - hy, 0, 384)
    core_a[1].wait_recv()
    add_core(2, hy, 0, 384)
    u0.spread()
    a0.a()
    a1.a()
    o0.mid()
    d1.ring()
    a0.b()
    norm_grad[...] += mm(low_grads[1], w_qkv[1], "NT")
    a1.mid()
    u1.spread()
    norm_grad[...] += mm(low_grads[2], w_qkv[2], "NT")
    u0.back()
    a1.b()

    def sink_input(r, grad):
        ig_s[r, :] = grad.astype(BF16)

    norm_back(norm_grad, gain_one, unit_one, rstd_one, lambda r: middle_grad[r, :], sink_input, 0)

    def gain_start():
        copies = []
        for n, d in enumerate(COMBOS):
            par_to, y_to, c_to = peer(*d)
            copies.append(
                send(
                    gain_part.at[0, :, at128(2 * y_to + c_to)],
                    gain_buf.at[n],
                    address(par_to, y_to, c_to),
                )
            )
        return copies

    gain_base = take(pairs - 1)

    def gain_copy(d):
        return remote(gain_sum.at[0], gain_buf.at[6 + d], ring(d)[1], gain_base + d - 1)

    def gain_middle(copies):
        for copy in copies:
            copy.wait_recv()
        total = gain_part[0, :, hcol]
        for n in range(len(COMBOS)):
            total = total + gain_buf[n]
        gain_sum[0] = total
        each_ring(lambda d: gain_copy(d).start())

    def gain_end():
        each_ring(lambda d: gain_copy(d).wait_recv())
        gain_sum[1] = gain_sum[0]

        def add_gain(d):
            gain_sum[1] = gain_sum[1] + gain_buf[6 + d]

        each_ring(add_gain)
        gains[...] = gain_sum[1]

    o0.ring()
    a0.mid()
    ig_copies += scatter_out(ig_s, ig_out, COMBOS[:4])
    d1.spread()
    u1.back()
    ig_copies += scatter_out(ig_s, ig_out, COMBOS[4:])
    a1.ring()
    o0.spread()
    gain_copies = gain_start()
    ig_own = local(ig_s.at[half256, hcol], ig_out.at[member])
    a0.ring()
    d1.back()
    d0.ring()
    a1.spread()
    a0.spread()
    o0.back()
    gain_middle(gain_copies)
    d0.spread()
    lo_copies += scatter_out(lo_s, lo_out, COMBOS[:4])
    a1.back()
    d0.back()
    a0.back()
    gain_end()

    for chunk in chunks:
        chunk.end()
    for copy in lo_copies + ig_copies:
        copy.wait_recv()
    lo_own.wait()
    ig_own.wait()
    for copy in sends:
        copy.wait_send()
    for chunk in chunks:
        chunk.sent()
    each_ring(lambda d: gain_copy(d).wait_send())
    for d in (1, 2):

        @pl.when(pair + d < pairs)
        def _():
            for order in range(2):
                for copy in forward[order, d]:
                    copy.wait_send()

        @pl.when(pair >= d)
        def _():
            for copy in backward[d]:
                copy.wait_send()


def widen_kernel(lo, ig, fin, gains, *refs):
    lo_o, ig_o, q_o, k_o, v_o, o_o, u_o, d_o, g_o, f_o = refs[:10]
    ig_b, fin_b, lo_b, gains_b, ig_w, fin_w, qkv_w, g_w, f_w, sem_in, sem_out = refs[10:]
    parts = [(fin.at[2], fin_b.at[2], 2, 0)]
    for u in (0, 1):
        for half in range(2):
            rows = pl.ds(half * 256, 256)
            parts.append((fin.at[u, rows], fin_b.at[u, rows], u, half))
    for half in range(2):
        rows = pl.ds(half * 4, 4)
        parts.append((ig.at[rows], ig_b.at[rows], 3, half))
    parts.append((lo, lo_b, 4, 0))
    parts.append((gains, gains_b, 5, 0))
    arriving = [
        pltpu.make_async_copy(source, into, sem_in.at[n])
        for n, (source, into, _, _) in enumerate(parts)
    ]
    for copy in arriving:
        copy.start()
    leaving = []

    def leave(source, out):
        copy = pltpu.make_async_copy(source, out, sem_out.at[len(leaving)])
        copy.start()
        leaving.append(copy)

    for copy, (_, _, u, n) in zip(arriving, parts, strict=True):
        copy.wait()
        if u == 5:
            g_w[...] = gains_b[0]
            f_w[...] = gains_b[1]
            leave(g_w, g_o)
            leave(f_w, f_o)
        elif u == 4:
            leave(lo_b, lo_o)
        elif u == 3:
            rows = pl.ds(n * 4, 4)
            ig_w[rows] = ig_b[rows].astype(F32)
            leave(ig_w.at[rows], ig_o.at[rows])
        elif u < 2:
            rows = pl.ds(n * 256, 256)
            fin_w[u, rows] = fin_b[u, rows].astype(F32)
            leave(fin_w.at[u, rows], (d_o, u_o)[u].at[rows])
        else:
            for i, out in enumerate((q_o, k_o, v_o)):
                qkv_w[i] = fin_b[2, pl.ds(i * 128, 128)].astype(F32).T
                leave(qkv_w.at[i], out)
            fin_w[2, pl.ds(0, 128)] = fin_b[2, pl.ds(384, 128)].astype(F32)
            leave(fin_w.at[2, pl.ds(0, 128)], o_o)
    for copy in leaving:
        copy.wait()


def body(
    tokens,
    norm_gain,
    query_weight,
    key_weight,
    value_weight,
    attention_output_weight,
    feedforward_norm_gain,
    up_weight,
    down_weight,
    segment_ids,
    out_grad,
):
    batch, length, share = tokens.shape
    width, head_cols = query_weight.shape
    units = up_weight.shape[1]
    pairs = lax.axis_size("seq") // 2
    assert lax.axis_size("head") == 4 and batch == 8 and length == BLOCK
    assert (width, share, head_cols, units) == (512, 128, 128, 512)
    assert pairs >= OWNERS and pairs % 2 == 0
    others = pairs - 1
    anywhere = pl.BlockSpec(memory_space=pl.ANY)
    vmem = pl.BlockSpec(memory_space=pltpu.VMEM)
    passed = sum(chunk[6] for chunk in CHUNKS)
    copies = 7 * 4 + 1 + 7 * KINDS + 8 + 4 + 5 + len(CHUNKS) * (3 + 2 * others)
    copies += passed * (1 + others) + (len(CHUNKS) - passed) + 7 + others
    square = (512, 512)
    buffers = dict(
        xin=(square, BF16),
        ogs=(square, BF16),
        w_qkv=((3, 512, 512), BF16),
        w_o=(square, BF16),
        w_u=((4, 512, 512), BF16),
        w_d=((4, 512, 512), BF16),
        seg_other=((8, 256), jnp.int32),
        unit_one=(square, F32),
        unit_two=(square, F32),
        rstd_one=((512, 128), F32),
        rstd_two=((512, 128), F32),
        normed=(square, BF16),
        normed_two=(square, BF16),
        feat=((2, 512, 512), BF16),
        val=(square, BF16),
        mask=((2, 256, 256), F32),
        seg_col=((2, 256, 128), F32),
        carry_on=((2, 256, 128), F32),
        own_s=((2, 256, 128), F32),
        own_z=((2, 8, 128), F32),
        msg_s=((256, 128), BF16),
        msg_z=((2, 8, 128), F32),
        buf_s=((2, 256, 128), BF16),
        buf_z=((2, 2, 8, 128), F32),
        state=((8, 128, 256), BF16),
        scores_low=((8, 512, 256), BF16),
        attn=(square, BF16),
        attn_wide=(square, F32),
        den_inv=(square, F32),
        middle=(square, F32),
        work=(square, F32),
        work_two=(square, F32),
        hid=(square, BF16),
        hid_grad=(square, BF16),
        ffn=(square, F32),
        norm_grad=(square, F32),
        middle_grad=(square, F32),
        middle_low=(square, BF16),
        num_grad=(square, BF16),
        den_grad=(square, BF16),
        grad_s=((2, 256, 128), F32),
        grad_z=((2, 8, 128), F32),
        msg_gs=((256, 128), BF16),
        msg_gz=((8, 128), F32),
        buf_gs=((2, 256, 128), BF16),
        buf_gz=((2, 8, 128), F32),
        key_acc=(square, F32),
        val_acc=(square, F32),
        low_grads=((3, 512, 512), BF16),
        lo_s=(square, BF16),
        ig_s=(square, BF16),
        part=((3, 2, 2, 512, 512), BF16),
        buf_core=((3, 2, 512, 512), BF16),
        gain_part=((1, 8, 512), F32),
        gain_sum=((2, 8, 128), F32),
        gain_buf=((7 + others, 8, 128), F32),
    )
    shapes = list(buffers.values())
    for _, _, rows, _, lanes, _, _ in CHUNKS:
        piece = rows // 2 // OWNERS
        shapes.append(((3, rows // 2, lanes), BF16))
        shapes.append(((others, piece, lanes), BF16))
        shapes.append(((piece, lanes), BF16))
        shapes.append(((piece, lanes), BF16))
    scratch = [pltpu.VMEM(*spec) for spec in shapes]
    scratch += [
        pltpu.SemaphoreType.DMA((8 + 2 + len(CHUNKS) + passed,)),
        pltpu.SemaphoreType.DMA((copies,)),
        pltpu.SemaphoreType.DMA((copies,)),
    ]
    lo, ig, fin, gains = pl.pallas_call(
        functools.partial(layer_kernel, pairs, list(buffers)),
        out_shape=(
            jax.ShapeDtypeStruct((batch, length, share), BF16),
            jax.ShapeDtypeStruct((batch, length, share), BF16),
            jax.ShapeDtypeStruct((3, 512, 512), BF16),
            jax.ShapeDtypeStruct((8, 128), F32),
        ),
        in_specs=[anywhere] * 8 + [vmem] * 3,
        out_specs=(anywhere, anywhere, anywhere, vmem),
        scratch_shapes=scratch,
        compiler_params=pltpu.CompilerParams(
            collective_id=0, has_side_effects=True, vmem_limit_bytes=58 * MIB
        ),
        cost_estimate=pl.CostEstimate(
            flops=11 * 10**9, bytes_accessed=8 * MIB, transcendentals=4 * 10**6
        ),
        name="layer",
    )(
        tokens,
        out_grad,
        query_weight,
        key_weight,
        value_weight,
        attention_output_weight,
        up_weight,
        down_weight,
        segment_ids,
        norm_gain[None],
        feedforward_norm_gain[None],
    )

    lo, ig, q_w, k_w, v_w, o_w, u_w, d_w, g_one, g_two = pl.pallas_call(
        widen_kernel,
        out_shape=(
            jax.ShapeDtypeStruct((batch, length, share), BF16),
            jax.ShapeDtypeStruct((batch, length, share), F32),
            jax.ShapeDtypeStruct((512, 128), F32),
            jax.ShapeDtypeStruct((512, 128), F32),
            jax.ShapeDtypeStruct((512, 128), F32),
            jax.ShapeDtypeStruct((128, 512), F32),
            jax.ShapeDtypeStruct((512, 512), F32),
            jax.ShapeDtypeStruct((512, 512), F32),
            jax.ShapeDtypeStruct((128,), F32),
            jax.ShapeDtypeStruct((128,), F32),
        ),
        in_specs=[anywhere] * 4,
        out_specs=(anywhere,) * 10,
        scratch_shapes=[
            pltpu.VMEM((batch, length, share), BF16),
            pltpu.VMEM((3, 512, 512), BF16),
            pltpu.VMEM((batch, length, share), BF16),
            pltpu.VMEM((8, 128), F32),
            pltpu.VMEM((batch, length, share), F32),
            pltpu.VMEM((3, 512, 512), F32),
            pltpu.VMEM((3, 512, 128), F32),
            pltpu.VMEM((128,), F32),
            pltpu.VMEM((128,), F32),
            pltpu.SemaphoreType.DMA((9,)),
            pltpu.SemaphoreType.DMA((13,)),
        ],
        compiler_params=pltpu.CompilerParams(vmem_limit_bytes=58 * MIB),
        name="widen",
    )(lo, ig, fin, gains)
    return (lo, ig, g_one, q_w, k_w, v_w, o_w, g_two, u_w, d_w)


def solution(mesh):
    in_specs = (
        P(None, "seq", "head"),
        P(),
        P(None, "head"),
        P(None, "head"),
        P(None, "head"),
        P("head", None),
        P(),
        P(None, "head"),
        P("head", None),
        P(None, "seq"),
        P(None, "seq", "head"),
    )
    out_specs = (
        P(None, "seq", "head"),
        P(None, "seq", "head"),
        P("head"),
        P(None, "head"),
        P(None, "head"),
        P(None, "head"),
        P("head", None),
        P("head"),
        P(None, "head"),
        P("head", None),
    )
    return jax.shard_map(body, mesh=mesh, in_specs=in_specs, out_specs=out_specs, check_vma=False)
```

```python
import functools
from types import SimpleNamespace

import jax
import jax.numpy as jnp
from jax import lax
from jax.experimental import pallas as pl
from jax.experimental.pallas import tpu as pltpu
from jax.sharding import PartitionSpec as P

DH = 64
BLOCK = 256
EPSILON = 1e-05
MESH = pl.DeviceIdType.MESH
F32 = jnp.float32
BF16 = jnp.bfloat16
MIB = 1 << 20
KINDS = 4
OWNERS = 4
CHUNKS = (
    (0, 0, 512, 0, 256, True, True),
    (0, 0, 512, 256, 256, True, False),
    (1, 0, 512, 0, 256, False, False),
    (1, 0, 512, 256, 256, False, False),
    (2, 384, 128, 0, 512, False, False),
    (2, 0, 384, 0, 256, False, False),
    (2, 0, 384, 256, 256, True, False),
)
COMBOS = ((0, 1, 0), (0, 1, 1), (1, 1, 0), (1, 1, 1), (1, 0, 0), (1, 0, 1), (0, 0, 1))


def mm(left, right, form="NN"):
    dims = {"NN": ((1,), (0,)), "NT": ((1,), (1,)), "TN": ((0,), (0,))}[form]
    return lax.dot_general(left, right, (dims, ((), ())), preferred_element_type=F32)


def loop(count, step, unroll=1):
    def run(i, carry):
        step(i)
        return carry

    lax.fori_loop(0, count, run, 0, unroll=unroll)


def span(start, size, multiple=None):
    return pl.ds(pl.multiple_of(start, multiple or size), size)


def rows_loop(total, chunk, step):
    loop(total // chunk, lambda i: step(span(i * chunk, chunk)))


def at128(i):
    return span(i * 128, 128)


def layer_kernel(pairs, names, *refs):
    (tok, og_in, wq, wk, wv, wo, wu, wd, seg, gain_one, gain_two) = refs[:11]
    (lo_out, ig_out, fin, gains) = refs[11:15]
    r_ = SimpleNamespace(**dict(zip(names, refs[15:])))
    chunk_refs = refs[15 + len(names) : -3]
    local_sem, send_sem, recv_sem = refs[-3:]
    xin, ogs, w_qkv, w_o, w_u = (
        r_.xin, r_.ogs, r_.w_qkv, r_.w_o, r_.w_u,
    )
    w_d, unit_one, unit_two, rstd_one, rstd_two = (
        r_.w_d, r_.unit_one, r_.unit_two, r_.rstd_one, r_.rstd_two,
    )
    normed, normed_two, feat, val, mask = (
        r_.normed, r_.normed_two, r_.feat, r_.val, r_.mask,
    )
    seg_col, carry_on, state, scores_low, own_s = (
        r_.seg_col, r_.carry_on, r_.state, r_.scores_low, r_.own_s,
    )
    own_z, msg_s, msg_z, buf_s, buf_z = (
        r_.own_z, r_.msg_s, r_.msg_z, r_.buf_s, r_.buf_z,
    )
    grad_s, grad_z, msg_gs, msg_gz, buf_gs = (
        r_.grad_s, r_.grad_z, r_.msg_gs, r_.msg_gz, r_.buf_gs,
    )
    buf_gz, attn, attn_wide, den_inv, middle = (
        r_.buf_gz, r_.attn, r_.attn_wide, r_.den_inv, r_.middle,
    )
    work, work_two, hid, hid_grad, ffn = (
        r_.work, r_.work_two, r_.hid, r_.hid_grad, r_.ffn,
    )
    norm_grad, middle_grad, middle_low, num_grad, den_grad = (
        r_.norm_grad, r_.middle_grad, r_.middle_low, r_.num_grad, r_.den_grad,
    )
    key_acc, val_acc, low_grads, lo_s, ig_s = (
        r_.key_acc, r_.val_acc, r_.low_grads, r_.lo_s, r_.ig_s,
    )
    gain_sum = r_.gain_sum
    part, buf_core, gain_part, gain_buf, seg_other = (
        r_.part, r_.buf_core, r_.gain_part, r_.gain_buf, r_.seg_other,
    )

    s = lax.axis_index("seq")
    h = lax.axis_index("head")
    pair, par = lax.div(s, 2), lax.rem(s, 2)
    hy, hc = lax.div(h, 2), lax.rem(h, 2)
    member = par * 4 + h
    zb = lax.rem(pair, 2)

    counter = [0]
    sends = []
    local_ids = iter(range(1000))

    def take(n=1):
        counter[0] += n
        return counter[0] - n

    def guarded(cond, act):
        if cond is None:
            act()
        else:
            pl.when(cond)(act)

    def peer(dp, dy, dc):
        return (1 - par if dp else par, 1 - hy if dy else hy, 1 - hc if dc else hc)

    def address(par_to, y_to, c_to):
        return (2 * pair + par_to, 2 * y_to + c_to)

    core, ypeer, xpeer = (address(*peer(*d)) for d in ((0, 0, 1), (0, 1, 0), (1, 0, 0)))
    zpeer = (2 * (pair + 1 - 2 * zb) + par, h)

    def ring(d):
        to = lax.rem(pair + d, pairs)
        return to, (2 * to + par, h)

    def remote(src, dst, device, i=None):
        i = take() if i is None else i
        return pltpu.make_async_remote_copy(
            src_ref=src,
            dst_ref=dst,
            send_sem=send_sem.at[i],
            recv_sem=recv_sem.at[i],
            device_id=device,
            device_id_type=MESH,
        )

    def start(copy):
        copy.start()
        sends.append(copy)
        return copy

    def send(src, dst, device):
        return start(remote(src, dst, device))

    def local(src, dst):
        copy = pltpu.make_async_copy(src, dst, local_sem.at[next(local_ids)])
        copy.start()
        return copy

    def each_ring(act):
        if pairs <= 4:
            for d in range(1, pairs):
                act(d)
        else:
            loop(pairs - 1, lambda i: act(i + 1))

    hcol = at128(h)
    half256 = span(par * 256, 256)
    own_w = [
        [local(w, w_qkv.at[i, :, hcol]) for i, w in enumerate((wq, wk, wv))],
        [local(wo, w_o.at[hcol])],
        [local(wu, w_u.at[h])],
        [local(wd, w_d.at[h])],
    ]
    own_tok = local(tok.at[member], xin.at[half256, hcol])
    own_og = local(og_in.at[member], ogs.at[half256, hcol])
    row8 = lax.broadcasted_iota(jnp.int32, (8, 128), 0)
    neutral = jnp.where(row8 == 4, -1.0, 0.0).astype(F32)
    for slot in range(2):
        buf_s[slot] = jnp.zeros((256, 128), BF16)
        buf_gs[slot] = jnp.zeros((256, 128), BF16)
        buf_gz[slot] = jnp.zeros((8, 128), F32)
        for order in range(2):
            buf_z[slot, order] = neutral

    barrier = pltpu.get_barrier_semaphore()
    for d in COMBOS:
        pl.semaphore_signal(barrier, inc=1, device_id=address(*peer(*d)), device_id_type=MESH)
    each_ring(
        lambda d: pl.semaphore_signal(
            barrier, inc=1, device_id=ring(d)[1], device_id_type=MESH
        )
    )
    pl.semaphore_wait(barrier, len(COMBOS) + pairs - 1)

    class Exchange:
        def __init__(self, src, dst, seven):
            self.src, self.dst, self.seven, self.i = src, dst, seven, take()

        def go(self, combos):
            for d in combos:
                par_to, y_to, c_to = peer(*d)
                to = address(par_to, y_to, c_to)
                remote(*self.views(par_to, y_to, c_to), to, self.i).start()

        def all(self):
            return remote(self.seven, self.seven, core, self.i)

    class Inward(Exchange):
        def views(self, par_to, y_to, c_to):
            return self.src.at[par_to * 4 + 2 * y_to + c_to], self.dst.at[half256, hcol]

    class Outward(Exchange):
        def views(self, par_to, y_to, c_to):
            rows, cols = span(par_to * 256, 256), at128(2 * y_to + c_to)
            return self.src.at[rows, cols], self.dst.at[member]

    tok_move = Inward(tok, xin, xin.at[pl.ds(0, 448)])
    og_move = Inward(og_in, ogs, ogs.at[pl.ds(0, 448)])
    lo_move = Outward(lo_s, lo_out, lo_s.at[pl.ds(0, 448)])
    ig_move = Outward(ig_s, ig_out, ig_s.at[pl.ds(0, 448)])

    across = 2 * (1 - hy) + hc
    quarter = par + 2 * zb
    quarter_x = 1 - par + 2 * zb

    def view(kind, shard, eighth=None, eighths=2):
        rows = 32 if kind == 1 else 128
        unit = rows // 2
        if kind == 0:
            where = slice(None) if eighth is None else span(eighth * unit, unit * eighths, unit)
            return w_qkv.at[:, where, at128(shard)]
        if kind == 1:
            if eighth is None:
                return w_o.at[at128(shard)]
            return w_o.at[span(shard * 128 + eighth * unit, unit * eighths, unit)]
        ref = w_u if kind == 2 else w_d
        if eighth is None:
            return ref.at[shard]
        return ref.at[shard, span(eighth * unit, unit * eighths, unit)]

    wt = {}

    def pass_on_weight(kind, eighth, eighths, device, shard=None):
        ref = view(kind, across if shard is None else shard, eighth, eighths)
        return send(ref, ref, device)

    def weight_y(kind):
        wt[kind, "y"] = pass_on_weight(kind, 2 * quarter, 2, ypeer, h)

    def weight_core(kind):
        own = view(kind, h)
        wt[kind, "own"] = send(own, own, core)
        wt[kind, "c"] = []

    def weight_near(kind):
        wt[kind, "y"].wait_recv()
        wt[kind, "x"] = pass_on_weight(kind, 2 * quarter, 2, xpeer)
        wt[kind, "z"] = pass_on_weight(kind, 2 * quarter, 2, zpeer)

    def weight_far(kind):
        wt[kind, "x"].wait_recv()
        wt[kind, "far"] = pass_on_weight(kind, 2 * quarter_x, 2, zpeer)
        wt[kind, "c"].append(pass_on_weight(kind, 4 * zb, 4, core))

    def weight_last(kind):
        wt[kind, "z"].wait_recv()
        wt[kind, "far"].wait_recv()
        wt[kind, "c"].append(pass_on_weight(kind, 4 * (1 - zb), 4, core))

    def weight_own(kind):
        wt[kind, "own"].wait_recv()

    def weight_ready(kind):
        for copy in wt[kind, "c"]:
            copy.wait_recv()

    for copies in own_w:
        for copy in copies:
            copy.wait()
    seg_copy = send(seg, seg_other, xpeer)
    weight_y(0)
    tok_move.go(COMBOS[0:2])
    tok_move.go(COMBOS[2:4])
    tok_move.go(COMBOS[4:])
    weight_core(0)
    weight_y(1)
    weight_y(2)
    weight_y(3)
    weight_core(1)
    weight_core(2)
    weight_core(3)
    weight_near(0)
    og_move.go(COMBOS[0:2])
    og_move.go(COMBOS[2:4])
    og_move.go(COMBOS[4:])
    tok_move.all().wait_recv()
    own_tok.wait()

    def norm_rows(source, gain, unit_ref, rstd_ref, out_ref):
        def step(r):
            x = source(r)
            center = x - jnp.mean(x, axis=-1, keepdims=True)
            scale = lax.rsqrt(jnp.mean(center * center, axis=-1, keepdims=True) + EPSILON)
            unit = center * scale
            unit_ref[r, :] = unit
            rstd_ref[r, :] = jnp.broadcast_to(scale, (unit.shape[0], 128))
            out_ref[r, :] = (unit * gain[...]).astype(BF16)

        rows_loop(512, 64, step)

    norm_rows(lambda r: xin[r, :].astype(F32), gain_one, unit_one, rstd_one, normed)

    weight_far(0)
    seg_copy.wait_recv()
    own_row = seg[pl.ds(member, 1), :]
    other_row = seg_other[pl.ds(member, 1), :]
    seg_rows = (
        (own_row * (1 - par) + other_row * par).astype(F32),
        (own_row * par + other_row * (1 - par)).astype(F32),
    )
    first = lax.broadcasted_iota(jnp.int32, (256, 256), 0)
    second = lax.broadcasted_iota(jnp.int32, (256, 256), 1)
    for b in range(2):
        along = jnp.broadcast_to(seg_rows[b], (256, 256))
        down = along.T
        mask[b] = jnp.where((along == down) & (second <= first), 1.0, 0.0)
        seg_col[b] = down[:, :128]
    weight_own(0)
    lane = lax.broadcasted_iota(jnp.int32, (1, 128), 1)
    low_lanes = lane < 64
    spread = (
        lax.broadcasted_iota(jnp.int32, (128, 128), 0) // 64
        == lax.broadcasted_iota(jnp.int32, (128, 128), 1) // 64
    )

    def place(i):
        b, pr = lax.div(i, 4), lax.rem(i, 4)
        return b, pr, span(b * 256, 256), at128(pr)

    def side_place(i, side):
        return place(lax.div(i, 2) * 4 + 2 * side + lax.rem(i, 2))

    def pack(square):
        return jnp.where(low_lanes, square[:64], square[64:])

    def two(rows):
        zero = jnp.zeros_like(rows)
        return jnp.concatenate(
            [jnp.where(low_lanes, rows, zero), jnp.where(low_lanes, zero, rows)], axis=0
        )

    def pick(stacked):
        return jnp.where(low_lanes, stacked[:256], stacked[256:])

    def packed_rows(pr):
        return span(pr * 64, 64)

    last_rows = [seg_col[b, pl.ds(255, 1), :] for b in range(2)]
    keep_mid = jnp.where(last_rows[0] >= last_rows[1], 1.0, 0.0)

    def project(side):
        cols = span(side * 256, 256)

        def step_kind(i):
            work[:, :256] = mm(normed[...], w_qkv[i, :, cols])

            def step(r):
                v = work[r, :256]
                feat[i, r, cols] = jnp.where(
                    v > 0, v + 1.0, jnp.exp(jnp.minimum(v, 0.0))
                ).astype(BF16)

            rows_loop(512, 64, step)

        loop(2, step_kind)
        val[:, cols] = mm(normed[...], w_qkv[2, :, cols]).astype(BF16)

    def own_state(i, side):
        b, pr, rows, cols = side_place(i, side)
        tail = seg_col[b] == seg_col[b, pl.ds(255, 1), :]
        keys = feat[1, rows, cols].astype(F32)
        keys = jnp.where(tail, keys, 0.0)
        own_s[b, packed_rows(pr), :] = pack(mm(keys.astype(BF16), val[rows, cols], "TN"))
        own_z[b, pl.ds(pr, 1), :] = jnp.sum(keys, axis=0, keepdims=True)

    def shift(d, pieces, base):
        to = lax.rem(pair + d + pairs, pairs)
        device = (2 * to + par, h)
        return [remote(src, dst, device, base + i) for i, (src, dst) in enumerate(pieces)]

    forward = {}

    def make_state(order, side):
        loop(4, lambda i: own_state(i, side), 2)
        rows = span(side * 128, 128)
        msg_s[rows, :] = (own_s[1, rows, :] + keep_mid * own_s[0, rows, :]).astype(BF16)
        msg_z[order] = jnp.where(row8 == 4, last_rows[1], own_z[1] + keep_mid * own_z[0])

    def send_state(order, side):
        rows = span(side * 128, 128)
        for d in (1, 2):
            copies = shift(
                d,
                [
                    (msg_s.at[rows], buf_s.at[d - 1, rows]),
                    (msg_z.at[order], buf_z.at[d - 1, order]),
                ],
                take(2),
            )
            forward[order, d] = copies

            @pl.when(pair + d < pairs)
            def _():
                for copy in copies:
                    copy.start()

    own_z[...] = jnp.zeros_like(own_z)
    project(hy)
    make_state(0, hy)
    send_state(0, hy)
    weight_near(1)
    weight_last(0)
    weight_near(2)
    weight_ready(0)
    project(1 - hy)
    make_state(1, 1 - hy)
    send_state(1, 1 - hy)
    weight_far(1)
    weight_near(3)

    ones = jnp.ones((256, 128), BF16)
    ready = {}

    def receive_state(order):
        for d in (1, 2):

            @pl.when(pair >= d)
            def _():
                for copy in forward[order, d]:
                    copy.wait_recv()

        if order == 0:
            last_in = buf_z[0, 0, pl.ds(4, 1), :]
            ready["keep_in"] = jnp.where(buf_z[1, 0, pl.ds(4, 1), :] >= last_in, 1.0, 0.0)
            ready["keep_first"] = jnp.where(last_in >= last_rows[0], 1.0, 0.0)
            carry_on[0] = jnp.where(seg_col[0] == last_in, 1.0, 0.0)
            carry_on[1] = jnp.where(seg_col[1] == last_rows[0], 1.0, 0.0)
        buf_z[0, order] = buf_z[0, order] + ready["keep_in"] * buf_z[1, order]

    def enter(order, side):
        def step(i):
            pr = 2 * side + i
            entering = buf_s[0, packed_rows(pr), :].astype(F32) + ready["keep_in"] * buf_s[
                1, packed_rows(pr), :
            ].astype(F32)
            z_in = buf_z[0, order, pl.ds(pr, 1), :]
            middle_s = own_s[0, packed_rows(pr), :] + ready["keep_first"] * entering
            middle_z = own_z[0, pl.ds(pr, 1), :] + ready["keep_first"] * z_in
            for b, (packed, z_row) in enumerate(((entering, z_in), (middle_s, middle_z))):
                wide = jnp.where(spread, jnp.broadcast_to(z_row, (128, 128)).T, 0.0)
                state[b * 4 + pr, :, :128] = two(packed).astype(BF16)
                state[b * 4 + pr, :, 128:] = wide.astype(BF16)

        loop(2, step)

    def attend(i, side):
        b, pr, rows, cols = side_place(i, side)
        q, k, v = feat[0, rows, cols], feat[1, rows, cols], val[rows, cols]
        scores = mm(two(q), k, "NT")
        m = mask[b]
        low = jnp.concatenate([scores[:256] * m, scores[256:] * m], axis=0).astype(BF16)
        scores_low[b * 4 + pr] = low
        both = mm(low, jnp.concatenate([v, ones], axis=1))
        carried = mm(q, state[b * 4 + pr])
        c = carry_on[b]
        numer = pick(both[:, :128]) + c * carried[:, :128]
        denom = pick(both[:, 128:]) + c * carried[:, 128:]
        inverse = 1.0 / denom
        result = numer * inverse
        den_inv[rows, cols] = inverse
        attn_wide[rows, cols] = result
        attn[rows, cols] = result.astype(BF16)

    receive_state(0)
    enter(0, hy)
    loop(4, lambda i: attend(i, hy), 2)
    weight_far(2)
    receive_state(1)
    enter(1, 1 - hy)
    weight_last(1)
    loop(4, lambda i: attend(i, 1 - hy), 2)
    keep_first = ready["keep_first"]
    weight_own(1)
    weight_ready(1)
    weight_far(3)
    work[...] = mm(attn[...], w_o[...])

    def mid_step(r):
        middle[r, :] = xin[r, :].astype(F32) + work[r, :]

    rows_loop(512, 64, mid_step)
    norm_rows(
        lambda r: middle[r, :].astype(BF16).astype(F32), gain_two, unit_two, rstd_two, normed_two
    )
    og_move.all().wait_recv()
    own_og.wait()
    weight_own(2)
    weight_own(3)

    def core_send(view_src, view_dst):
        return send(view_src, view_dst, core)

    def add_core(u, jy, row, rows):
        def step(i):
            r = span(row + i * 64, 64)
            part[u, jy, hc, r, :] = (
                part[u, jy, hc, r, :].astype(F32) + buf_core[u, jy, r, :].astype(F32)
            ).astype(BF16)

        loop(rows // 64, step)

    owner = None if pairs == OWNERS else pair < OWNERS
    apart = 0 if pairs == OWNERS else 1
    in_ring = pairs - 1 if apart else 1

    class Chunk:
        def __init__(self, n):
            self.u, self.row, self.rows, self.lane, self.lanes = CHUNKS[n][:5]
            self.y_first, self.x_then_z = CHUNKS[n][5:]
            self.half = self.rows // 2
            self.piece = self.half // OWNERS
            self.buf, self.ring_buf, self.own, self.own_x = chunk_refs[4 * n : 4 * n + 4]
            self.cols = pl.ds(self.lane, self.lanes)
            self.devices = (ypeer, xpeer) if self.y_first else (xpeer, ypeer)
            self.ring_base = self.spread_base = None

        def rows_of(self, half, at=0, size=None):
            return span(self.row + half * self.half + at, size or self.half, 16)

        def at(self, jy, half):
            return part.at[self.u, jy, hc, self.rows_of(half), self.cols]

        def a(self):
            self.first = send(self.at(1 - hy, 1 - par), self.buf.at[0], self.devices[0])

        def b(self):
            source = (1 - hy, par) if self.y_first else (hy, 1 - par)
            self.other = send(self.at(*source), self.buf.at[1], self.devices[0])

        def mid(self):
            self.first.wait_recv()
            jy, half = (hy, 1 - par) if self.y_first else (1 - hy, par)

            def step(i):
                r = self.rows_of(half, i * self.piece, self.piece)
                got = self.buf[0, span(i * self.piece, self.piece), :].astype(F32)
                part[self.u, jy, hc, r, self.cols] = (
                    part[self.u, jy, hc, r, self.cols].astype(F32) + got
                ).astype(BF16)

            loop(OWNERS, step)
            self.second = send(self.at(jy, half), self.buf.at[2], self.devices[1])

        def ring_copy(self, d):
            to, device = ring(d)
            rows = self.rows_of(par, lax.rem(to, OWNERS) * self.piece, self.piece)
            copy = remote(
                part.at[self.u, hy, hc, rows, self.cols],
                self.ring_buf.at[d - 1],
                device,
                self.ring_base + apart * (d - 1),
            )
            return copy, None if pairs == OWNERS else to < OWNERS

        def ring(self):
            self.other.wait_recv()
            self.second.wait_recv()

            def step(i):
                r = self.rows_of(par, i * self.piece, self.piece)
                b = span(i * self.piece, self.piece)
                got = self.buf[1, b, :].astype(F32) + self.buf[2, b, :].astype(F32)
                part[self.u, hy, hc, r, self.cols] = (
                    part[self.u, hy, hc, r, self.cols].astype(F32) + got
                ).astype(BF16)

            loop(OWNERS, step)
            self.ring_base = take(in_ring)

            def go(d):
                copy, cond = self.ring_copy(d)
                guarded(cond, copy.start)

            each_ring(go)

        def final(self, index, half=par):
            rows = self.rows_of(half, lax.rem(index, OWNERS) * self.piece, self.piece)
            return fin.at[self.u, rows, self.cols]

        def spread_copy(self, d):
            return remote(
                self.own, self.final(pair), ring(d)[1], self.spread_base + apart * (d - 1)
            )

        def spread(self):
            self.spread_base = take(in_ring)
            sem = local_sem.at[next(local_ids)]
            self.kept = pltpu.make_async_copy(self.own, self.final(pair), sem)
            if self.x_then_z:
                self.across = remote(self.own, self.own_x, xpeer)
                self.spread_x_base = take(in_ring)
                sem = local_sem.at[next(local_ids)]
                self.kept_x = pltpu.make_async_copy(self.own_x, self.final(pair, 1 - par), sem)

            def total():
                self.each(self.ring_base, lambda d: self.ring_copy(d)[0].wait_recv(), True)
                rows = self.rows_of(par, lax.rem(pair, OWNERS) * self.piece, self.piece)
                self.own[...] = part[self.u, hy, hc, rows, self.cols]

                def more(d):
                    self.own[...] = (
                        self.own[...].astype(F32) + self.ring_buf[d - 1].astype(F32)
                    ).astype(BF16)

                if pairs == OWNERS:
                    value = part[self.u, hy, hc, rows, self.cols].astype(F32)
                    for d in range(1, pairs):
                        value = value + self.ring_buf[d - 1].astype(F32)
                    self.own[...] = value.astype(BF16)
                else:
                    each_ring(more)
                if self.x_then_z:
                    self.across.start()
                each_ring(lambda d: self.spread_copy(d).start())
                self.kept.start()

            guarded(owner, total)

        def spread_x_copy(self, d):
            return remote(
                self.own_x,
                self.final(pair, 1 - par),
                ring(d)[1],
                self.spread_x_base + apart * (d - 1),
            )

        def each(self, base, act, arriving):
            if apart:
                each_ring(act)
                return
            together = remote(self.ring_buf, self.ring_buf, xpeer, base)
            (together.wait_recv if arriving else together.wait_send)()

        def arrived(self, base, copy_of):
            def one(d):
                giver = lax.rem(pair - d + pairs, pairs)
                guarded(giver < OWNERS, copy_of(d).wait_recv)

            self.each(base, one, True)

        def back(self):
            if self.x_then_z:

                def pass_on():
                    self.across.wait_recv()
                    each_ring(lambda d: self.spread_x_copy(d).start())
                    self.kept_x.start()

                guarded(owner, pass_on)
                return
            self.arrived(self.spread_base, self.spread_copy)
            guarded(owner, self.kept.wait)
            rows = fin.at[self.u, self.rows_of(par), self.cols]
            self.last = send(rows, rows, xpeer)

        def end(self):
            if self.x_then_z:
                self.arrived(self.spread_base, self.spread_copy)
                self.arrived(self.spread_x_base, self.spread_x_copy)
                guarded(owner, self.kept.wait)
                guarded(owner, self.kept_x.wait)
            else:
                self.last.wait_recv()

        def sent(self):
            def one(d):
                copy, cond = self.ring_copy(d)
                guarded(cond, copy.wait_send)

            def spread_sent():
                self.each(self.spread_base, lambda d: self.spread_copy(d).wait_send(), False)
                if self.x_then_z:
                    self.across.wait_send()
                    self.each(
                        self.spread_x_base, lambda d: self.spread_x_copy(d).wait_send(), False
                    )

            self.each(self.ring_base, one, False)
            guarded(owner, spread_sent)

    d0, d1, u0, u1, o0, a0, a1 = chunks = [Chunk(n) for n in range(len(CHUNKS))]

    def zero_rows(r):
        ffn[r, :] = jnp.zeros((64, 512), F32)
        norm_grad[r, :] = jnp.zeros((64, 512), F32)

    rows_loop(512, 64, zero_rows)

    def feed(jc, jy):
        j = 2 * jy + jc
        work[...] = mm(normed_two[...], w_u[j])
        work_two[...] = mm(ogs[...], w_d[j], "NT")

        def step(r):
            v = work[r, :]
            sigma = 1.0 / (1.0 + jnp.exp(-v))
            hid[r, :] = (v * sigma).astype(BF16)
            hid_grad[r, :] = (work_two[r, :] * (sigma * (1.0 + v * (1.0 - sigma)))).astype(BF16)

        rows_loop(512, 64, step)
        part[0, jy, jc] = mm(hid[...], ogs[...], "TN").astype(BF16)
        part[1, jy, jc] = mm(normed_two[...], hid_grad[...], "TN").astype(BF16)

    def feed_on(jc, jy):
        j = 2 * jy + jc
        ffn[...] += mm(hid[...], w_d[j])
        norm_grad[...] += mm(hid_grad[...], w_u[j], "NT")

    def core_feed(jy):
        return core_send(part.at[0:2, jy, 1 - hc], buf_core.at[0:2, jy])

    def core_fed(copy, jy):
        copy.wait_recv()
        add_core(0, jy, 0, 512)
        add_core(1, jy, 0, 512)

    feed(1 - hc, hy)
    core_f = core_feed(hy)
    feed_on(1 - hc, hy)
    feed(hc, hy)
    core_fed(core_f, hy)
    weight_last(2)
    weight_last(3)
    u0.b()
    feed_on(hc, hy)
    weight_ready(2)
    weight_ready(3)
    u1.b()
    feed(1 - hc, 1 - hy)
    core_f = core_feed(1 - hy)
    feed_on(1 - hc, 1 - hy)
    feed(hc, 1 - hy)
    core_fed(core_f, 1 - hy)
    u0.a()
    d1.a()
    feed_on(hc, 1 - hy)

    gain_part[0] = jnp.zeros((8, 512), F32)
    row_512 = lax.broadcasted_iota(jnp.int32, (8, 512), 0)

    def norm_back(grad_ref, gain, unit_ref, rstd_ref, base, sink, row):
        def step(r):
            grad = grad_ref[r, :]
            unit = unit_ref[r, :]
            scaled = grad * gain[...]
            mean_one = jnp.mean(scaled, axis=-1, keepdims=True)
            mean_two = jnp.mean(scaled * unit, axis=-1, keepdims=True)
            rstd = rstd_ref[r, :]
            rstd = jnp.concatenate([rstd] * 4, axis=1)
            sink(r, base(r) + rstd * (scaled - mean_one - unit * mean_two))
            total = jnp.sum(grad * unit, axis=0, keepdims=True)
            gain_part[0] = gain_part[0] + jnp.where(row_512 == row, total, 0.0)

        rows_loop(512, 64, step)

    def sink_middle(r, grad):
        middle_grad[r, :] = grad
        middle_low[r, :] = grad.astype(BF16)
        lo_s[r, :] = (middle[r, :] + ffn[r, :]).astype(BF16)

    norm_back(
        norm_grad, gain_two, unit_two, rstd_two, lambda r: ogs[r, :].astype(F32), sink_middle, 1
    )

    d0.a()
    lo_own = local(lo_s.at[half256, hcol], lo_out.at[member])
    out_rows = pl.ds(384, 128)
    work_two[...] = mm(attn[...], middle_low[...], "TN")
    for j in range(4):
        part[2, j // 2, j % 2, out_rows, :] = work_two[j * 128 : (j + 1) * 128, :].astype(BF16)
    core_o = core_send(part.at[2, :, 1 - hc, out_rows], buf_core.at[2, :, out_rows])
    work[...] = mm(middle_low[...], w_o[...], "NT")

    u1.a()
    head_ones = jnp.where(spread, 1.0, 0.0).astype(BF16)
    head_ones = jnp.concatenate([head_ones, head_ones], axis=0)
    first_lane = lax.rem(lane, 64) == 0
    second_lane = lax.rem(lane, 64) == 1

    def split(wide):
        high = wide.astype(BF16)
        return high, (wide - high.astype(F32)).astype(BF16)

    grad_z[...] = jnp.zeros_like(grad_z)

    def outer(i):
        b, pr, rows, cols = place(i)
        grad, inverse = work[rows, cols], den_inv[rows, cols]
        gnum = (grad * inverse).astype(BF16)
        high, low = split(grad * attn_wide[rows, cols])
        gden = -mm(jnp.concatenate([high, low], axis=1), head_ones) * inverse
        dhigh = gden.astype(BF16).astype(F32)
        num_grad[rows, cols] = gnum
        den_grad[rows, cols] = jnp.where(
            first_lane, dhigh, jnp.where(second_lane, gden - dhigh, 0.0)
        ).astype(BF16)
        queries = feat[0, rows, cols].astype(F32) * carry_on[b]
        grad_s[b, packed_rows(pr), :] = pack(mm(queries.astype(BF16), gnum, "TN"))
        grad_z[b, pl.ds(pr, 1), :] = jnp.sum(queries * gden, axis=0, keepdims=True)

    loop(8, outer, 2)
    lo_move.go(COMBOS[4:])
    msg_gs[...] = (grad_s[0] + keep_first * grad_s[1]).astype(BF16)
    msg_gz[...] = jnp.where(row8 == 4, keep_first * keep_mid, grad_z[0] + keep_first * grad_z[1])
    backward = {}
    for d in (1, 2):
        pieces = [(msg_gs, buf_gs.at[d - 1]), (msg_gz, buf_gz.at[d - 1])]
        backward[d] = shift(-d, pieces, take(2))

        @pl.when(pair >= d)
        def _():
            for copy in backward[d]:
                copy.start()

    d1.mid()
    u0.mid()

    marks = jnp.where(first_lane | second_lane, 1.0, 0.0).astype(BF16)
    marks = jnp.broadcast_to(marks, (256, 128))

    def inner(i):
        b, pr, rows, cols = place(i)
        q, k, v = feat[0, rows, cols], feat[1, rows, cols], val[rows, cols]
        gnum, gden = num_grad[rows, cols], den_grad[rows, cols]
        gnum_two = two(gnum)
        grads = jnp.concatenate([gnum_two, two(gden)], axis=1)
        values = jnp.concatenate([v, marks], axis=1)
        m = mask[b]
        gsc = mm(grads, values, "NT")
        gsc = jnp.concatenate([gsc[:256] * m, gsc[256:] * m], axis=0).astype(BF16)
        qgrad = pick(mm(gsc, k)) + carry_on[b] * mm(
            jnp.concatenate([gnum, gden], axis=1), state[i], "NT"
        )
        low_grads[0, rows, cols] = (qgrad * jnp.minimum(q.astype(F32), 1.0)).astype(BF16)
        key_acc[rows, cols] = mm(gsc, two(q), "TN")
        val_acc[rows, cols] = mm(scores_low[i], gnum_two, "TN")

    loop(4, inner, 2)
    core_o.wait_recv()
    add_core(2, 0, 384, 128)
    add_core(2, 1, 384, 128)
    u1.mid()
    d0.b()
    d1.b()
    loop(4, lambda i: inner(4 + i), 2)

    u0.ring()
    o0.a()
    d0.mid()
    o0.b()
    for d in (1, 2):

        @pl.when(pair + d < pairs)
        def _():
            for copy in backward[d]:
                copy.wait_recv()

    pass_on = buf_gz[0, pl.ds(4, 1), :]
    buf_gz[0] = buf_gz[0] + pass_on * buf_gz[1]

    def leave(i):
        b, pr, rows, cols = place(i)
        leaving = buf_gs[0, packed_rows(pr), :].astype(F32) + pass_on * buf_gs[
            1, packed_rows(pr), :
        ].astype(F32)
        z_leaving = buf_gz[0, pl.ds(pr, 1), :]
        first_block = (1 - b).astype(F32)
        scale = first_block * keep_mid + (1.0 - first_block)
        leaving = scale * leaving + first_block * grad_s[1, packed_rows(pr), :]
        z_leaving = scale * z_leaving + first_block * grad_z[1, pl.ds(pr, 1), :]
        square = two(leaving).astype(BF16)
        k, v = feat[1, rows, cols], val[rows, cols]
        tail = seg_col[b] == seg_col[b, pl.ds(255, 1), :]
        kgrad = key_acc[rows, cols] + jnp.where(tail, mm(v, square, "NT") + z_leaving, 0.0)
        low_grads[1, rows, cols] = (kgrad * jnp.minimum(k.astype(F32), 1.0)).astype(BF16)
        vgrad = val_acc[rows, cols] + jnp.where(tail, mm(k, square), 0.0)
        low_grads[2, rows, cols] = vgrad.astype(BF16)

    loop(8, leave, 2)

    u1.ring()
    def qkv_weight(i):
        work[...] = mm(low_grads[i], normed[...], "TN")
        for j in range(4):
            part[2, j // 2, j % 2, at128(i), :] = work[j * 128 : (j + 1) * 128, :].astype(BF16)

    loop(3, qkv_weight)
    qkv_rows = pl.ds(0, 384)
    core_a = [
        core_send(part.at[2, jy, 1 - hc, qkv_rows], buf_core.at[2, jy, qkv_rows])
        for jy in (1 - hy, hy)
    ]
    norm_grad[...] = mm(low_grads[0], w_qkv[0], "NT")
    core_a[0].wait_recv()
    add_core(2, 1 - hy, 0, 384)
    core_a[1].wait_recv()
    add_core(2, hy, 0, 384)
    u0.spread()
    a0.a()
    a1.a()
    o0.mid()
    d1.ring()
    a0.b()
    norm_grad[...] += mm(low_grads[1], w_qkv[1], "NT")
    a1.mid()
    u1.spread()
    norm_grad[...] += mm(low_grads[2], w_qkv[2], "NT")
    u0.back()
    a1.b()

    def sink_input(r, grad):
        ig_s[r, :] = grad.astype(BF16)

    norm_back(norm_grad, gain_one, unit_one, rstd_one, lambda r: middle_grad[r, :], sink_input, 0)

    def gain_start():
        copies = []
        for n, d in enumerate(COMBOS):
            par_to, y_to, c_to = peer(*d)
            copies.append(
                send(
                    gain_part.at[0, :, at128(2 * y_to + c_to)],
                    gain_buf.at[n],
                    address(par_to, y_to, c_to),
                )
            )
        return copies

    gain_base = take(pairs - 1)

    def gain_copy(d):
        return remote(gain_sum.at[0], gain_buf.at[6 + d], ring(d)[1], gain_base + d - 1)

    def gain_middle(copies):
        for copy in copies:
            copy.wait_recv()
        total = gain_part[0, :, hcol]
        for n in range(len(COMBOS)):
            total = total + gain_buf[n]
        gain_sum[0] = total
        each_ring(lambda d: gain_copy(d).start())

    def gain_end():
        each_ring(lambda d: gain_copy(d).wait_recv())
        gain_sum[1] = gain_sum[0]

        def add_gain(d):
            gain_sum[1] = gain_sum[1] + gain_buf[6 + d]

        each_ring(add_gain)
        gains[...] = gain_sum[1]

    o0.ring()
    a0.mid()
    ig_move.go(COMBOS[:4])
    d1.spread()
    u1.back()
    ig_move.go(COMBOS[4:])
    a1.ring()
    o0.spread()
    gain_copies = gain_start()
    ig_own = local(ig_s.at[half256, hcol], ig_out.at[member])
    a0.ring()
    d1.back()
    d0.ring()
    a1.spread()
    a0.spread()
    o0.back()
    gain_middle(gain_copies)
    d0.spread()
    lo_move.go(COMBOS[:4])
    a1.back()
    d0.back()
    a0.back()
    gain_end()

    for chunk in chunks:
        chunk.end()
    lo_move.all().wait_recv()
    ig_move.all().wait_recv()
    lo_own.wait()
    ig_own.wait()
    for copy in sends:
        copy.wait_send()
    for move in (tok_move, og_move, lo_move, ig_move):
        move.all().wait_send()
    for chunk in chunks:
        chunk.sent()
    each_ring(lambda d: gain_copy(d).wait_send())
    for d in (1, 2):

        @pl.when(pair + d < pairs)
        def _():
            for order in range(2):
                for copy in forward[order, d]:
                    copy.wait_send()

        @pl.when(pair >= d)
        def _():
            for copy in backward[d]:
                copy.wait_send()


def widen_kernel(lo, ig, fin, gains, *refs):
    lo_o, ig_o, q_o, k_o, v_o, o_o, u_o, d_o, g_o, f_o = refs[:10]
    ig_b, fin_b, lo_b, gains_b, ig_w, fin_w, qkv_w, g_w, f_w, sem_in, sem_out = refs[10:]
    parts = [(fin.at[2], fin_b.at[2], 2, 0)]
    for u in (0, 1):
        for half in range(2):
            rows = pl.ds(half * 256, 256)
            parts.append((fin.at[u, rows], fin_b.at[u, rows], u, half))
    for half in range(2):
        rows = pl.ds(half * 4, 4)
        parts.append((ig.at[rows], ig_b.at[rows], 3, half))
    parts.append((lo, lo_b, 4, 0))
    parts.append((gains, gains_b, 5, 0))
    arriving = [
        pltpu.make_async_copy(source, into, sem_in.at[n])
        for n, (source, into, _, _) in enumerate(parts)
    ]
    for copy in arriving:
        copy.start()
    leaving = []

    def leave(source, out):
        copy = pltpu.make_async_copy(source, out, sem_out.at[len(leaving)])
        copy.start()
        leaving.append(copy)

    for copy, (_, _, u, n) in zip(arriving, parts, strict=True):
        copy.wait()
        if u == 5:
            g_w[...] = gains_b[0]
            f_w[...] = gains_b[1]
            leave(g_w, g_o)
            leave(f_w, f_o)
        elif u == 4:
            leave(lo_b, lo_o)
        elif u == 3:
            rows = pl.ds(n * 4, 4)
            ig_w[rows] = ig_b[rows].astype(F32)
            leave(ig_w.at[rows], ig_o.at[rows])
        elif u < 2:
            rows = pl.ds(n * 256, 256)
            fin_w[u, rows] = fin_b[u, rows].astype(F32)
            leave(fin_w.at[u, rows], (d_o, u_o)[u].at[rows])
        else:
            for i, out in enumerate((q_o, k_o, v_o)):
                qkv_w[i] = fin_b[2, pl.ds(i * 128, 128)].astype(F32).T
                leave(qkv_w.at[i], out)
            fin_w[2, pl.ds(0, 128)] = fin_b[2, pl.ds(384, 128)].astype(F32)
            leave(fin_w.at[2, pl.ds(0, 128)], o_o)
    for copy in leaving:
        copy.wait()


def body(
    tokens,
    norm_gain,
    query_weight,
    key_weight,
    value_weight,
    attention_output_weight,
    feedforward_norm_gain,
    up_weight,
    down_weight,
    segment_ids,
    out_grad,
):
    batch, length, share = tokens.shape
    width, head_cols = query_weight.shape
    units = up_weight.shape[1]
    pairs = lax.axis_size("seq") // 2
    assert lax.axis_size("head") == 4 and batch == 8 and length == BLOCK
    assert (width, share, head_cols, units) == (512, 128, 128, 512)
    assert pairs >= OWNERS and pairs % 2 == 0
    others = pairs - 1
    in_ring = 1 if pairs == OWNERS else others
    anywhere = pl.BlockSpec(memory_space=pl.ANY)
    vmem = pl.BlockSpec(memory_space=pltpu.VMEM)
    passed = sum(chunk[6] for chunk in CHUNKS)
    copies = 4 + 1 + 7 * KINDS + 8 + 4 + 5 + len(CHUNKS) * (3 + 2 * in_ring)
    copies += passed * (1 + in_ring) + (len(CHUNKS) - passed) + 7 + others
    square = (512, 512)
    buffers = dict(
        xin=(square, BF16),
        ogs=(square, BF16),
        w_qkv=((3, 512, 512), BF16),
        w_o=(square, BF16),
        w_u=((4, 512, 512), BF16),
        w_d=((4, 512, 512), BF16),
        seg_other=((8, 256), jnp.int32),
        unit_one=(square, F32),
        unit_two=(square, F32),
        rstd_one=((512, 128), F32),
        rstd_two=((512, 128), F32),
        normed=(square, BF16),
        normed_two=(square, BF16),
        feat=((2, 512, 512), BF16),
        val=(square, BF16),
        mask=((2, 256, 256), F32),
        seg_col=((2, 256, 128), F32),
        carry_on=((2, 256, 128), F32),
        own_s=((2, 256, 128), F32),
        own_z=((2, 8, 128), F32),
        msg_s=((256, 128), BF16),
        msg_z=((2, 8, 128), F32),
        buf_s=((2, 256, 128), BF16),
        buf_z=((2, 2, 8, 128), F32),
        state=((8, 128, 256), BF16),
        scores_low=((8, 512, 256), BF16),
        attn=(square, BF16),
        attn_wide=(square, F32),
        den_inv=(square, F32),
        middle=(square, F32),
        work=(square, F32),
        work_two=(square, F32),
        hid=(square, BF16),
        hid_grad=(square, BF16),
        ffn=(square, F32),
        norm_grad=(square, F32),
        middle_grad=(square, F32),
        middle_low=(square, BF16),
        num_grad=(square, BF16),
        den_grad=(square, BF16),
        grad_s=((2, 256, 128), F32),
        grad_z=((2, 8, 128), F32),
        msg_gs=((256, 128), BF16),
        msg_gz=((8, 128), F32),
        buf_gs=((2, 256, 128), BF16),
        buf_gz=((2, 8, 128), F32),
        key_acc=(square, F32),
        val_acc=(square, F32),
        low_grads=((3, 512, 512), BF16),
        lo_s=(square, BF16),
        ig_s=(square, BF16),
        part=((3, 2, 2, 512, 512), BF16),
        buf_core=((3, 2, 512, 512), BF16),
        gain_part=((1, 8, 512), F32),
        gain_sum=((2, 8, 128), F32),
        gain_buf=((7 + others, 8, 128), F32),
    )
    shapes = list(buffers.values())
    for _, _, rows, _, lanes, _, _ in CHUNKS:
        piece = rows // 2 // OWNERS
        shapes.append(((3, rows // 2, lanes), BF16))
        shapes.append(((others, piece, lanes), BF16))
        shapes.append(((piece, lanes), BF16))
        shapes.append(((piece, lanes), BF16))
    scratch = [pltpu.VMEM(*spec) for spec in shapes]
    scratch += [
        pltpu.SemaphoreType.DMA((8 + 2 + len(CHUNKS) + passed,)),
        pltpu.SemaphoreType.DMA((copies,)),
        pltpu.SemaphoreType.DMA((copies,)),
    ]
    lo, ig, fin, gains = pl.pallas_call(
        functools.partial(layer_kernel, pairs, list(buffers)),
        out_shape=(
            jax.ShapeDtypeStruct((batch, length, share), BF16),
            jax.ShapeDtypeStruct((batch, length, share), BF16),
            jax.ShapeDtypeStruct((3, 512, 512), BF16),
            jax.ShapeDtypeStruct((8, 128), F32),
        ),
        in_specs=[anywhere] * 8 + [vmem] * 3,
        out_specs=(anywhere, anywhere, anywhere, vmem),
        scratch_shapes=scratch,
        compiler_params=pltpu.CompilerParams(
            collective_id=0, has_side_effects=True, vmem_limit_bytes=58 * MIB
        ),
        cost_estimate=pl.CostEstimate(
            flops=11 * 10**9, bytes_accessed=8 * MIB, transcendentals=4 * 10**6
        ),
        name="layer",
    )(
        tokens,
        out_grad,
        query_weight,
        key_weight,
        value_weight,
        attention_output_weight,
        up_weight,
        down_weight,
        segment_ids,
        norm_gain[None],
        feedforward_norm_gain[None],
    )

    lo, ig, q_w, k_w, v_w, o_w, u_w, d_w, g_one, g_two = pl.pallas_call(
        widen_kernel,
        out_shape=(
            jax.ShapeDtypeStruct((batch, length, share), BF16),
            jax.ShapeDtypeStruct((batch, length, share), F32),
            jax.ShapeDtypeStruct((512, 128), F32),
            jax.ShapeDtypeStruct((512, 128), F32),
            jax.ShapeDtypeStruct((512, 128), F32),
            jax.ShapeDtypeStruct((128, 512), F32),
            jax.ShapeDtypeStruct((512, 512), F32),
            jax.ShapeDtypeStruct((512, 512), F32),
            jax.ShapeDtypeStruct((128,), F32),
            jax.ShapeDtypeStruct((128,), F32),
        ),
        in_specs=[anywhere] * 4,
        out_specs=(anywhere,) * 10,
        scratch_shapes=[
            pltpu.VMEM((batch, length, share), BF16),
            pltpu.VMEM((3, 512, 512), BF16),
            pltpu.VMEM((batch, length, share), BF16),
            pltpu.VMEM((8, 128), F32),
            pltpu.VMEM((batch, length, share), F32),
            pltpu.VMEM((3, 512, 512), F32),
            pltpu.VMEM((3, 512, 128), F32),
            pltpu.VMEM((128,), F32),
            pltpu.VMEM((128,), F32),
            pltpu.SemaphoreType.DMA((9,)),
            pltpu.SemaphoreType.DMA((13,)),
        ],
        compiler_params=pltpu.CompilerParams(vmem_limit_bytes=58 * MIB),
        name="widen",
    )(lo, ig, fin, gains)
    return (lo, ig, g_one, q_w, k_w, v_w, o_w, g_two, u_w, d_w)


def solution(mesh):
    in_specs = (
        P(None, "seq", "head"),
        P(),
        P(None, "head"),
        P(None, "head"),
        P(None, "head"),
        P("head", None),
        P(),
        P(None, "head"),
        P("head", None),
        P(None, "seq"),
        P(None, "seq", "head"),
    )
    out_specs = (
        P(None, "seq", "head"),
        P(None, "seq", "head"),
        P("head"),
        P(None, "head"),
        P(None, "head"),
        P(None, "head"),
        P("head", None),
        P("head"),
        P(None, "head"),
        P("head", None),
    )
    return jax.shard_map(body, mesh=mesh, in_specs=in_specs, out_specs=out_specs, check_vma=False)
```
